128 devices in a mesh: oct: 128 (over z, y, x, core).
Axes of the slice: x: 4, y: 4, z: 4, core: 2. Of those that a mesh axis runs over, the one named last changes fastest.
Arguments:
- points: float32 [8192, 3, 128], P('oct'), may hold values from -6 to 6
- dens: float32 [8192, 32, 128], P('oct'), may hold values from -6 to 6
- surface: float32 [8192, 3, 152], P('oct'), may hold values from -6 to 6
- counts: int32 [8192], P('oct'), may hold values from 1 to 128, as said below
- ulist: int32 [8192, 27], P('oct'), may hold values from -1 to 8191, as said below
- vlist: int32 [1024, 316], P('oct'), may hold values from -1 to 1023, as said below
- up_inverse: float32 [152, 152], replicated, may hold values from -0.5 to 0.5
- down_inverse: float32 [152, 152], replicated, may hold values from -0.5 to 0.5
- shift_up: float32 [8, 152, 152], replicated, may hold values from -0.15625 to 0.15625
- shift_down: float32 [8, 152, 152], replicated, may hold values from -0.5 to 0.5
- coarse: float32 [8, 152, 152], replicated, may hold values from -0.25 to 0.25
- translate: bfloat16 [316, 152, 152], replicated, may hold values from -0.0390625 to 0.0390625
Outputs:
- potential: float32 [8192, 32, 128], P('oct')
The draws below stay inside these ranges and needn't reach their ends.
Inputs may be any that keep to these rules, and one draw needn't show every extreme that they name: `counts`: each leaf has 1 to 128 stations in use; the first leaf of every slab of 64 leaves is full. `ulist`: slot 0 holds the leaf itself; slots 1 to 8 hold -1 or leaves of the next lower slab of 64 leaves, slots 9 to 17 -1 or leaves of the leaf's own slab, slots 18 to 26 -1 or leaves of the next upper slab. `vlist`: every id is -1 or a node of the same slab of 8 nodes or of an adjacent one.
All inputs are finite; a program needn't handle non-finite values.
Results may differ from the reference program's by a relative error of at most 0.0017.
Values may be sent and summed in bfloat16 or wider, within the bound.
A program may use at most 192 MiB of HBM per device.

```python
import jax
import jax.numpy as jnp
from jax import lax

Q = 32
EQ = 152
NTYPE = 316
NU = 27
LEAF_DEV = 64
PTS = 128
NODE_DEV = 8
LEAVES = 8192
NODES = 1024
N_OCT = 128


def draw_counts(key, part):
    drawn = jax.random.randint(key, (LEAVES,), 1, PTS + 1)
    leaf_ids = jnp.arange(LEAVES)
    return jnp.where(leaf_ids % LEAF_DEV == 0, PTS, drawn).astype(jnp.int32)


def draw_ulist(key, part):
    key_list = jax.random.split(key, 2)
    leaf_ids = jnp.arange(LEAVES)
    slab_ids = leaf_ids // LEAF_DEV
    slot_ids = jnp.arange(NU)
    lower_end = 1 + (NU - 1) // 3
    upper_start = lower_end + (NU - lower_end) // 2
    slot_offsets = jnp.where(slot_ids < lower_end, -1, jnp.where(slot_ids < upper_start, 0, 1))
    offsets = jnp.broadcast_to(slot_offsets[None, :], (LEAVES, NU))
    within_slab = jax.random.randint(key_list[0], (LEAVES, NU), 0, LEAF_DEV)
    keep_draw = jax.random.randint(key_list[1], (LEAVES, NU), 0, 5)
    target_slab = slab_ids[:, None] + offsets
    chosen = target_slab * LEAF_DEV + within_slab
    usable = (target_slab >= 0) & (target_slab < LEAVES // LEAF_DEV) & (keep_draw > 0)
    chosen = jnp.where(usable, chosen, -1)
    chosen = chosen.at[:, 0].set(leaf_ids)
    chosen = chosen.at[0, NU - 1].set(-1)
    return chosen.astype(jnp.int32)


def draw_vlist(key, part):
    key_list = jax.random.split(key, 3)
    node_ids = jnp.arange(NODES)
    slab_ids = node_ids // NODE_DEV
    offsets = jax.random.randint(key_list[0], (NODES, NTYPE), -1, 2)
    within_slab = jax.random.randint(key_list[1], (NODES, NTYPE), 0, NODE_DEV)
    keep_draw = jax.random.randint(key_list[2], (NODES, NTYPE), 0, 5)
    target_slab = slab_ids[:, None] + offsets
    chosen = target_slab * NODE_DEV + within_slab
    usable = (target_slab >= 0) & (target_slab < NODES // NODE_DEV) & (keep_draw > 1)
    chosen = jnp.where(usable, chosen, -1)
    chosen = chosen.at[0, 0].set(-1)
    chosen = chosen.at[NODES - 2, 1].set(NODES - 1)
    return chosen.astype(jnp.int32)


def levels(stream_key, dims, shards, least, top_value):
    factor_of, own = 1.0, jax.random.fold_in(stream_key, 6)
    for dim, parts in shards:
        heights = jnp.exp(jax.random.uniform(jax.random.fold_in(own, dim), (parts,), jnp.float32, least / len(shards), top_value / len(shards)))
        factor_of = factor_of * jnp.repeat(heights, dims[dim] // parts).reshape([-1 if axis == dim else 1 for axis in range(len(dims))])
    return factor_of


def scatter_about(rng, dims, spread, bound, cuts=(), dtype=jnp.bfloat16):
    values = spread * jax.random.normal(rng, dims, jnp.float32)
    if cuts:
        values = values * levels(rng, dims, cuts, -0.22, 0.18)
    return jnp.clip(values, -bound, bound).astype(dtype)


def setup_inputs(seed: int = 0) -> dict:
    streams_of = jax.random.split(jax.random.key(seed), 13)
    return {
        "points": scatter_about(streams_of[0], (LEAVES, 3, PTS), 1.0, 6.0, ((0, 128),), jnp.float32),
        "dens": scatter_about(streams_of[1], (LEAVES, Q, PTS), 1.0, 6.0, ((0, 128),), jnp.float32),
        "surface": scatter_about(streams_of[2], (LEAVES, 3, EQ), 1.0, 6.0, ((0, 128),), jnp.float32),
        "counts": draw_counts(jax.random.fold_in(streams_of[12], 71), 0),
        "ulist": draw_ulist(jax.random.fold_in(streams_of[12], 71), 0),
        "vlist": draw_vlist(jax.random.fold_in(streams_of[12], 71), 0),
        "up_inverse": scatter_about(streams_of[6], (EQ, EQ), EQ ** -0.5, 0.5, (), jnp.float32),
        "down_inverse": scatter_about(streams_of[7], (EQ, EQ), EQ ** -0.5, 0.5, (), jnp.float32),
        "shift_up": scatter_about(streams_of[8], (8, EQ, EQ), (8 * EQ) ** -0.5, 0.15625, (), jnp.float32),
        "shift_down": scatter_about(streams_of[9], (8, EQ, EQ), EQ ** -0.5, 0.5, (), jnp.float32),
        "coarse": scatter_about(streams_of[10], (8, EQ, EQ), (3 * EQ) ** -0.5, 0.25, (), jnp.float32),
        "translate": scatter_about(streams_of[11], (NTYPE, EQ, EQ), (EQ * NTYPE // 2) ** -0.5, 0.0390625),
    }


HIGHEST = lax.Precision.HIGHEST


def kernel(left_pts, right_pts):
    total_sq = jnp.zeros((left_pts.shape[1], right_pts.shape[1]), jnp.float32)
    for coord_index in range(3):
        offset = left_pts[coord_index][:, None] - right_pts[coord_index][None, :]
        total_sq = total_sq + offset * offset
    return jnp.exp(-0.5 * total_sq)


def near_field(target_pts, target_ids, source_base, sources):
    source_count = sources.shape[0]
    local_ids = target_ids - source_base
    usable = (target_ids >= 0) & (local_ids >= 0) & (local_ids < source_count)
    safe_ids = jnp.clip(local_ids, 0, source_count - 1).astype(jnp.int32)

    def one_leaf(leaf_pts, leaf_ids, leaf_usable):
        picked = sources[leaf_ids]
        weights = jnp.where(leaf_usable[:, None, None], picked[:, 3:, :], 0.0)
        kernels = jax.vmap(kernel, in_axes=(0, None))(picked[:, :3, :], leaf_pts)
        slot_count, q_width, p_width = weights.shape
        flat_weights = jnp.transpose(weights, (1, 0, 2)).reshape(q_width, slot_count * p_width)
        return jnp.dot(flat_weights, kernels.reshape(slot_count * p_width, leaf_pts.shape[1]),
                       precision=HIGHEST, preferred_element_type=jnp.float32)

    def block_fn(block):
        return jax.vmap(one_leaf)(block[0], block[1], block[2])

    leaf_count = target_pts.shape[0]
    blocked = (target_pts.reshape((leaf_count // 4, 4) + target_pts.shape[1:]),
               safe_ids.reshape(leaf_count // 4, 4, -1),
               usable.reshape(leaf_count // 4, 4, -1))
    result = lax.map(block_fn, blocked)
    return result.reshape(leaf_count, sources.shape[1] - 3, target_pts.shape[2])


def reference(points, dens, surface, counts, ulist, vlist, up_inverse, down_inverse, shift_up, shift_down, coarse, translate):
    leaf_total, q_width, p_width = dens.shape
    eq_width = surface.shape[2]
    slots = jnp.arange(p_width).astype(jnp.int32)
    mask = (slots[None, :] < counts[:, None]).astype(jnp.float32)[:, None, :]
    masked = dens * mask
    up_kernel = jax.vmap(kernel)(points, surface)
    check = jnp.einsum("lqp,lpe->lqe", masked, up_kernel, precision=HIGHEST)
    leaf_eq = jnp.dot(check.reshape(-1, eq_width), up_inverse, precision=HIGHEST,
                      preferred_element_type=jnp.float32).reshape(leaf_total, q_width, eq_width)
    node_eq = jnp.einsum("ncqe,cef->nqf", leaf_eq.reshape(-1, 8, q_width, eq_width), shift_up, precision=HIGHEST)
    node_send = node_eq.astype(jnp.bfloat16)
    current = jnp.einsum("ncqe,cef->nqf", node_eq.reshape(-1, 8, q_width, eq_width), shift_up, precision=HIGHEST)
    bit_count = N_OCT.bit_length() - 1
    device_ids = jnp.arange(N_OCT).astype(jnp.int32)
    slab_local = jnp.zeros((N_OCT, q_width, eq_width), jnp.float32)
    for level_start in range(0, bit_count, 3):
        width_bits = min(3, bit_count - level_start)
        group_size = 2 ** width_bits
        current = jnp.einsum("mcqe,cef->mqf", current.reshape(-1, group_size, q_width, eq_width),
                             shift_up[:group_size], precision=HIGHEST)
        parents = current[jnp.right_shift(device_ids, level_start + width_bits)]
        child_slot = jnp.right_shift(device_ids, level_start) & 7
        slab_local = slab_local + jnp.einsum("mqe,mef->mqf", parents, coarse[child_slot], precision=HIGHEST)
    translate_wide = translate.astype(jnp.float32)

    def far_block(block_ids):
        usable = block_ids >= 0
        safe_ids = jnp.clip(block_ids, 0, node_send.shape[0] - 1).astype(jnp.int32)
        picked = jnp.where(usable[:, :, None, None], node_send[safe_ids].astype(jnp.float32), 0.0)
        return jnp.einsum("ntqe,tef->nqf", picked, translate_wide, precision=HIGHEST)

    node_dev = vlist.shape[0] // N_OCT
    far_node = lax.map(far_block, vlist.reshape(N_OCT, node_dev, -1)).reshape(-1, q_width, eq_width)
    parent_part = jnp.einsum("mqe,cef->mcqf", slab_local, shift_down, precision=HIGHEST).reshape(-1, q_width, eq_width)
    node_local = far_node + parent_part
    leaf_local = jnp.einsum("nqe,cef->ncqf", node_local, shift_down, precision=HIGHEST).reshape(leaf_total, q_width, eq_width)
    leaf_down = jnp.dot(leaf_local.reshape(-1, eq_width), down_inverse, precision=HIGHEST,
                        preferred_element_type=jnp.float32).reshape(leaf_total, q_width, eq_width)
    far_pot = jnp.einsum("lqe,lpe->lqp", leaf_down, up_kernel, precision=HIGHEST)
    sources = jnp.concatenate([points, masked], axis=1)
    near = near_field(points, ulist, 0, sources)
    return (far_pot + near) * mask
```

```python
import functools

import jax
import jax.numpy as jnp
from jax import lax
from jax.experimental import pallas as pl
from jax.experimental.pallas import tpu as pltpu
from jax.sharding import PartitionSpec as P

HIGHEST = lax.Precision.HIGHEST
BF = jnp.bfloat16
F32 = jnp.float32
LIST = 128


def split2(x):
    hi = x.astype(BF)
    lo = (x - hi.astype(F32)).astype(BF)
    return hi, lo


def split3(x):
    a = x.astype(BF).astype(F32)
    r = x - a
    b = r.astype(BF).astype(F32)
    return a, b, r - b


def rows8(shape):
    return lax.broadcasted_iota(jnp.int32, shape, 0)


LOG2E = 1.4426950408889634


def source_tiles(coords):
    out = []
    norm = None
    row = rows8((8, 128))
    for c in coords:
        x = jnp.broadcast_to(c, (8, 128))
        a, b, d = split3(LOG2E * x)
        first = (row <= 1) | (row == 4)
        out.append(jnp.where(first, a, jnp.where(row <= 3, b, jnp.where(row == 5, d, 0.0))))
        norm = x * x if norm is None else norm + x * x
    a, b, d = split3((-0.5 * LOG2E) * norm)
    out.append(
        jnp.where(row == 0, a, jnp.where(row == 1, b, jnp.where(row == 2, d, jnp.where(row <= 5, 1.0, 0.0))))
    )
    return out


def target_tiles(coords):
    out = []
    norm = None
    row = rows8((8, 128))
    for c in coords:
        x = jnp.broadcast_to(c, (8, 128))
        a, b, d = split3(x)
        first = (row == 0) | (row == 2) | (row == 5)
        second = (row == 1) | (row == 3)
        out.append(jnp.where(first, a, jnp.where(second, b, jnp.where(row == 4, d, 0.0))))
        norm = x * x if norm is None else norm + x * x
    a, b, d = split3((-0.5 * LOG2E) * norm)
    out.append(
        jnp.where(row <= 2, 1.0, jnp.where(row == 3, a, jnp.where(row == 4, b, jnp.where(row == 5, d, 0.0))))
    )
    return out


def near_kernel(leaves, cnt, units, ptr, leaf, total_ref, p0, p1, p2, d0, d1, d2, surf, down, out, f_s, m_s, w_s, e_s, acc):
    lane = lax.broadcasted_iota(jnp.int32, (32, 128), 1)
    lane_big = lax.broadcasted_iota(jnp.int32, (128, 128), 1)
    zero_unit = 4 * (3 * leaves + 2 * leaves)

    def put_features(coords4, base_units):
        tiles = []
        for coords in coords4:
            tiles += source_tiles(coords)
        turned = jnp.concatenate(tiles, axis=0).astype(BF).T
        for i in range(4):
            own = (lane_big >= 32 * i) & (lane_big < 32 * i + 32)
            f_s[pl.ds(base_units[i], 4)] = jnp.where(own, turned, jnp.zeros_like(turned)).reshape(4, 32, 128)

    def put_density(tile, base):
        for k in range(4):
            r = tile if k == 0 else pltpu.roll(tile, 32 * k, 1)
            hi, lo = split2(r)
            m_s[base + k] = jnp.concatenate([hi, lo], axis=0)

    for slab, (p, d) in enumerate(((p0, d0), (p1, d1), (p2, d2))):

        def prep(g, carry, slab=slab, p=p, d=d):
            coords4 = [[p[c, pl.ds(4 * g + i, 1), :] for c in range(3)] for i in range(4)]
            put_features(coords4, [4 * (slab * leaves + 4 * g + i) for i in range(4)])
            for i in range(4):
                j = 4 * g + i
                masked = jnp.where(lane < cnt[slab * leaves + j], d[j], 0.0)
                put_density(masked, 4 * (slab * leaves + j))
            return carry

        lax.fori_loop(0, leaves // 4, prep, 0)

    def prep_surface(g, carry):
        coords4 = [[surf[3 * (i % 2) + c, pl.ds(2 * g + i // 2, 1), :] for c in range(3)] for i in range(4)]
        put_features(coords4, [4 * (3 * leaves + 4 * g + i) for i in range(4)])
        for i in range(4):
            put_density(down[2 * g + i // 2, :, pl.ds(128 * (i % 2), 128)], 4 * (3 * leaves + 4 * g + i))
        return carry

    lax.fori_loop(0, leaves // 2, prep_surface, 0)
    f_s[pl.ds(zero_unit, 4)] = jnp.zeros((4, 32, 128), BF)
    m_s[pl.ds(zero_unit, 4)] = jnp.zeros((4, 64, 128), BF)

    def prep_target(j, carry):
        tile = jnp.concatenate(target_tiles([p1[c, pl.ds(j, 1), :] for c in range(3)]), axis=0).astype(BF)
        w_s[j] = jnp.concatenate([tile] * 4, axis=0)
        acc[j] = jnp.zeros((64, 256), F32)
        return carry

    lax.fori_loop(0, leaves, prep_target, 0)

    lane64 = lax.broadcasted_iota(jnp.int32, (64, 128), 1)

    def exponents(i, slot):
        base, l = ptr[i], leaf[i]
        left = jnp.concatenate([f_s[units[base + v]] for v in range(4)], axis=0)
        right = jnp.concatenate([f_s[units[base + 4 + v]] for v in range(4)], axis=0)
        w = w_s[l]
        e_s[slot, 0] = jnp.dot(left, w, preferred_element_type=F32)
        e_s[slot, 1] = jnp.dot(right, w, preferred_element_type=F32)

    def weights(base):
        t = [m_s[units[base + v]] for v in range(4)]
        return jnp.where(
            lane64 < 64, jnp.where(lane64 < 32, t[0], t[1]), jnp.where(lane64 < 96, t[2], t[3])
        )

    def apply(i, slot):
        base, l = ptr[i], leaf[i]
        m = jnp.concatenate([weights(base + 8), weights(base + 12)], axis=1)
        k = jnp.exp2(e_s[slot].reshape(256, 128))
        hi, lo = split2(k)
        acc[l] += jnp.dot(m, jnp.concatenate([hi, lo], axis=1), preferred_element_type=F32)

    half = 4
    for u in range(half):
        exponents(u, u)

    def body(i, carry):
        at = 2 * half * i
        for u in range(half):
            exponents(at + half + u, half + u)
            apply(at + u, u)
        for u in range(half):
            exponents(at + 2 * half + u, u)
            apply(at + half + u, half + u)
        return carry

    lax.fori_loop(0, total_ref[0], body, 0)

    def finish(j, carry):
        a = acc[j]
        v = (a[:32, :128] + a[:32, 128:]) + (a[32:, :128] + a[32:, 128:])
        out[j] = jnp.where(lane < cnt[leaves + j], v, 0.0)
        return carry

    lax.fori_loop(0, leaves, finish, 0)


def near_call(cnt, units_list, ptr, leaf, total, pts, dens, surf, down):
    leaves = dens[0].shape[0]
    units = 4 * (3 * leaves + 2 * leaves) + 4
    smem = pl.BlockSpec(memory_space=pltpu.SMEM)
    vmem = pl.BlockSpec(memory_space=pltpu.VMEM)
    return pl.pallas_call(
        functools.partial(near_kernel, leaves),
        out_shape=jax.ShapeDtypeStruct(dens[0].shape, F32),
        in_specs=[smem] * 5 + [vmem] * 8,
        out_specs=vmem,
        scratch_shapes=[
            pltpu.VMEM((units, 32, 128), BF),
            pltpu.VMEM((units, 64, 128), BF),
            pltpu.VMEM((leaves, 128, 128), BF),
            pltpu.VMEM((8, 2, 128, 128), F32),
            pltpu.VMEM((leaves, 64, 256), F32),
        ],
        compiler_params=pltpu.CompilerParams(vmem_limit_bytes=60 * 1024 * 1024),
        name="near",
    )(cnt, units_list, ptr, leaf, total, *pts, *dens, surf, down)


def make_lists(ulist, counts3, first):
    leaves = ulist.shape[0]
    ids = jnp.arange(3 * leaves)
    rel = jnp.where(ulist >= 0, ulist - first, -1)
    cnt = jnp.sum(jnp.where(rel[:, :, None] == ids, counts3, 0), axis=-1)
    num = (cnt + 31) // 32
    slots = ulist.shape[1]
    before = jnp.arange(slots)[:, None] < jnp.arange(slots)[None, :]
    start = 5 + jnp.sum(jnp.where(before, num[:, :, None], 0), axis=1)
    place = jnp.arange(LIST)
    at = place - start[:, :, None]
    inside = (at >= 0) & (at < num[:, :, None])
    zero_unit = 20 * leaves
    unit = zero_unit + jnp.sum(jnp.where(inside, 4 * rel[:, :, None] + at - zero_unit, 0), axis=1)
    surface_unit = 12 * leaves + 8 * jnp.arange(leaves)[:, None] + place
    unit = jnp.where(place < 5, surface_unit, unit).astype(jnp.int32)
    turned = (unit - unit % 4) + (place - unit) % 4
    n = (5 + jnp.sum(num, axis=1) + 7) // 8
    upto = jnp.arange(leaves)[:, None] <= jnp.arange(leaves)[None, :]
    end = jnp.sum(jnp.where(upto, n[:, None], 0), axis=0)
    begin = end - n
    chunk = jnp.arange(16 * leaves + 16)
    inside = (chunk[:, None] >= begin) & (chunk[:, None] < end)
    leaf = jnp.sum(jnp.where(inside, jnp.arange(leaves), 0), axis=1)
    ptr = jnp.sum(jnp.where(inside, 16 * (16 * jnp.arange(leaves) + chunk[:, None] - begin), 0), axis=1)
    ptr = jnp.where(chunk < end[-1], ptr, 256 * leaves)
    both = jnp.stack([unit.reshape(leaves, 16, 8), turned.reshape(leaves, 16, 8)], axis=2).reshape(-1)
    both = jnp.concatenate([both, jnp.full((16,), zero_unit)])
    rounds = ((end[-1] + 7) // 8).reshape(1)
    return [v.astype(jnp.int32) for v in (both, ptr, leaf, rounds)]


def far_kernel(step, table, sel, nodes, out):
    width = table.shape[1]
    lane = lax.broadcasted_iota(jnp.int32, (32, 128), 1)

    @pl.when(pl.program_id(0) == 0)
    def _():
        out[...] = jnp.zeros_like(out)

    zero = jnp.zeros((32, 128), BF)
    picks = sel[...]
    total = None
    for k in range(0, step, 2):
        sums = []
        for e in (k, k + 1):
            s = jnp.dot(table[e], picks, preferred_element_type=F32)
            hi, lo = split2(s)
            sums.append(jnp.concatenate([hi, lo], axis=0))
        rows = []
        for e in (k, k + 1):
            x = nodes[e]
            for n in range(8):
                own = (lane >= 32 * (n % 4)) & (lane < 32 * (n % 4) + 32)
                part = jnp.where(own, x, zero)
                rows.append(jnp.concatenate([part, zero] if n < 4 else [zero, part], axis=1))
        r = jnp.dot(
            jnp.concatenate(sums, axis=1), jnp.concatenate(rows, axis=0), preferred_element_type=F32
        )
        r = r[:width] + r[width:]
        total = r if total is None else total + r
    out[...] += total


def far_call(table, sel, nodes):
    count, width, types = table.shape
    step = 8
    return pl.pallas_call(
        lambda *refs: far_kernel(step, *refs),
        grid=(count // step,),
        out_shape=jax.ShapeDtypeStruct((width, 256), F32),
        in_specs=[
            pl.BlockSpec((step, width, types), lambda i: (i, 0, 0)),
            pl.BlockSpec((types, 256), lambda i: (0, 0)),
            pl.BlockSpec((step, 32, 128), lambda i: (i, 0, 0)),
        ],
        out_specs=pl.BlockSpec((width, 256), lambda i: (0, 0)),
        compiler_params=pltpu.CompilerParams(vmem_limit_bytes=48 * 1024 * 1024),
        name="far",
    )(table, sel, nodes)


def far_inputs(vlist, base, cycle):
    rel = jnp.where(vlist >= 0, vlist - base, -1)
    sel = (rel.T[:, :, None] == jnp.arange(32)).astype(BF).reshape(rel.shape[1], 256)
    turned = jnp.transpose(cycle, (2, 0, 1))
    nodes = jnp.pad(jnp.concatenate([turned] * 4, axis=2), ((0, 0), (0, 8), (0, 0)))
    return sel, nodes


def extended(value, sides, width):
    for axis, dim in sides:
        count, length = (lax.axis_size(axis), value.shape[dim])
        up = [(i, (i + 1) % count) for i in range(count - 1)]
        down = [(j, i) for i, j in up]
        last = lax.slice_in_dim(value, length - width, length, axis=dim)
        first = lax.slice_in_dim(value, 0, width, axis=dim)
        before = lax.ppermute(last, axis, up)
        after = lax.ppermute(first, axis, down)
        value = jnp.concatenate([before, value, after], axis=dim)
    return value


def swapped(value, axis, bit):
    mask = 2**bit
    pairs = [(source, source ^ mask) for source in range(lax.axis_size(axis))]
    return lax.ppermute(value, axis, pairs)


def kernel(left_pts, right_pts):
    total_sq = jnp.zeros((left_pts.shape[1], right_pts.shape[1]), jnp.float32)
    for coord_index in range(3):
        offset = left_pts[coord_index][:, None] - right_pts[coord_index][None, :]
        total_sq = total_sq + offset * offset
    return jnp.exp(-0.5 * total_sq)


def local(
    points,
    dens,
    surface,
    counts,
    ulist,
    vlist,
    up_inverse,
    down_inverse,
    shift_up,
    shift_down,
    coarse,
    translate,
):
    leaf_count, q_width, p_width = dens.shape
    eq_width = surface.shape[2]
    node_count = vlist.shape[0]
    index = lax.axis_index("oct")
    slots = jnp.arange(p_width)
    mask = (slots[None, :] < counts[:, None]).astype(jnp.float32)[:, None, :]
    masked = dens * mask
    count = lax.axis_size("oct")
    up = [(i, (i + 1) % count) for i in range(count - 1)]
    down = [(i, j) for j, i in up]
    turned_points = jnp.transpose(points, (1, 0, 2))
    points3 = [lax.ppermute(turned_points, "oct", up), turned_points, lax.ppermute(turned_points, "oct", down)]
    dens3 = [lax.ppermute(dens, "oct", up), dens, lax.ppermute(dens, "oct", down)]
    counts3 = jnp.concatenate([lax.ppermute(counts, "oct", up), counts, lax.ppermute(counts, "oct", down)])
    lists = make_lists(ulist, counts3, (index - 1) * leaf_count)
    up_kernel = jax.vmap(kernel)(points, surface)
    check = jnp.einsum("lqp,lpe->lqe", masked, up_kernel, precision=HIGHEST)
    leaf_eq = jnp.dot(
        check.reshape(-1, eq_width),
        up_inverse,
        precision=HIGHEST,
        preferred_element_type=jnp.float32,
    ).reshape(leaf_count, q_width, eq_width)
    node_eq = jnp.einsum(
        "ncqe,cef->nqf", leaf_eq.reshape(-1, 8, q_width, eq_width), shift_up, precision=HIGHEST
    )
    node_send = node_eq.astype(jnp.bfloat16).reshape(node_count, q_width * eq_width)
    slab_eq = jnp.einsum("cqe,cef->qf", node_eq, shift_up, precision=HIGHEST)
    cycle = extended(node_send, (("oct", 0),), node_count)
    bit_count = lax.axis_size("oct").bit_length() - 1
    slab_local = jnp.zeros((q_width, eq_width), jnp.float32)
    current = slab_eq
    for level_start in range(0, bit_count, 3):
        width_bits = min(3, bit_count - level_start)
        child_slot = jnp.right_shift(index, level_start) & 7
        current = jnp.dot(
            current, shift_up[child_slot], precision=HIGHEST, preferred_element_type=jnp.float32
        )
        for bit_number in range(level_start, level_start + width_bits):
            current = current + swapped(current, "oct", bit_number)
        slab_local = slab_local + jnp.dot(
            current, coarse[child_slot], precision=HIGHEST, preferred_element_type=jnp.float32
        )
    cycle = cycle.reshape(3 * node_count, q_width, eq_width)
    sel, nodes = far_inputs(vlist, (index - 1) * node_count, cycle)
    far_node = far_call(jnp.transpose(translate, (1, 2, 0)), sel, nodes)
    far_node = far_node.T.reshape(node_count, q_width, eq_width)
    parent_part = jnp.einsum("qe,cef->cqf", slab_local, shift_down, precision=HIGHEST)
    node_local = far_node + parent_part
    leaf_local = jnp.einsum("nqe,cef->ncqf", node_local, shift_down, precision=HIGHEST).reshape(
        leaf_count, q_width, eq_width
    )
    wide = 256
    pad = wide - eq_width
    leaf_down = jnp.dot(
        leaf_local.reshape(-1, eq_width),
        jnp.pad(down_inverse, ((0, 0), (0, pad))),
        precision=HIGHEST,
        preferred_element_type=jnp.float32,
    ).reshape(leaf_count, q_width, wide)
    surf = jnp.pad(jnp.transpose(surface, (1, 0, 2)), ((0, 0), (0, 0), (0, pad)))
    surf = jnp.concatenate([surf[:, :, :128], surf[:, :, 128:]], axis=0)
    return near_call(counts3, *lists, points3, dens3, surf, leaf_down)


def solution(mesh):
    placed = (
        P("oct", None, None),
        P("oct", None, None),
        P("oct", None, None),
        P("oct"),
        P("oct", None),
        P("oct", None),
        P(),
        P(),
        P(),
        P(),
        P(),
        P(),
    )
    return jax.shard_map(
        local, mesh=mesh, in_specs=placed, out_specs=P("oct", None, None), check_vma=False
    )
```

```python
import functools

import jax
import jax.numpy as jnp
from jax import lax
from jax.experimental import pallas as pl
from jax.experimental.pallas import tpu as pltpu
from jax.sharding import PartitionSpec as P

HIGHEST = lax.Precision.HIGHEST
BF = jnp.bfloat16
F32 = jnp.float32
LIST = 128


def split2(x):
    hi = x.astype(BF)
    lo = (x - hi.astype(F32)).astype(BF)
    return hi, lo


def split3(x):
    a = x.astype(BF).astype(F32)
    r = x - a
    b = r.astype(BF).astype(F32)
    return a, b, r - b


def rows8(shape):
    return lax.broadcasted_iota(jnp.int32, shape, 0)


LOG2E = 1.4426950408889634


def source_tiles(coords):
    out = []
    norm = None
    row = rows8((8, 128))
    for c in coords:
        x = jnp.broadcast_to(c, (8, 128))
        a, b, d = split3(LOG2E * x)
        first = (row <= 1) | (row == 4)
        out.append(jnp.where(first, a, jnp.where(row <= 3, b, jnp.where(row == 5, d, 0.0))))
        norm = x * x if norm is None else norm + x * x
    a, b, d = split3((-0.5 * LOG2E) * norm)
    out.append(
        jnp.where(row == 0, a, jnp.where(row == 1, b, jnp.where(row == 2, d, jnp.where(row <= 5, 1.0, 0.0))))
    )
    return out


def target_tiles(coords):
    out = []
    norm = None
    row = rows8((8, 128))
    for c in coords:
        x = jnp.broadcast_to(c, (8, 128))
        a, b, d = split3(x)
        first = (row == 0) | (row == 2) | (row == 5)
        second = (row == 1) | (row == 3)
        out.append(jnp.where(first, a, jnp.where(second, b, jnp.where(row == 4, d, 0.0))))
        norm = x * x if norm is None else norm + x * x
    a, b, d = split3((-0.5 * LOG2E) * norm)
    out.append(
        jnp.where(row <= 2, 1.0, jnp.where(row == 3, a, jnp.where(row == 4, b, jnp.where(row == 5, d, 0.0))))
    )
    return out


def near_kernel(leaves, cnt, units, ptr, leaf, total_ref, p0, p1, p2, d0, d1, d2, surf, down, out, f_s, m_s, w_s, e_s, acc):
    lane = lax.broadcasted_iota(jnp.int32, (32, 128), 1)
    lane_big = lax.broadcasted_iota(jnp.int32, (128, 128), 1)
    zero_unit = 4 * (3 * leaves + 2 * leaves)

    def put_features(coords4, base_units):
        tiles = []
        for coords in coords4:
            tiles += source_tiles(coords)
        turned = jnp.concatenate(tiles, axis=0).astype(BF).T
        for i in range(4):
            own = (lane_big >= 32 * i) & (lane_big < 32 * i + 32)
            f_s[pl.ds(base_units[i], 4)] = jnp.where(own, turned, jnp.zeros_like(turned)).reshape(4, 32, 128)

    def put_density(tile, base):
        for k in range(4):
            r = tile if k == 0 else pltpu.roll(tile, 32 * k, 1)
            hi, lo = split2(r)
            m_s[base + k] = jnp.concatenate([hi, lo], axis=0)

    for slab, (p, d) in enumerate(((p0, d0), (p1, d1), (p2, d2))):

        def prep(g, carry, slab=slab, p=p, d=d):
            coords4 = [[p[c, pl.ds(4 * g + i, 1), :] for c in range(3)] for i in range(4)]
            put_features(coords4, [4 * (slab * leaves + 4 * g + i) for i in range(4)])
            for i in range(4):
                j = 4 * g + i
                masked = jnp.where(lane < cnt[slab * leaves + j], d[j], 0.0)
                put_density(masked, 4 * (slab * leaves + j))
            return carry

        lax.fori_loop(0, leaves // 4, prep, 0)

    def prep_surface(g, carry):
        coords4 = [[surf[3 * (i % 2) + c, pl.ds(2 * g + i // 2, 1), :] for c in range(3)] for i in range(4)]
        put_features(coords4, [4 * (3 * leaves + 4 * g + i) for i in range(4)])
        for i in range(4):
            put_density(down[2 * g + i // 2, :, pl.ds(128 * (i % 2), 128)], 4 * (3 * leaves + 4 * g + i))
        return carry

    lax.fori_loop(0, leaves // 2, prep_surface, 0)
    f_s[pl.ds(zero_unit, 4)] = jnp.zeros((4, 32, 128), BF)
    m_s[pl.ds(zero_unit, 4)] = jnp.zeros((4, 64, 128), BF)

    def prep_target(j, carry):
        tile = jnp.concatenate(target_tiles([p1[c, pl.ds(j, 1), :] for c in range(3)]), axis=0).astype(BF)
        w_s[j] = jnp.concatenate([tile] * 4, axis=0)
        acc[j] = jnp.zeros((64, 256), F32)
        return carry

    lax.fori_loop(0, leaves, prep_target, 0)

    lane64 = lax.broadcasted_iota(jnp.int32, (64, 128), 1)

    def exponents(i, slot):
        base, l = ptr[i], leaf[i]
        left = jnp.concatenate([f_s[units[base + v]] for v in range(4)], axis=0)
        right = jnp.concatenate([f_s[units[base + 4 + v]] for v in range(4)], axis=0)
        w = w_s[l]
        e_s[slot, 0] = jnp.dot(left, w, preferred_element_type=F32)
        e_s[slot, 1] = jnp.dot(right, w, preferred_element_type=F32)

    def weights(base):
        t = [m_s[units[base + v]] for v in range(4)]
        return jnp.where(
            lane64 < 64, jnp.where(lane64 < 32, t[0], t[1]), jnp.where(lane64 < 96, t[2], t[3])
        )

    def apply(i, slot):
        base, l = ptr[i], leaf[i]
        m = jnp.concatenate([weights(base + 8), weights(base + 12)], axis=1)
        k = jnp.exp2(e_s[slot].reshape(256, 128))
        hi, lo = split2(k)
        acc[l] += jnp.dot(m, jnp.concatenate([hi, lo], axis=1), preferred_element_type=F32)

    half = 4
    for u in range(half):
        exponents(u, u)

    def body(i, carry):
        at = 2 * half * i
        for u in range(half):
            exponents(at + half + u, half + u)
            apply(at + u, u)
        for u in range(half):
            exponents(at + 2 * half + u, u)
            apply(at + half + u, half + u)
        return carry

    lax.fori_loop(0, total_ref[0], body, 0)

    def finish(j, carry):
        a = acc[j]
        v = (a[:32, :128] + a[:32, 128:]) + (a[32:, :128] + a[32:, 128:])
        out[j] = jnp.where(lane < cnt[leaves + j], v, 0.0)
        return carry

    lax.fori_loop(0, leaves, finish, 0)


def near_call(cnt, units_list, ptr, leaf, total, pts, dens, surf, down):
    leaves = dens[0].shape[0]
    units = 4 * (3 * leaves + 2 * leaves) + 4
    smem = pl.BlockSpec(memory_space=pltpu.SMEM)
    vmem = pl.BlockSpec(memory_space=pltpu.VMEM)
    return pl.pallas_call(
        functools.partial(near_kernel, leaves),
        out_shape=jax.ShapeDtypeStruct(dens[0].shape, F32),
        in_specs=[smem] * 5 + [vmem] * 8,
        out_specs=vmem,
        scratch_shapes=[
            pltpu.VMEM((units, 32, 128), BF),
            pltpu.VMEM((units, 64, 128), BF),
            pltpu.VMEM((leaves, 128, 128), BF),
            pltpu.VMEM((8, 2, 128, 128), F32),
            pltpu.VMEM((leaves, 64, 256), F32),
        ],
        compiler_params=pltpu.CompilerParams(vmem_limit_bytes=60 * 1024 * 1024),
        name="near",
    )(cnt, units_list, ptr, leaf, total, *pts, *dens, surf, down)


def make_lists(ulist, counts3, first):
    leaves = ulist.shape[0]
    ids = jnp.arange(3 * leaves)
    rel = jnp.where(ulist >= 0, ulist - first, -1)
    cnt = jnp.sum(jnp.where(rel[:, :, None] == ids, counts3, 0), axis=-1)
    num = (cnt + 31) // 32
    slots = ulist.shape[1]
    before = jnp.arange(slots)[:, None] < jnp.arange(slots)[None, :]
    start = 5 + jnp.sum(jnp.where(before, num[:, :, None], 0), axis=1)
    place = jnp.arange(LIST)
    at = place - start[:, :, None]
    inside = (at >= 0) & (at < num[:, :, None])
    zero_unit = 20 * leaves
    unit = zero_unit + jnp.sum(jnp.where(inside, 4 * rel[:, :, None] + at - zero_unit, 0), axis=1)
    surface_unit = 12 * leaves + 8 * jnp.arange(leaves)[:, None] + place
    unit = jnp.where(place < 5, surface_unit, unit).astype(jnp.int32)
    turned = (unit - unit % 4) + (place - unit) % 4
    n = (5 + jnp.sum(num, axis=1) + 7) // 8
    upto = jnp.arange(leaves)[:, None] <= jnp.arange(leaves)[None, :]
    end = jnp.sum(jnp.where(upto, n[:, None], 0), axis=0)
    begin = end - n
    chunk = jnp.arange(16 * leaves + 16)
    inside = (chunk[:, None] >= begin) & (chunk[:, None] < end)
    leaf = jnp.sum(jnp.where(inside, jnp.arange(leaves), 0), axis=1)
    ptr = jnp.sum(jnp.where(inside, 16 * (16 * jnp.arange(leaves) + chunk[:, None] - begin), 0), axis=1)
    ptr = jnp.where(chunk < end[-1], ptr, 256 * leaves)
    both = jnp.stack([unit.reshape(leaves, 16, 8), turned.reshape(leaves, 16, 8)], axis=2).reshape(-1)
    both = jnp.concatenate([both, jnp.full((16,), zero_unit)])
    rounds = ((end[-1] + 7) // 8).reshape(1)
    return [v.astype(jnp.int32) for v in (both, ptr, leaf, rounds)]


def far_kernel(step, table, sel, nodes, out):
    width = table.shape[1]
    lane = lax.broadcasted_iota(jnp.int32, (32, 128), 1)

    @pl.when(pl.program_id(0) == 0)
    def _():
        out[...] = jnp.zeros_like(out)

    zero = jnp.zeros((32, 128), BF)
    picks = sel[...]
    total = None
    for k in range(0, step, 2):
        sums = []
        for e in (k, k + 1):
            s = jnp.dot(table[e], picks, preferred_element_type=F32)
            hi, lo = split2(s)
            sums.append(jnp.concatenate([hi, lo], axis=0))
        rows = []
        for e in (k, k + 1):
            x = nodes[e]
            for n in range(8):
                own = (lane >= 32 * (n % 4)) & (lane < 32 * (n % 4) + 32)
                part = jnp.where(own, x, zero)
                rows.append(jnp.concatenate([part, zero] if n < 4 else [zero, part], axis=1))
        r = jnp.dot(
            jnp.concatenate(sums, axis=1), jnp.concatenate(rows, axis=0), preferred_element_type=F32
        )
        r = r[:width] + r[width:]
        total = r if total is None else total + r
    out[...] += total


def far_call(table, sel, nodes):
    count, width, types = table.shape
    step = 8
    return pl.pallas_call(
        lambda *refs: far_kernel(step, *refs),
        grid=(count // step,),
        out_shape=jax.ShapeDtypeStruct((width, 256), F32),
        in_specs=[
            pl.BlockSpec((step, width, types), lambda i: (i, 0, 0)),
            pl.BlockSpec((types, 256), lambda i: (0, 0)),
            pl.BlockSpec((step, 32, 128), lambda i: (i, 0, 0)),
        ],
        out_specs=pl.BlockSpec((width, 256), lambda i: (0, 0)),
        compiler_params=pltpu.CompilerParams(vmem_limit_bytes=48 * 1024 * 1024),
        name="far",
    )(table, sel, nodes)


def far_inputs(vlist, base, cycle):
    rel = jnp.where(vlist >= 0, vlist - base, -1)
    sel = (rel.T[:, :, None] == jnp.arange(32)).astype(BF).reshape(rel.shape[1], 256)
    turned = jnp.transpose(cycle, (2, 0, 1))
    nodes = jnp.pad(jnp.concatenate([turned] * 4, axis=2), ((0, 0), (0, 8), (0, 0)))
    return sel, nodes


def dot3(a, b):
    ah, al = split2(a)
    bh, bl = split2(b)
    left = jnp.concatenate([ah, al], axis=0)
    r = jnp.dot(left, bh, preferred_element_type=F32)
    m = a.shape[0]
    return r[:m] + (r[m:] + jnp.dot(ah, bl, preferred_element_type=F32))


def up_kernel(
    pts, dens, surf, up_inv, shift_up, coarse,
    pts_lo, pts_hi, dens_lo, dens_hi, nodes, slab,
    check, node, near_top, far_top, send, recv,
):
    leaves, q_width = dens.shape[0], dens.shape[1]
    width = up_inv.shape[0]
    count = lax.axis_size("oct")
    me = lax.axis_index("oct")
    right = lax.rem(me + 1, count)
    left = lax.rem(me + count - 1, count)
    child = lax.rem(me, 8)
    row = me // 8
    rows = count // 8
    mates = [me - child + lax.rem(child + k, 8) for k in range(1, 8)]
    cousins = [lax.rem(row + k, rows) * 8 + child for k in range(1, rows)]

    barrier = pltpu.get_barrier_semaphore()
    for other in [left, right] + mates + cousins:
        pl.semaphore_signal(barrier, inc=1, device_id=(other,), device_id_type=pl.DeviceIdType.MESH)
    pl.semaphore_wait(barrier, 2 + len(mates) + len(cousins))

    def push(src, dst, sem, device):
        copy = pltpu.make_async_remote_copy(
            src_ref=src, dst_ref=dst, send_sem=send.at[sem], recv_sem=recv.at[sem],
            device_id=(device,), device_id_type=pl.DeviceIdType.MESH,
        )
        copy.start()
        return copy

    halo = [
        push(pts, pts_lo, 0, right),
        push(pts, pts_hi, 1, left),
        push(dens, dens_lo, 2, right),
        push(dens, dens_hi, 3, left),
    ]

    lane = lax.broadcasted_iota(jnp.int32, (32, 128), 1).astype(F32)
    lane_big = lax.broadcasted_iota(jnp.int32, (128, 128), 1)

    def leaf_group(g, carry):
        tiles = []
        for i in range(4):
            tiles += source_tiles([pts[c, pl.ds(4 * g + i, 1), :] for c in range(3)])
        turned = jnp.concatenate(tiles, axis=0).astype(BF).T
        for i in range(4):
            j = 4 * g + i
            own = (lane_big >= 32 * i) & (lane_big < 32 * i + 32)
            f = jnp.where(own, turned, jnp.zeros_like(turned))
            w = jnp.concatenate(
                [
                    jnp.concatenate(
                        target_tiles([surf[3 * h + c, pl.ds(j, 1), :] for c in range(3)]), axis=0
                    ).astype(BF)
                    for h in range(2)
                ],
                axis=1,
            )
            k = jnp.exp2(jnp.dot(f, jnp.concatenate([w] * 4, axis=0), preferred_element_type=F32))
            hi, lo = split2(k)
            used = jnp.broadcast_to(pts[3, pl.ds(j, 1), :], (32, 128))
            mh, ml = split2(jnp.where(lane < used, dens[j], 0.0))
            r = jnp.dot(
                jnp.concatenate([mh, ml], axis=0), jnp.concatenate([hi, lo], axis=1), preferred_element_type=F32
            )
            c = 4 * lax.rem(g, 2) + i
            n = g // 2
            check[c, pl.ds(pl.multiple_of(32 * n, 32), 32), :] = (r[:32, :256] + r[:32, 256:]) + (
                r[32:, :256] + r[32:, 256:]
            )
        return carry

    lax.fori_loop(0, leaves // 4, leaf_group, 0)
    node[...] = jnp.zeros_like(node)

    def merge(c, carry):
        both = dot3(up_inv[...], shift_up[c])
        node[...] += dot3(check[c][:, :width], both)
        return carry

    lax.fori_loop(0, 8, merge, 0)
    nodes[1] = node[...].astype(BF)
    halo.append(push(nodes.at[1], nodes.at[0], 4, right))
    halo.append(push(nodes.at[1], nodes.at[2], 5, left))

    def climb(c, total):
        return total + dot3(node[pl.ds(pl.multiple_of(32 * c, 32), 32), :], shift_up[c])

    top = lax.fori_loop(0, 8, climb, jnp.zeros((q_width, width), F32))
    near_top[0] = dot3(top, shift_up[child])
    copies = [push(near_top.at[0], near_top.at[k], 5 + k, mates[k - 1]) for k in range(1, 8)]
    for copy in copies:
        copy.wait_recv()
    top1 = near_top[0]
    for k in range(1, 8):
        top1 = top1 + near_top[k]
    far_top[0] = top1
    more = [push(far_top.at[0], far_top.at[k], 12 + k, cousins[k - 1]) for k in range(1, rows)]
    total = dot3(top1, coarse[child])
    for copy in more:
        copy.wait_recv()
    half = row // 8
    own = jnp.zeros((q_width, width), F32)
    other = jnp.zeros((q_width, width), F32)
    for k in range(8):
        src = lax.rem(row + rows - k, rows)
        pair = dot3(jnp.concatenate([far_top[k], far_top[k + 8]], axis=0), shift_up[lax.rem(src, 8)])
        same = jnp.where(src // 8 == half, 1.0, 0.0)
        a, b = pair[:q_width], pair[q_width:]
        own = own + (same * a + (1.0 - same) * b)
        other = other + ((1.0 - same) * a + same * b)
    top3 = dot3(own, shift_up[half]) + dot3(other, shift_up[1 - half])
    total = total + dot3(own, coarse[lax.rem(row, 8)]) + dot3(top3, coarse[half])
    slab[...] = total
    for copy in halo:
        copy.wait_recv()
    for copy in halo + copies + more:
        copy.wait_send()


def up_call(pts, dens, surf, up_inv, shift_up, coarse):
    leaves, q_width, _ = dens.shape
    width = up_inv.shape[0]
    vmem = pl.BlockSpec(memory_space=pltpu.VMEM)
    hbm = pl.BlockSpec(memory_space=pl.ANY)
    like = jax.ShapeDtypeStruct
    return pl.pallas_call(
        up_kernel,
        out_shape=[
            like(pts.shape, F32), like(pts.shape, F32), like(dens.shape, F32), like(dens.shape, F32),
            like((3, 8 * q_width, width), BF), like((q_width, width), F32),
        ],
        in_specs=[vmem] * 6,
        out_specs=[hbm] * 4 + [vmem] * 2,
        scratch_shapes=[
            pltpu.VMEM((8, 8 * q_width, 256), F32),
            pltpu.VMEM((8 * q_width, width), F32),
            pltpu.VMEM((8, q_width, width), F32),
            pltpu.VMEM((16, q_width, width), F32),
            pltpu.SemaphoreType.DMA((28,)),
            pltpu.SemaphoreType.DMA((28,)),
        ],
        compiler_params=pltpu.CompilerParams(
            vmem_limit_bytes=48 * 1024 * 1024, collective_id=0, has_side_effects=True
        ),
        name="upward",
    )(pts, dens, surf, up_inv, shift_up, coarse)


def local(
    points,
    dens,
    surface,
    counts,
    ulist,
    vlist,
    up_inverse,
    down_inverse,
    shift_up,
    shift_down,
    coarse,
    translate,
):
    leaf_count, q_width, p_width = dens.shape
    eq_width = surface.shape[2]
    node_count = vlist.shape[0]
    index = lax.axis_index("oct")
    turned_points = jnp.concatenate(
        [
            jnp.transpose(points, (1, 0, 2)),
            jnp.broadcast_to(counts.astype(F32)[None, :, None], (1, leaf_count, p_width)),
        ],
        axis=0,
    )
    surf = jnp.pad(jnp.transpose(surface, (1, 0, 2)), ((0, 0), (0, 0), (0, 256 - eq_width)))
    surf = jnp.concatenate([surf[:, :, :128], surf[:, :, 128:]], axis=0)
    points_lo, points_hi, dens_lo, dens_hi, cycle, slab_local = up_call(
        turned_points, dens, surf, up_inverse, shift_up, coarse
    )
    points3 = [points_lo, turned_points, points_hi]
    dens3 = [dens_lo, dens, dens_hi]
    counts3 = jnp.concatenate([p[3, :, 0] for p in points3]).astype(jnp.int32)
    lists = make_lists(ulist, counts3, (index - 1) * leaf_count)
    cycle = cycle.reshape(3 * node_count, q_width, eq_width)
    sel, nodes = far_inputs(vlist, (index - 1) * node_count, cycle)
    far_node = far_call(jnp.transpose(translate, (1, 2, 0)), sel, nodes)
    far_node = far_node.T.reshape(node_count, q_width, eq_width)
    parent_part = jnp.einsum("qe,cef->cqf", slab_local, shift_down, precision=HIGHEST)
    node_local = far_node + parent_part
    leaf_local = jnp.einsum("nqe,cef->ncqf", node_local, shift_down, precision=HIGHEST).reshape(
        leaf_count, q_width, eq_width
    )
    wide = 256
    pad = wide - eq_width
    leaf_down = jnp.dot(
        leaf_local.reshape(-1, eq_width),
        jnp.pad(down_inverse, ((0, 0), (0, pad))),
        precision=HIGHEST,
        preferred_element_type=jnp.float32,
    ).reshape(leaf_count, q_width, wide)
    return near_call(counts3, *lists, points3, dens3, surf, leaf_down)


def solution(mesh):
    placed = (
        P("oct", None, None),
        P("oct", None, None),
        P("oct", None, None),
        P("oct"),
        P("oct", None),
        P("oct", None),
        P(),
        P(),
        P(),
        P(),
        P(),
        P(),
    )
    return jax.shard_map(
        local, mesh=mesh, in_specs=placed, out_specs=P("oct", None, None), check_vma=False
    )
```

```python
import functools

import jax
import jax.numpy as jnp
from jax import lax
from jax.experimental import pallas as pl
from jax.experimental.pallas import tpu as pltpu
from jax.sharding import PartitionSpec as P

BF = jnp.bfloat16
F32 = jnp.float32
LIST = 128


def split2(x):
    hi = x.astype(BF)
    lo = (x - hi.astype(F32)).astype(BF)
    return hi, lo


def split3(x):
    a = x.astype(BF).astype(F32)
    r = x - a
    b = r.astype(BF).astype(F32)
    return a, b, r - b


def rows8(shape):
    return lax.broadcasted_iota(jnp.int32, shape, 0)


LOG2E = 1.4426950408889634


def source_tiles(coords):
    out = []
    norm = None
    row = rows8((8, 128))
    for c in coords:
        x = jnp.broadcast_to(c, (8, 128))
        a, b, d = split3(LOG2E * x)
        first = (row <= 1) | (row == 4)
        out.append(jnp.where(first, a, jnp.where(row <= 3, b, jnp.where(row == 5, d, 0.0))))
        norm = x * x if norm is None else norm + x * x
    a, b, d = split3((-0.5 * LOG2E) * norm)
    out.append(
        jnp.where(row == 0, a, jnp.where(row == 1, b, jnp.where(row == 2, d, jnp.where(row <= 5, 1.0, 0.0))))
    )
    return out


def target_tiles(coords):
    out = []
    norm = None
    row = rows8((8, 128))
    for c in coords:
        x = jnp.broadcast_to(c, (8, 128))
        a, b, d = split3(x)
        first = (row == 0) | (row == 2) | (row == 5)
        second = (row == 1) | (row == 3)
        out.append(jnp.where(first, a, jnp.where(second, b, jnp.where(row == 4, d, 0.0))))
        norm = x * x if norm is None else norm + x * x
    a, b, d = split3((-0.5 * LOG2E) * norm)
    out.append(
        jnp.where(row <= 2, 1.0, jnp.where(row == 3, a, jnp.where(row == 4, b, jnp.where(row == 5, d, 0.0))))
    )
    return out


def near_kernel(leaves, cnt, units, ptr, leaf, total_ref, p0, p1, p2, d0, d1, d2, surf, down, out, f_s, m_s, w_s, e_s, acc):
    lane = lax.broadcasted_iota(jnp.int32, (32, 128), 1)
    lane_big = lax.broadcasted_iota(jnp.int32, (128, 128), 1)
    zero_unit = 4 * (3 * leaves + 2 * leaves)

    def put_features(coords4, base_units):
        tiles = []
        for coords in coords4:
            tiles += source_tiles(coords)
        turned = jnp.concatenate(tiles, axis=0).astype(BF).T
        for i in range(4):
            own = (lane_big >= 32 * i) & (lane_big < 32 * i + 32)
            f_s[pl.ds(base_units[i], 4)] = jnp.where(own, turned, jnp.zeros_like(turned)).reshape(4, 32, 128)

    def put_density(tile, base):
        for k in range(4):
            r = tile if k == 0 else pltpu.roll(tile, 32 * k, 1)
            hi, lo = split2(r)
            m_s[base + k] = jnp.concatenate([hi, lo], axis=0)

    for slab, (p, d) in enumerate(((p0, d0), (p1, d1), (p2, d2))):

        def prep(g, carry, slab=slab, p=p, d=d):
            coords4 = [[p[c, pl.ds(4 * g + i, 1), :] for c in range(3)] for i in range(4)]
            put_features(coords4, [4 * (slab * leaves + 4 * g + i) for i in range(4)])
            for i in range(4):
                j = 4 * g + i
                masked = jnp.where(lane < cnt[slab * leaves + j], d[j], 0.0)
                put_density(masked, 4 * (slab * leaves + j))
            return carry

        lax.fori_loop(0, leaves // 4, prep, 0)

    def prep_surface(g, carry):
        coords4 = [[surf[3 * (i % 2) + c, pl.ds(2 * g + i // 2, 1), :] for c in range(3)] for i in range(4)]
        put_features(coords4, [4 * (3 * leaves + 4 * g + i) for i in range(4)])
        for i in range(4):
            put_density(down[2 * g + i // 2, :, pl.ds(128 * (i % 2), 128)], 4 * (3 * leaves + 4 * g + i))
        return carry

    lax.fori_loop(0, leaves // 2, prep_surface, 0)
    f_s[pl.ds(zero_unit, 4)] = jnp.zeros((4, 32, 128), BF)
    m_s[pl.ds(zero_unit, 4)] = jnp.zeros((4, 64, 128), BF)

    def prep_target(j, carry):
        tile = jnp.concatenate(target_tiles([p1[c, pl.ds(j, 1), :] for c in range(3)]), axis=0).astype(BF)
        w_s[j] = jnp.concatenate([tile] * 4, axis=0)
        acc[j] = jnp.zeros((64, 256), F32)
        return carry

    lax.fori_loop(0, leaves, prep_target, 0)

    lane64 = lax.broadcasted_iota(jnp.int32, (64, 128), 1)

    def exponents(i, slot):
        base, l = ptr[i], leaf[i]
        left = jnp.concatenate([f_s[units[base + v]] for v in range(4)], axis=0)
        right = jnp.concatenate([f_s[units[base + 4 + v]] for v in range(4)], axis=0)
        w = w_s[l]
        e_s[slot, 0] = jnp.dot(left, w, preferred_element_type=F32)
        e_s[slot, 1] = jnp.dot(right, w, preferred_element_type=F32)

    def weights(base):
        t = [m_s[units[base + v]] for v in range(4)]
        return jnp.where(
            lane64 < 64, jnp.where(lane64 < 32, t[0], t[1]), jnp.where(lane64 < 96, t[2], t[3])
        )

    def apply(i, slot):
        base, l = ptr[i], leaf[i]
        m = jnp.concatenate([weights(base + 8), weights(base + 12)], axis=1)
        k = jnp.exp2(e_s[slot].reshape(256, 128))
        hi, lo = split2(k)
        acc[l] += jnp.dot(m, jnp.concatenate([hi, lo], axis=1), preferred_element_type=F32)

    half = 4
    for u in range(half):
        exponents(u, u)

    def body(i, carry):
        at = 2 * half * i
        for u in range(half):
            exponents(at + half + u, half + u)
            apply(at + u, u)
        for u in range(half):
            exponents(at + 2 * half + u, u)
            apply(at + half + u, half + u)
        return carry

    lax.fori_loop(0, total_ref[0], body, 0)

    def finish(j, carry):
        a = acc[j]
        v = (a[:32, :128] + a[:32, 128:]) + (a[32:, :128] + a[32:, 128:])
        out[j] = jnp.where(lane < cnt[leaves + j], v, 0.0)
        return carry

    lax.fori_loop(0, leaves, finish, 0)


def near_call(cnt, units_list, ptr, leaf, total, pts, dens, surf, down):
    leaves = dens[0].shape[0]
    units = 4 * (3 * leaves + 2 * leaves) + 4
    smem = pl.BlockSpec(memory_space=pltpu.SMEM)
    vmem = pl.BlockSpec(memory_space=pltpu.VMEM)
    return pl.pallas_call(
        functools.partial(near_kernel, leaves),
        out_shape=jax.ShapeDtypeStruct(dens[0].shape, F32),
        in_specs=[smem] * 5 + [vmem] * 8,
        out_specs=vmem,
        scratch_shapes=[
            pltpu.VMEM((units, 32, 128), BF),
            pltpu.VMEM((units, 64, 128), BF),
            pltpu.VMEM((leaves, 128, 128), BF),
            pltpu.VMEM((8, 2, 128, 128), F32),
            pltpu.VMEM((leaves, 64, 256), F32),
        ],
        compiler_params=pltpu.CompilerParams(vmem_limit_bytes=60 * 1024 * 1024),
        name="near",
    )(cnt, units_list, ptr, leaf, total, *pts, *dens, surf, down)


def make_lists(ulist, counts3, first):
    leaves = ulist.shape[0]
    ids = jnp.arange(3 * leaves)
    rel = jnp.where(ulist >= 0, ulist - first, -1)
    cnt = jnp.sum(jnp.where(rel[:, :, None] == ids, counts3, 0), axis=-1)
    num = (cnt + 31) // 32
    slots = ulist.shape[1]
    before = jnp.arange(slots)[:, None] < jnp.arange(slots)[None, :]
    start = 5 + jnp.sum(jnp.where(before, num[:, :, None], 0), axis=1)
    place = jnp.arange(LIST)
    at = place - start[:, :, None]
    inside = (at >= 0) & (at < num[:, :, None])
    zero_unit = 20 * leaves
    unit = zero_unit + jnp.sum(jnp.where(inside, 4 * rel[:, :, None] + at - zero_unit, 0), axis=1)
    surface_unit = 12 * leaves + 8 * jnp.arange(leaves)[:, None] + place
    unit = jnp.where(place < 5, surface_unit, unit).astype(jnp.int32)
    turned = (unit - unit % 4) + (place - unit) % 4
    n = (5 + jnp.sum(num, axis=1) + 7) // 8
    upto = jnp.arange(leaves)[:, None] <= jnp.arange(leaves)[None, :]
    end = jnp.sum(jnp.where(upto, n[:, None], 0), axis=0)
    begin = end - n
    chunk = jnp.arange(16 * leaves + 16)
    inside = (chunk[:, None] >= begin) & (chunk[:, None] < end)
    leaf = jnp.sum(jnp.where(inside, jnp.arange(leaves), 0), axis=1)
    ptr = jnp.sum(jnp.where(inside, 16 * (16 * jnp.arange(leaves) + chunk[:, None] - begin), 0), axis=1)
    ptr = jnp.where(chunk < end[-1], ptr, 256 * leaves)
    both = jnp.stack([unit.reshape(leaves, 16, 8), turned.reshape(leaves, 16, 8)], axis=2).reshape(-1)
    both = jnp.concatenate([both, jnp.full((16,), zero_unit)])
    rounds = ((end[-1] + 7) // 8).reshape(1)
    return [v.astype(jnp.int32) for v in (both, ptr, leaf, rounds)]


def dot3(a, b):
    ah, al = split2(a)
    bh, bl = split2(b)
    left = jnp.concatenate([ah, al], axis=0)
    r = jnp.dot(left, bh, preferred_element_type=F32)
    m = a.shape[0]
    return r[:m] + (r[m:] + jnp.dot(ah, bl, preferred_element_type=F32))


def up_kernel(
    pts, dens, surf, sel, up_inv, down_inv, shift_up, shift_down, coarse, table,
    pts_lo, pts_hi, dens_lo, dens_hi, down,
    check, node, nodes, near_top, far_top, held, sources, far_sum, send, recv, table_sem,
):
    leaves, q_width = dens.shape[0], dens.shape[1]
    width = up_inv.shape[0]
    count = lax.axis_size("oct")
    me = lax.axis_index("oct")
    right = lax.rem(me + 1, count)
    left = lax.rem(me + count - 1, count)
    child = lax.rem(me, 8)
    row = me // 8
    rows = count // 8
    mates = [me - child + lax.rem(child + k, 8) for k in range(1, 8)]
    cousins = [lax.rem(row + k, rows) * 8 + child for k in range(1, rows)]

    def fetch(b):
        part = pl.ds(pl.multiple_of(STEP * b, STEP), STEP)
        return pltpu.make_async_copy(table.at[part], held.at[part], table_sem.at[b])

    def fetch_start(b, carry):
        fetch(b).start()
        return carry

    blocks = held.shape[0] // STEP
    lax.fori_loop(0, blocks, fetch_start, 0)
    barrier = pltpu.get_barrier_semaphore()
    for other in [left, right] + mates + cousins:
        pl.semaphore_signal(barrier, inc=1, device_id=(other,), device_id_type=pl.DeviceIdType.MESH)
    pl.semaphore_wait(barrier, 2 + len(mates) + len(cousins))

    def push(src, dst, sem, device):
        copy = pltpu.make_async_remote_copy(
            src_ref=src, dst_ref=dst, send_sem=send.at[sem], recv_sem=recv.at[sem],
            device_id=(device,), device_id_type=pl.DeviceIdType.MESH,
        )
        copy.start()
        return copy

    halo = [
        push(pts, pts_lo, 0, right),
        push(pts, pts_hi, 1, left),
        push(dens, dens_lo, 2, right),
        push(dens, dens_hi, 3, left),
    ]

    lane = lax.broadcasted_iota(jnp.int32, (32, 128), 1).astype(F32)
    lane_big = lax.broadcasted_iota(jnp.int32, (128, 128), 1)

    def leaf_group(g, carry):
        tiles = []
        for i in range(4):
            tiles += source_tiles([pts[c, pl.ds(4 * g + i, 1), :] for c in range(3)])
        turned = jnp.concatenate(tiles, axis=0).astype(BF).T
        for i in range(4):
            j = 4 * g + i
            own = (lane_big >= 32 * i) & (lane_big < 32 * i + 32)
            f = jnp.where(own, turned, jnp.zeros_like(turned))
            w = jnp.concatenate(
                [
                    jnp.concatenate(
                        target_tiles([surf[3 * h + c, pl.ds(j, 1), :] for c in range(3)]), axis=0
                    ).astype(BF)
                    for h in range(2)
                ],
                axis=1,
            )
            k = jnp.exp2(jnp.dot(f, jnp.concatenate([w] * 4, axis=0), preferred_element_type=F32))
            hi, lo = split2(k)
            used = jnp.broadcast_to(pts[3, pl.ds(j, 1), :], (32, 128))
            mh, ml = split2(jnp.where(lane < used, dens[j], 0.0))
            r = jnp.dot(
                jnp.concatenate([mh, ml], axis=0), jnp.concatenate([hi, lo], axis=1), preferred_element_type=F32
            )
            c = 4 * lax.rem(g, 2) + i
            n = g // 2
            check[c, pl.ds(pl.multiple_of(32 * n, 32), 32), :] = (r[:32, :256] + r[:32, 256:]) + (
                r[32:, :256] + r[32:, 256:]
            )
        return carry

    lax.fori_loop(0, leaves // 4, leaf_group, 0)
    node[...] = jnp.zeros_like(node)
    far_sum[...] = jnp.zeros_like(far_sum)
    down[...] = jnp.zeros_like(down)

    def merge(c, carry):
        both = dot3(up_inv[...], shift_up[c])
        node[...] += dot3(check[c][:, :width], both)
        return carry

    lax.fori_loop(0, 8, merge, 0)
    nodes[1, :, :width] = node[...].astype(BF)
    halo.append(push(nodes.at[1], nodes.at[0], 4, right))
    halo.append(push(nodes.at[1], nodes.at[2], 5, left))

    def climb(c, total):
        return total + dot3(node[pl.ds(pl.multiple_of(32 * c, 32), 32), :], shift_up[c])

    top = lax.fori_loop(0, 8, climb, jnp.zeros((q_width, width), F32))
    near_top[0, :, :width] = dot3(top, shift_up[child])
    copies = [push(near_top.at[0], near_top.at[k], 5 + k, mates[k - 1]) for k in range(1, 8)]

    def turn(slab):
        x = nodes[slab].astype(F32)
        for i in range(8):
            rows32 = x[32 * i : 32 * i + 32]
            turned = jnp.concatenate([rows32] * 4, axis=0).T
            sources[slab, :, i, :] = turned[:width]

    turn(1)
    for copy in halo[4:]:
        copy.wait_recv()
    turn(0)
    turn(2)
    picks = sel[...]

    def far_block(b, carry):
        fetch(b).wait()
        far_sum[:width, :] += far_step(lambda k: held[STEP * b + k], picks, lambda k: [sources[h, STEP * b + k] for h in range(3)], width)
        return carry

    lax.fori_loop(0, blocks // 3, far_block, 0)
    for copy in copies:
        copy.wait_recv()
    top1 = near_top[0, :, :width]
    for k in range(1, 8):
        top1 = top1 + near_top[k, :, :width]
    far_top[0, :, :width] = top1
    more = [push(far_top.at[0], far_top.at[k], 12 + k, cousins[k - 1]) for k in range(1, rows)]
    total = dot3(top1, coarse[child])
    lax.fori_loop(blocks // 3, 2 * blocks // 3, far_block, 0)
    for copy in more:
        copy.wait_recv()
    half = row // 8
    own = jnp.zeros((q_width, width), F32)
    other = jnp.zeros((q_width, width), F32)
    for k in range(8):
        src = lax.rem(row + rows - k, rows)
        pair = dot3(jnp.concatenate([far_top[k, :, :width], far_top[k + 8, :, :width]], axis=0), shift_up[lax.rem(src, 8)])
        same = jnp.where(src // 8 == half, 1.0, 0.0)
        a, b = pair[:q_width], pair[q_width:]
        own = own + (same * a + (1.0 - same) * b)
        other = other + ((1.0 - same) * a + same * b)
    top3 = dot3(own, shift_up[half]) + dot3(other, shift_up[1 - half])
    total = total + dot3(own, coarse[lax.rem(row, 8)]) + dot3(top3, coarse[half])
    lax.fori_loop(2 * blocks // 3, blocks, far_block, 0)
    node[...] = far_sum[...].T[:, :width]

    def parent(c, carry):
        at = pl.ds(pl.multiple_of(32 * c, 32), 32)
        node[at, :] = node[at, :] + dot3(total, shift_down[c])
        return carry

    lax.fori_loop(0, 8, parent, 0)

    def descend(c, carry):
        leaf = dot3(node[...], dot3(shift_down[c], down_inv[...]))
        for n in range(8):
            down[8 * n + c, :, :width] = leaf[32 * n : 32 * n + 32]
        return carry

    lax.fori_loop(0, 8, descend, 0)
    for copy in halo[:4]:
        copy.wait_recv()
    for copy in halo + copies + more:
        copy.wait_send()


STEP = 8


def far_step(table_at, picks, rows_at, width):
    lane = lax.broadcasted_iota(jnp.int32, (32, 128), 1)
    zero = jnp.zeros((32, 128), BF)
    total = None
    for k in range(0, STEP, 2):
        sums = []
        rows = []
        for e in (k, k + 1):
            s = jnp.dot(table_at(e), picks, preferred_element_type=F32)
            hi, lo = split2(s)
            sums.append(jnp.concatenate([hi, lo], axis=0))
            x = jnp.concatenate(rows_at(e) + [jnp.zeros((8, 128), F32)], axis=0).astype(BF)
            for n in range(8):
                own = (lane >= 32 * (n % 4)) & (lane < 32 * (n % 4) + 32)
                part = jnp.where(own, x, zero)
                rows.append(jnp.concatenate([part, zero] if n < 4 else [zero, part], axis=1))
        r = jnp.dot(
            jnp.concatenate(sums, axis=1), jnp.concatenate(rows, axis=0), preferred_element_type=F32
        )
        r = r[:width] + r[width:]
        total = r if total is None else total + r
    return total


def up_call(pts, dens, surf, sel, up_inv, down_inv, shift_up, shift_down, coarse, table):
    leaves, q_width, _ = dens.shape
    width = up_inv.shape[0]
    vmem = pl.BlockSpec(memory_space=pltpu.VMEM)
    hbm = pl.BlockSpec(memory_space=pl.ANY)
    like = jax.ShapeDtypeStruct
    rows = 8 * q_width
    return pl.pallas_call(
        up_kernel,
        out_shape=[
            like(pts.shape, F32), like(pts.shape, F32), like(dens.shape, F32), like(dens.shape, F32),
            like((leaves, q_width, 256), F32),
        ],
        in_specs=[vmem] * 9 + [hbm],
        out_specs=[hbm] * 4 + [vmem],
        scratch_shapes=[
            pltpu.VMEM((8, rows, 256), F32),
            pltpu.VMEM((rows, width), F32),
            pltpu.VMEM((3, rows, 256), BF),
            pltpu.VMEM((8, q_width, 256), F32),
            pltpu.VMEM((16, q_width, 256), F32),
            pltpu.VMEM(table.shape, BF),
            pltpu.VMEM((3, width, 8, 128), F32),
            pltpu.VMEM((256, rows), F32),
            pltpu.SemaphoreType.DMA((28,)),
            pltpu.SemaphoreType.DMA((28,)),
            pltpu.SemaphoreType.DMA((table.shape[0] // STEP,)),
        ],
        compiler_params=pltpu.CompilerParams(
            vmem_limit_bytes=56 * 1024 * 1024, collective_id=0, has_side_effects=True
        ),
        name="upward",
    )(pts, dens, surf, sel, up_inv, down_inv, shift_up, shift_down, coarse, table)


def local(
    points,
    dens,
    surface,
    counts,
    ulist,
    vlist,
    up_inverse,
    down_inverse,
    shift_up,
    shift_down,
    coarse,
    translate,
):
    leaf_count, q_width, p_width = dens.shape
    eq_width = surface.shape[2]
    node_count = vlist.shape[0]
    index = lax.axis_index("oct")
    turned_points = jnp.concatenate(
        [
            jnp.transpose(points, (1, 0, 2)),
            jnp.broadcast_to(counts.astype(F32)[None, :, None], (1, leaf_count, p_width)),
        ],
        axis=0,
    )
    surf = jnp.pad(jnp.transpose(surface, (1, 0, 2)), ((0, 0), (0, 0), (0, 256 - eq_width)))
    surf = jnp.concatenate([surf[:, :, :128], surf[:, :, 128:]], axis=0)
    rel = jnp.where(vlist >= 0, vlist - (index - 1) * node_count, -1)
    sel = (rel.T[:, :, None] == jnp.arange(32)).astype(BF).reshape(rel.shape[1], 256)
    points_lo, points_hi, dens_lo, dens_hi, leaf_down = up_call(
        turned_points, dens, surf, sel, up_inverse, down_inverse, shift_up, shift_down, coarse,
        jnp.transpose(translate, (1, 2, 0)),
    )
    points3 = [points_lo, turned_points, points_hi]
    dens3 = [dens_lo, dens, dens_hi]
    counts3 = jnp.concatenate([p[3, :, 0] for p in points3]).astype(jnp.int32)
    lists = make_lists(ulist, counts3, (index - 1) * leaf_count)
    return near_call(counts3, *lists, points3, dens3, surf, leaf_down)


def solution(mesh):
    placed = (
        P("oct", None, None),
        P("oct", None, None),
        P("oct", None, None),
        P("oct"),
        P("oct", None),
        P("oct", None),
        P(),
        P(),
        P(),
        P(),
        P(),
        P(),
    )
    return jax.shard_map(
        local, mesh=mesh, in_specs=placed, out_specs=P("oct", None, None), check_vma=False
    )
```

```python
import functools

import jax
import jax.numpy as jnp
from jax import lax
from jax.experimental import pallas as pl
from jax.experimental.pallas import tpu as pltpu
from jax.sharding import PartitionSpec as P

BF = jnp.bfloat16
F32 = jnp.float32


def split2(x):
    hi = x.astype(BF)
    lo = (x - hi.astype(F32)).astype(BF)
    return hi, lo


def split3(x):
    a = x.astype(BF).astype(F32)
    r = x - a
    b = r.astype(BF).astype(F32)
    return a, b, r - b


def rows8(shape):
    return lax.broadcasted_iota(jnp.int32, shape, 0)


LOG2E = 1.4426950408889634


def source_tiles(coords):
    out = []
    norm = None
    row = rows8((8, 128))
    for c in coords:
        x = jnp.broadcast_to(c, (8, 128))
        a, b, d = split3(LOG2E * x)
        first = (row <= 1) | (row == 4)
        out.append(jnp.where(first, a, jnp.where(row <= 3, b, jnp.where(row == 5, d, 0.0))))
        norm = x * x if norm is None else norm + x * x
    a, b, d = split3((-0.5 * LOG2E) * norm)
    out.append(
        jnp.where(row == 0, a, jnp.where(row == 1, b, jnp.where(row == 2, d, jnp.where(row <= 5, 1.0, 0.0))))
    )
    return out


def target_tiles(coords):
    out = []
    norm = None
    row = rows8((8, 128))
    for c in coords:
        x = jnp.broadcast_to(c, (8, 128))
        a, b, d = split3(x)
        first = (row == 0) | (row == 2) | (row == 5)
        second = (row == 1) | (row == 3)
        out.append(jnp.where(first, a, jnp.where(second, b, jnp.where(row == 4, d, 0.0))))
        norm = x * x if norm is None else norm + x * x
    a, b, d = split3((-0.5 * LOG2E) * norm)
    out.append(
        jnp.where(row <= 2, 1.0, jnp.where(row == 3, a, jnp.where(row == 4, b, jnp.where(row == 5, d, 0.0))))
    )
    return out


LIST_ROWS = 128
TABLE_ROWS = 2 * LIST_ROWS
LEAF_AT, PTR_AT, COUNT_AT, ROUNDS_AT = 0, 12, 26, 31
GROUP = 16


def plan_kernel(leaves, first, ulist, c0, c1, c2, out, ids):
    slots = ulist.shape[0]
    lane = lax.broadcasted_iota(jnp.int32, (32, 128), 1)
    ids[...] = jnp.full((32, 128), -1, jnp.int32)
    ids[:slots, :leaves] = ulist[...]
    rel = ids[...]
    rel = jnp.where(rel >= 0, rel - first[0], -1)
    counts = [c[0, :1, :].astype(jnp.int32) for c in (c0, c1, c2)]
    nun = [jnp.right_shift(jnp.broadcast_to(c, (32, 128)) + 31, 5) for c in counts]
    low = jnp.where(lane < leaves, nun[0], pltpu.roll(nun[1], leaves, 1))
    from_low = jnp.take_along_axis(low, jnp.clip(rel, 0, 127), axis=1, mode="promise_in_bounds")
    from_high = jnp.take_along_axis(nun[2], jnp.clip(rel - 2 * leaves, 0, 127), axis=1, mode="promise_in_bounds")
    num = jnp.where(rel < 0, 0, jnp.where(rel < 2 * leaves, from_low, from_high))
    before = lax.broadcasted_iota(jnp.int32, (32, 32), 1) < lax.broadcasted_iota(jnp.int32, (32, 32), 0)
    start = 5 + jnp.dot(
        jnp.where(before, 1.0, 0.0).astype(BF), num.astype(F32).astype(BF), preferred_element_type=F32
    ).astype(jnp.int32)
    place = lax.broadcasted_iota(jnp.int32, (LIST_ROWS, 128), 0)
    mine = lax.broadcasted_iota(jnp.int32, (LIST_ROWS, 128), 1)
    unit = jnp.where(place < 4, 12 * leaves + 4 * mine + place, jnp.where(place == 4, 16 * leaves + mine, 17 * leaves))
    for s in range(slots):
        at = place - start[s : s + 1]
        inside = (at >= 0) & (at < num[s : s + 1])
        unit = jnp.where(inside, 4 * rel[s : s + 1] + at, unit)
    out[:LIST_ROWS, :] = unit
    out[LIST_ROWS:TABLE_ROWS, :] = jnp.bitwise_and(unit, -4) + jnp.bitwise_and(place - unit, 3)
    n = jnp.right_shift(start[31:] + num[31:] + 7, 3)
    n = jnp.where(lane[:1] < leaves, n, 0)
    column = jnp.broadcast_to(n.astype(F32), (128, 128)).T
    upto = lax.broadcasted_iota(jnp.int32, (128, 128), 1) <= lax.broadcasted_iota(jnp.int32, (128, 128), 0)
    end = jnp.dot(jnp.where(upto, 1.0, 0.0).astype(BF), column.astype(BF), preferred_element_type=F32)
    begin = (end - column).astype(jnp.int32)
    end = end.astype(jnp.int32)
    total = end[127:]
    out[TABLE_ROWS:, :] = jnp.zeros((32, 128), jnp.int32)
    for r in range(9):
        chunk = 128 * r + mine
        inside = (chunk >= begin) & (chunk < end)
        leaf = jnp.sum(jnp.where(inside, place, 0), axis=0, keepdims=True)
        ptr = jnp.sum(jnp.where(inside, (chunk - begin) * 1024 + place, 0), axis=0, keepdims=True)
        ptr = jnp.where(chunk[:1] < total, ptr, 120 * 128)
        out[TABLE_ROWS + LEAF_AT + r : TABLE_ROWS + LEAF_AT + r + 1, :] = leaf
        out[TABLE_ROWS + PTR_AT + r : TABLE_ROWS + PTR_AT + r + 1, :] = ptr
    for slab in range(3):
        out[TABLE_ROWS + COUNT_AT + slab : TABLE_ROWS + COUNT_AT + slab + 1, :] = counts[slab]
    out[TABLE_ROWS + ROUNDS_AT :, :] = jnp.right_shift(total + GROUP - 1, 4)


def plan_call(first, ulist, points3):
    leaves = ulist.shape[1]
    row = pl.BlockSpec((1, 8, 128), lambda i: (4, 0, 0))
    return pl.pallas_call(
        functools.partial(plan_kernel, leaves),
        grid=(1,),
        out_shape=jax.ShapeDtypeStruct((TABLE_ROWS + 32, 128), jnp.int32),
        in_specs=[pl.BlockSpec(memory_space=pltpu.SMEM), pl.BlockSpec(memory_space=pltpu.VMEM), row, row, row],
        out_specs=pl.BlockSpec(memory_space=pltpu.VMEM),
        scratch_shapes=[pltpu.VMEM((32, 128), jnp.int32)],
        name="plan",
    )(first, ulist, *points3).reshape(-1)


def near_kernel(leaves, plan, p0, p1, p2, d0, d1, d2, surf, down, down_tail, out, f_s, m_s, w_s, e_s, acc):
    lane = lax.broadcasted_iota(jnp.int32, (32, 128), 1)
    maps = 128 * TABLE_ROWS

    def used(slab, j):
        return plan[maps + 128 * (COUNT_AT + slab) + j]

    lane_big = lax.broadcasted_iota(jnp.int32, (128, 128), 1)
    row_big = lax.broadcasted_iota(jnp.int32, (128, 128), 0)
    zero_unit = 4 * (3 * leaves + leaves + leaves // 4)
    shifts = jnp.concatenate(
        [jnp.where(lane_big == (row_big + 32 * k) % 128, 1.0, 0.0).astype(BF) for k in range(1, 4)], axis=1
    )

    def put_features(coords4, base):
        tiles = []
        for coords in coords4:
            tiles += source_tiles(coords)
        tile = jnp.concatenate(tiles, axis=0).astype(BF)
        turned = tile.T
        for i in range(4):
            own = (lane_big >= 32 * i) & (lane_big < 32 * i + 32)
            f_s[pl.ds(base + 4 * i, 4)] = jnp.where(own, turned, jnp.zeros_like(turned)).reshape(4, 32, 128)

    def put_density(tiles, base):
        parts = []
        for i, tile in enumerate(tiles):
            hi, lo = split2(tile)
            parts.append(jnp.concatenate([hi, lo], axis=0))
            m_s[base + 4 * i] = parts[i]
        moved = jnp.dot(jnp.concatenate(parts, axis=0), shifts, preferred_element_type=F32).astype(BF)
        for i in range(4):
            for k in range(1, 4):
                m_s[base + 4 * i + k] = moved[64 * i : 64 * i + 64, 128 * (k - 1) : 128 * k]

    for slab, (p, d) in enumerate(((p0, d0), (p1, d1), (p2, d2))):

        def prep(g, carry, slab=slab, p=p, d=d):
            for half in range(4):
                first = 16 * g + 4 * half
                coords4 = [[p[c, pl.ds(first + i, 1), :] for c in range(3)] for i in range(4)]
                put_features(coords4, 4 * (slab * leaves + first))
                masked = [
                    jnp.where(lane < used(slab, first + i), d[first + i], 0.0) for i in range(4)
                ]
                put_density(masked, 4 * (slab * leaves + first))
            return carry

        lax.fori_loop(0, leaves // 16, prep, 0)

    def prep_surface(count, row0, view):
        def body(g, carry):
            for half in range(4):
                first = 16 * g + 4 * half
                coords4 = [[surf[c, pl.ds(row0 + first + i, 1), :] for c in range(3)] for i in range(4)]
                put_features(coords4, 4 * (3 * leaves + row0 + first))
                put_density([view(first + i) for i in range(4)], 4 * (3 * leaves + row0 + first))
            return carry

        lax.fori_loop(0, count // 16, body, 0)

    prep_surface(leaves, 0, lambda j: down[j])
    prep_surface(leaves // 4, leaves, lambda j: down_tail[j])
    f_s[pl.ds(zero_unit, 4)] = jnp.zeros((4, 32, 128), BF)
    m_s[pl.ds(zero_unit, 4)] = jnp.zeros((4, 64, 128), BF)

    def prep_target(g, carry):
        for i in range(4):
            j = 4 * g + i
            tile = jnp.concatenate(target_tiles([p1[c, pl.ds(j, 1), :] for c in range(3)]), axis=0).astype(BF)
            w_s[j] = jnp.concatenate([tile] * 4, axis=0)
            acc[j] = jnp.zeros((64, 256), F32)
        return carry

    lax.fori_loop(0, leaves // 4, prep_target, 0)

    lane64 = lax.broadcasted_iota(jnp.int32, (64, 128), 1)

    def exponents(i, slot):
        base, l = plan[maps + 128 * PTR_AT + i], plan[maps + 128 * LEAF_AT + i]
        left = jnp.concatenate([f_s[plan[base + 128 * v]] for v in range(4)], axis=0)
        right = jnp.concatenate([f_s[plan[base + 128 * (4 + v)]] for v in range(4)], axis=0)
        w = w_s[l]
        e_s[slot, 0] = jnp.dot(left, w, preferred_element_type=F32)
        e_s[slot, 1] = jnp.dot(right, w, preferred_element_type=F32)

    def weights(base):
        t = [m_s[plan[base + 128 * v]] for v in range(4)]
        return jnp.where(
            lane64 < 64, jnp.where(lane64 < 32, t[0], t[1]), jnp.where(lane64 < 96, t[2], t[3])
        )

    def apply(i, slot):
        base, l = plan[maps + 128 * PTR_AT + i], plan[maps + 128 * LEAF_AT + i]
        m = jnp.concatenate([weights(base + 128 * LIST_ROWS), weights(base + 128 * (LIST_ROWS + 4))], axis=1)
        k = jnp.exp2(e_s[slot].reshape(256, 128))
        hi, lo = split2(k)
        acc[l] += jnp.dot(m, jnp.concatenate([hi, lo], axis=1), preferred_element_type=F32)

    half = 8
    for u in range(half):
        exponents(u, u)

    def body(i, carry):
        at = 2 * half * i
        for u in range(half):
            exponents(at + half + u, half + u)
            apply(at + u, u)
        for u in range(half):
            exponents(at + 2 * half + u, u)
            apply(at + half + u, half + u)
        return carry

    lax.fori_loop(0, plan[maps + 128 * ROUNDS_AT], body, 0)

    def finish(g, carry):
        for i in range(4):
            j = 4 * g + i
            a = acc[j]
            v = (a[:32, :128] + a[:32, 128:]) + (a[32:, :128] + a[32:, 128:])
            out[j] = jnp.where(lane < used(1, j), v, 0.0)
        return carry

    lax.fori_loop(0, leaves // 4, finish, 0)


def near_call(plan, pts, dens, surf, down, down_tail):
    leaves = dens[0].shape[0]
    units = 4 * (3 * leaves + leaves + leaves // 4) + 4
    smem = pl.BlockSpec(memory_space=pltpu.SMEM)
    vmem = pl.BlockSpec(memory_space=pltpu.VMEM)
    return pl.pallas_call(
        functools.partial(near_kernel, leaves),
        out_shape=jax.ShapeDtypeStruct(dens[0].shape, F32),
        in_specs=[smem] + [vmem] * 9,
        out_specs=vmem,
        scratch_shapes=[
            pltpu.VMEM((units, 32, 128), BF),
            pltpu.VMEM((units, 64, 128), BF),
            pltpu.VMEM((leaves, 128, 128), BF),
            pltpu.VMEM((16, 2, 128, 128), F32),
            pltpu.VMEM((leaves, 64, 256), F32),
        ],
        compiler_params=pltpu.CompilerParams(vmem_limit_bytes=60 * 1024 * 1024),
        name="near",
    )(plan, *pts, *dens, surf, down, down_tail)


def dot3(a, b):
    ah, al = split2(a)
    bh, bl = split2(b)
    left = jnp.concatenate([ah, al], axis=0)
    r = jnp.dot(left, bh, preferred_element_type=F32)
    m = a.shape[0]
    return r[:m] + (r[m:] + jnp.dot(ah, bl, preferred_element_type=F32))


def up_kernel(
    pts, dens, surf, sel, up_inv, down_inv, shift_up, shift_down, coarse, table,
    pts_lo, pts_hi, dens_lo, dens_hi, down, down_tail,
    check, node, nodes, near_top, far_top, held, sources, far_sum, picked, leaf_sum, send, recv, table_sem,
):
    leaves, q_width = dens.shape[0], dens.shape[1]
    width = up_inv.shape[0]
    count = lax.axis_size("oct")
    me = lax.axis_index("oct")
    right = lax.rem(me + 1, count)
    left = lax.rem(me + count - 1, count)
    child = lax.rem(me, 8)
    row = me // 8
    rows = count // 8
    mates = [me - child + lax.rem(child + k, 8) for k in range(1, 8)]
    cousins = [lax.rem(row + k, rows) * 8 + child for k in range(1, rows)]

    def fetch(b):
        part = pl.ds(pl.multiple_of(STEP * width * b, 16), STEP * width)
        return pltpu.make_async_copy(table.at[part], held.at[part], table_sem.at[b])

    def fetch_start(b, carry):
        fetch(b).start()
        return carry

    blocks = width // STEP
    lax.fori_loop(0, blocks, fetch_start, 0)
    barrier = pltpu.get_barrier_semaphore()
    for other in [left, right] + mates + cousins:
        pl.semaphore_signal(barrier, inc=1, device_id=(other,), device_id_type=pl.DeviceIdType.MESH)
    pl.semaphore_wait(barrier, 2 + len(mates) + len(cousins))

    def push(src, dst, sem, device):
        copy = pltpu.make_async_remote_copy(
            src_ref=src, dst_ref=dst, send_sem=send.at[sem], recv_sem=recv.at[sem],
            device_id=(device,), device_id_type=pl.DeviceIdType.MESH,
        )
        copy.start()
        return copy

    halo = [
        push(pts, pts_lo, 0, right),
        push(pts, pts_hi, 1, left),
        push(dens, dens_lo, 2, right),
        push(dens, dens_hi, 3, left),
    ]

    lane = lax.broadcasted_iota(jnp.int32, (32, 128), 1).astype(F32)
    lane_big = lax.broadcasted_iota(jnp.int32, (128, 128), 1)

    def leaf_group(g, carry):
        tiles = []
        for i in range(4):
            tiles += source_tiles([pts[c, pl.ds(4 * g + i, 1), :] for c in range(3)])
        turned = jnp.concatenate(tiles, axis=0).astype(BF).T
        for i in range(4):
            j = 4 * g + i
            own = (lane_big >= 32 * i) & (lane_big < 32 * i + 32)
            f = jnp.where(own, turned, jnp.zeros_like(turned))
            w = jnp.concatenate(
                [
                    jnp.concatenate(
                        target_tiles([surf[3 * h + c, pl.ds(j, 1), :] for c in range(3)]), axis=0
                    ).astype(BF)
                    for h in range(2)
                ],
                axis=1,
            )
            k = jnp.exp2(jnp.dot(f, jnp.concatenate([w] * 4, axis=0), preferred_element_type=F32))
            hi, lo = split2(k)
            used = jnp.broadcast_to(pts[3, pl.ds(j, 1), :], (32, 128))
            mh, ml = split2(jnp.where(lane < used, dens[j], 0.0))
            r = jnp.dot(
                jnp.concatenate([mh, ml], axis=0), jnp.concatenate([hi, lo], axis=1), preferred_element_type=F32
            )
            c = 4 * lax.rem(g, 2) + i
            n = g // 2
            check[c, pl.ds(pl.multiple_of(32 * n, 32), 32), :] = (r[:32, :256] + r[:32, 256:]) + (
                r[32:, :256] + r[32:, 256:]
            )
        return carry

    lax.fori_loop(0, leaves // 4, leaf_group, 0)
    node[...] = jnp.zeros_like(node)
    far_sum[...] = jnp.zeros_like(far_sum)

    def merge(half, carry):
        parts = []
        for i in range(4):
            both = dot3(up_inv[...], shift_up[4 * half + i])
            parts.append(dot3(check[4 * half + i][:, :width], both))
        node[...] += (parts[0] + parts[1]) + (parts[2] + parts[3])
        return carry

    lax.fori_loop(0, 2, merge, 0)
    nodes[1, :, :width] = node[...].astype(BF)
    halo.append(push(nodes.at[1], nodes.at[0], 4, right))
    halo.append(push(nodes.at[1], nodes.at[2], 5, left))

    def climb(c, total):
        return total + dot3(node[pl.ds(pl.multiple_of(32 * c, 32), 32), :], shift_up[c])

    top = lax.fori_loop(0, 8, climb, jnp.zeros((q_width, width), F32))
    near_top[0, :, :width] = dot3(top, shift_up[child])
    copies = [push(near_top.at[0], near_top.at[k], 5 + k, mates[k - 1]) for k in range(1, 8)]

    def turn(slab):
        x = nodes[slab].astype(F32)
        for i in range(8):
            rows32 = x[32 * i : 32 * i + 32]
            turned = jnp.concatenate([rows32] * 4, axis=0).T
            sources[slab, :, i, :] = turned[:width]

    turn(1)
    for copy in halo[4:]:
        copy.wait_recv()
    turn(0)
    turn(2)

    def far_block(b, carry):
        fetch(b).wait()
        part = pl.ds(pl.multiple_of(STEP * width * b, 16), STEP * width)
        picked[...] = jnp.dot(held[part, :], sel[...], preferred_element_type=F32)
        far_step(far_sum, picked, lambda k: [sources[h, STEP * b + k] for h in range(3)], width)
        return carry

    lax.fori_loop(0, blocks // 3, far_block, 0)
    for copy in copies:
        copy.wait_recv()
    top1 = near_top[0, :, :width]
    for k in range(1, 8):
        top1 = top1 + near_top[k, :, :width]
    far_top[0, :, :width] = top1
    more = [push(far_top.at[0], far_top.at[k], 12 + k, cousins[k - 1]) for k in range(1, rows)]
    total = dot3(top1, coarse[child])
    lax.fori_loop(blocks // 3, 2 * blocks // 3, far_block, 0)
    for copy in more:
        copy.wait_recv()
    half = row // 8
    own = jnp.zeros((q_width, width), F32)
    other = jnp.zeros((q_width, width), F32)
    for k in range(8):
        src = lax.rem(row + rows - k, rows)
        pair = dot3(jnp.concatenate([far_top[k, :, :width], far_top[k + 8, :, :width]], axis=0), shift_up[lax.rem(src, 8)])
        same = jnp.where(src // 8 == half, 1.0, 0.0)
        a, b = pair[:q_width], pair[q_width:]
        own = own + (same * a + (1.0 - same) * b)
        other = other + ((1.0 - same) * a + same * b)
    top3 = dot3(own, shift_up[half]) + dot3(other, shift_up[1 - half])
    total = total + dot3(own, coarse[lax.rem(row, 8)]) + dot3(top3, coarse[half])
    lax.fori_loop(2 * blocks // 3, blocks, far_block, 0)
    node[...] = far_sum[...].T[:, :width]

    for c in range(8):
        at = slice(32 * c, 32 * c + 32)
        node[at, :] = node[at, :] + dot3(total, shift_down[c])
    leaf_sum[...] = jnp.zeros_like(leaf_sum)

    def descend(half, carry):
        tail = None
        for i in range(4):
            leaf_sum[i, :, :width] = dot3(node[...], dot3(shift_down[4 * half + i], down_inv[...]))
            last = leaf_sum[i, :, 128:]
            last = last if i == 0 else pltpu.roll(last, 32 * i, 1)
            tail = last if tail is None else tail + last
        for n in range(8):
            at = slice(32 * n, 32 * n + 32)
            for i in range(4):
                down[8 * n + 4 * half + i] = leaf_sum[i, at, :128]
            down_tail[2 * n + half] = tail[at]
        return carry

    lax.fori_loop(0, 2, descend, 0)
    for copy in halo[:4]:
        copy.wait_recv()
    for copy in halo + copies + more:
        copy.wait_send()


STEP = 8


def far_step(far_sum, picked, rows_at, width):
    lane = lax.broadcasted_iota(jnp.int32, (32, 128), 1)
    zero = jnp.zeros((32, 128), BF)
    owns = [(lane >= 32 * n) & (lane < 32 * n + 32) for n in range(4)]
    for half in range(2):
        cols = slice(128 * half, 128 * half + 128)
        total = None
        for k in range(0, STEP, 2):
            sums = []
            rows = []
            for e in (k, k + 1):
                s = picked[width * e : width * e + width, cols]
                hi = s.astype(BF).astype(F32)
                sums.append(jnp.concatenate([hi, s - hi], axis=0).astype(BF))
                x = jnp.concatenate(rows_at(e) + [jnp.zeros((8, 128), F32)], axis=0).astype(BF)
                rows += [jnp.where(own, x, zero) for own in owns]
            r = jnp.dot(
                jnp.concatenate(sums, axis=1), jnp.concatenate(rows, axis=0), preferred_element_type=F32
            )
            r = r[:width] + r[width:]
            total = r if total is None else total + r
        far_sum[:width, cols] += total


def up_call(pts, dens, surf, sel, up_inv, down_inv, shift_up, shift_down, coarse, table):
    leaves, q_width, _ = dens.shape
    width = up_inv.shape[0]
    vmem = pl.BlockSpec(memory_space=pltpu.VMEM)
    hbm = pl.BlockSpec(memory_space=pl.ANY)
    like = jax.ShapeDtypeStruct
    rows = 8 * q_width
    return pl.pallas_call(
        up_kernel,
        out_shape=[
            like(pts.shape, F32), like(pts.shape, F32), like(dens.shape, F32), like(dens.shape, F32),
            like((leaves, q_width, 128), F32), like((leaves // 4, q_width, 128), F32),
        ],
        in_specs=[vmem] * 9 + [hbm],
        out_specs=[hbm] * 4 + [vmem] * 2,
        scratch_shapes=[
            pltpu.VMEM((8, rows, 256), F32),
            pltpu.VMEM((rows, width), F32),
            pltpu.VMEM((3, rows, 256), BF),
            pltpu.VMEM((8, q_width, 256), F32),
            pltpu.VMEM((16, q_width, 256), F32),
            pltpu.VMEM(table.shape, BF),
            pltpu.VMEM((3, width, 8, 128), F32),
            pltpu.VMEM((256, rows), F32),
            pltpu.VMEM((STEP * width, 256), F32),
            pltpu.VMEM((4, rows, 256), F32),
            pltpu.SemaphoreType.DMA((28,)),
            pltpu.SemaphoreType.DMA((28,)),
            pltpu.SemaphoreType.DMA((width // STEP,)),
        ],
        compiler_params=pltpu.CompilerParams(
            vmem_limit_bytes=56 * 1024 * 1024, collective_id=0, has_side_effects=True
        ),
        name="upward",
    )(pts, dens, surf, sel, up_inv, down_inv, shift_up, shift_down, coarse, table)


def local(
    points,
    dens,
    surface,
    counts,
    ulist,
    vlist,
    up_inverse,
    down_inverse,
    shift_up,
    shift_down,
    coarse,
    translate,
):
    leaf_count, _, p_width = dens.shape
    eq_width = surface.shape[2]
    node_count = vlist.shape[0]
    index = lax.axis_index("oct")
    used = counts.astype(F32)
    turned_points = jnp.concatenate(
        [
            jnp.transpose(points, (1, 0, 2)),
            jnp.broadcast_to(used[None, :, None], (1, leaf_count, p_width)),
            jnp.broadcast_to(jnp.pad(used, (0, p_width - leaf_count))[None, None, :], (1, leaf_count, p_width)),
        ],
        axis=0,
    )
    turned_surface = jnp.transpose(surface, (1, 0, 2))
    surf_tail = jnp.pad(turned_surface[:, :, 128:], ((0, 0), (0, 0), (0, 160 - eq_width)))
    surf = jnp.concatenate(
        [turned_surface[:, :, :128], jnp.pad(surf_tail, ((0, 0), (0, 0), (0, 96)))], axis=0
    )
    surf_near = jnp.concatenate([turned_surface[:, :, :128], surf_tail.reshape(3, leaf_count // 4, 128)], axis=1)
    rel = jnp.where(vlist >= 0, vlist - (index - 1) * node_count, -1)
    sel = (rel.T[:, :, None] == jnp.arange(32)).astype(BF).reshape(rel.shape[1], 256)
    points_lo, points_hi, dens_lo, dens_hi, leaf_down, down_tail = up_call(
        turned_points, dens, surf, sel, up_inverse, down_inverse, shift_up, shift_down, coarse,
        jnp.transpose(translate, (1, 2, 0)).reshape(eq_width * eq_width, -1),
    )
    points3 = [points_lo, turned_points, points_hi]
    first = ((index - 1) * leaf_count).astype(jnp.int32).reshape(1)
    plan = plan_call(first, jnp.transpose(ulist), points3)
    return near_call(plan, points3, [dens_lo, dens, dens_hi], surf_near, leaf_down, down_tail)


def solution(mesh):
    placed = (
        P("oct", None, None),
        P("oct", None, None),
        P("oct", None, None),
        P("oct"),
        P("oct", None),
        P("oct", None),
        P(),
        P(),
        P(),
        P(),
        P(),
        P(),
    )
    return jax.shard_map(
        local, mesh=mesh, in_specs=placed, out_specs=P("oct", None, None), check_vma=False
    )
```

```python
import functools

import jax
import jax.numpy as jnp
from jax import lax
from jax.experimental import pallas as pl
from jax.experimental.pallas import tpu as pltpu
from jax.sharding import PartitionSpec as P

BF = jnp.bfloat16
F32 = jnp.float32


def split2(x):
    hi = x.astype(BF)
    lo = (x - hi.astype(F32)).astype(BF)
    return hi, lo


def split3(x):
    a = x.astype(BF).astype(F32)
    r = x - a
    b = r.astype(BF).astype(F32)
    return a, b, r - b


def rows8(shape):
    return lax.broadcasted_iota(jnp.int32, shape, 0)


LOG2E = 1.4426950408889634


def source_tiles(coords):
    out = []
    norm = None
    row = rows8((8, 128))
    for c in coords:
        x = jnp.broadcast_to(c, (8, 128))
        a, b, d = split3(LOG2E * x)
        first = (row <= 1) | (row == 4)
        out.append(jnp.where(first, a, jnp.where(row <= 3, b, jnp.where(row == 5, d, 0.0))))
        norm = x * x if norm is None else norm + x * x
    a, b, d = split3((-0.5 * LOG2E) * norm)
    out.append(
        jnp.where(row == 0, a, jnp.where(row == 1, b, jnp.where(row == 2, d, jnp.where(row <= 5, 1.0, 0.0))))
    )
    return out


def target_tiles(coords):
    out = []
    norm = None
    row = rows8((8, 128))
    for c in coords:
        x = jnp.broadcast_to(c, (8, 128))
        a, b, d = split3(x)
        first = (row == 0) | (row == 2) | (row == 5)
        second = (row == 1) | (row == 3)
        out.append(jnp.where(first, a, jnp.where(second, b, jnp.where(row == 4, d, 0.0))))
        norm = x * x if norm is None else norm + x * x
    a, b, d = split3((-0.5 * LOG2E) * norm)
    out.append(
        jnp.where(row <= 2, 1.0, jnp.where(row == 3, a, jnp.where(row == 4, b, jnp.where(row == 5, d, 0.0))))
    )
    return out


LIST_ROWS = 128
TABLE_ROWS = 2 * LIST_ROWS
LEAF_AT, PTR_AT, COUNT_AT, ROUNDS_AT = 0, 12, 26, 31
GROUP = 16


def plan_kernel(leaves, first, ulist, rows, out, ids):
    slots = ulist.shape[0]
    lane = lax.broadcasted_iota(jnp.int32, (32, 128), 1)
    ids[...] = jnp.full((32, 128), -1, jnp.int32)
    ids[:slots, :leaves] = ulist[...]
    rel = ids[...]
    rel = jnp.where(rel >= 0, rel - first[0], -1)
    counts = [rows[slab, :1, :] for slab in range(3)]
    nun = [jnp.right_shift(jnp.broadcast_to(c, (32, 128)) + 31, 5) for c in counts]
    low = jnp.where(lane < leaves, nun[0], pltpu.roll(nun[1], leaves, 1))
    from_low = jnp.take_along_axis(low, jnp.clip(rel, 0, 127), axis=1, mode="promise_in_bounds")
    from_high = jnp.take_along_axis(nun[2], jnp.clip(rel - 2 * leaves, 0, 127), axis=1, mode="promise_in_bounds")
    num = jnp.where(rel < 0, 0, jnp.where(rel < 2 * leaves, from_low, from_high))
    before = lax.broadcasted_iota(jnp.int32, (32, 32), 1) < lax.broadcasted_iota(jnp.int32, (32, 32), 0)
    start = 5 + jnp.dot(
        jnp.where(before, 1.0, 0.0).astype(BF), num.astype(F32).astype(BF), preferred_element_type=F32
    ).astype(jnp.int32)
    place = lax.broadcasted_iota(jnp.int32, (LIST_ROWS, 128), 0)
    mine = lax.broadcasted_iota(jnp.int32, (LIST_ROWS, 128), 1)
    unit = jnp.where(place < 4, 12 * leaves + 4 * mine + place, jnp.where(place == 4, 16 * leaves + mine, 17 * leaves))
    for s in range(slots):
        at = place - start[s : s + 1]
        inside = (at >= 0) & (at < num[s : s + 1])
        unit = jnp.where(inside, 4 * rel[s : s + 1] + at, unit)
    out[:LIST_ROWS, :] = unit
    out[LIST_ROWS:TABLE_ROWS, :] = jnp.bitwise_and(unit, -4) + jnp.bitwise_and(place - unit, 3)
    n = jnp.right_shift(start[31:] + num[31:] + 7, 3)
    n = jnp.where(lane[:1] < leaves, n, 0)
    column = jnp.broadcast_to(n.astype(F32), (128, 128)).T
    upto = lax.broadcasted_iota(jnp.int32, (128, 128), 1) <= lax.broadcasted_iota(jnp.int32, (128, 128), 0)
    end = jnp.dot(jnp.where(upto, 1.0, 0.0).astype(BF), column.astype(BF), preferred_element_type=F32)
    begin = (end - column).astype(jnp.int32)
    end = end.astype(jnp.int32)
    total = end[127:]
    out[TABLE_ROWS:, :] = jnp.zeros((32, 128), jnp.int32)
    for r in range(9):
        chunk = 128 * r + mine
        inside = (chunk >= begin) & (chunk < end)
        leaf = jnp.sum(jnp.where(inside, place, 0), axis=0, keepdims=True)
        ptr = jnp.sum(jnp.where(inside, (chunk - begin) * 1024 + place, 0), axis=0, keepdims=True)
        ptr = jnp.where(chunk[:1] < total, ptr, 120 * 128)
        out[TABLE_ROWS + LEAF_AT + r : TABLE_ROWS + LEAF_AT + r + 1, :] = leaf
        out[TABLE_ROWS + PTR_AT + r : TABLE_ROWS + PTR_AT + r + 1, :] = ptr
    for slab in range(3):
        out[TABLE_ROWS + COUNT_AT + slab : TABLE_ROWS + COUNT_AT + slab + 1, :] = counts[slab]
    out[TABLE_ROWS + ROUNDS_AT :, :] = jnp.right_shift(total + GROUP - 1, 4)


def plan_call(first, ulist, rows):
    leaves = ulist.shape[1]
    vmem = pl.BlockSpec(memory_space=pltpu.VMEM)
    return pl.pallas_call(
        functools.partial(plan_kernel, leaves),
        out_shape=jax.ShapeDtypeStruct((TABLE_ROWS + 32, 128), jnp.int32),
        in_specs=[pl.BlockSpec(memory_space=pltpu.SMEM), vmem, vmem],
        out_specs=vmem,
        scratch_shapes=[pltpu.VMEM((32, 128), jnp.int32)],
        name="plan",
    )(first, ulist, rows).reshape(-1)


def near_kernel(leaves, plan, p0, p1, p2, d0, d1, d2, surf, down, down_tail, out, f_s, m_s, w_s, e_s, acc):
    lane = lax.broadcasted_iota(jnp.int32, (32, 128), 1)
    maps = 128 * TABLE_ROWS

    def used(slab, j):
        return plan[maps + 128 * (COUNT_AT + slab) + j]

    lane_big = lax.broadcasted_iota(jnp.int32, (128, 128), 1)
    row_big = lax.broadcasted_iota(jnp.int32, (128, 128), 0)
    zero_unit = 4 * (3 * leaves + leaves + leaves // 4)
    shifts = jnp.concatenate(
        [jnp.where(lane_big == (row_big + 32 * k) % 128, 1.0, 0.0).astype(BF) for k in range(1, 4)], axis=1
    )

    def put_features(coords4, base):
        tiles = []
        for coords in coords4:
            tiles += source_tiles(coords)
        tile = jnp.concatenate(tiles, axis=0).astype(BF)
        turned = tile.T
        for i in range(4):
            own = (lane_big >= 32 * i) & (lane_big < 32 * i + 32)
            f_s[pl.ds(base + 4 * i, 4)] = jnp.where(own, turned, jnp.zeros_like(turned)).reshape(4, 32, 128)

    def put_density(tiles, base):
        parts = []
        for i, tile in enumerate(tiles):
            hi, lo = split2(tile)
            parts.append(jnp.concatenate([hi, lo], axis=0))
            m_s[base + 4 * i] = parts[i]
        moved = jnp.dot(jnp.concatenate(parts, axis=0), shifts, preferred_element_type=F32).astype(BF)
        for i in range(4):
            for k in range(1, 4):
                m_s[base + 4 * i + k] = moved[64 * i : 64 * i + 64, 128 * (k - 1) : 128 * k]

    for slab, (p, d) in enumerate(((p0, d0), (p1, d1), (p2, d2))):

        def prep(g, carry, slab=slab, p=p, d=d):
            for half in range(4):
                first = 16 * g + 4 * half
                coords4 = [[p[c, pl.ds(first + i, 1), :] for c in range(3)] for i in range(4)]
                put_features(coords4, 4 * (slab * leaves + first))
                masked = [
                    jnp.where(lane < used(slab, first + i), d[first + i], 0.0) for i in range(4)
                ]
                put_density(masked, 4 * (slab * leaves + first))
            return carry

        lax.fori_loop(0, leaves // 16, prep, 0)

    def prep_surface(count, row0, view):
        def body(g, carry):
            for half in range(4):
                first = 16 * g + 4 * half
                coords4 = [[surf[c, pl.ds(row0 + first + i, 1), :] for c in range(3)] for i in range(4)]
                put_features(coords4, 4 * (3 * leaves + row0 + first))
                put_density([view(first + i) for i in range(4)], 4 * (3 * leaves + row0 + first))
            return carry

        lax.fori_loop(0, count // 16, body, 0)

    prep_surface(leaves, 0, lambda j: down[j])
    prep_surface(leaves // 4, leaves, lambda j: down_tail[j])
    f_s[pl.ds(zero_unit, 4)] = jnp.zeros((4, 32, 128), BF)
    m_s[pl.ds(zero_unit, 4)] = jnp.zeros((4, 64, 128), BF)

    def prep_target(g, carry):
        for i in range(4):
            j = 4 * g + i
            tile = jnp.concatenate(target_tiles([p1[c, pl.ds(j, 1), :] for c in range(3)]), axis=0).astype(BF)
            w_s[j] = jnp.concatenate([tile] * 4, axis=0)
            acc[j] = jnp.zeros((64, 256), F32)
        return carry

    lax.fori_loop(0, leaves // 4, prep_target, 0)

    lane64 = lax.broadcasted_iota(jnp.int32, (64, 128), 1)

    def exponents(i, slot):
        base, l = plan[maps + 128 * PTR_AT + i], plan[maps + 128 * LEAF_AT + i]
        left = jnp.concatenate([f_s[plan[base + 128 * v]] for v in range(4)], axis=0)
        right = jnp.concatenate([f_s[plan[base + 128 * (4 + v)]] for v in range(4)], axis=0)
        w = w_s[l]
        e_s[slot, 0] = jnp.dot(left, w, preferred_element_type=F32)
        e_s[slot, 1] = jnp.dot(right, w, preferred_element_type=F32)

    def weights(base):
        t = [m_s[plan[base + 128 * v]] for v in range(4)]
        return jnp.where(
            lane64 < 64, jnp.where(lane64 < 32, t[0], t[1]), jnp.where(lane64 < 96, t[2], t[3])
        )

    def apply(i, slot):
        base, l = plan[maps + 128 * PTR_AT + i], plan[maps + 128 * LEAF_AT + i]
        m = jnp.concatenate([weights(base + 128 * LIST_ROWS), weights(base + 128 * (LIST_ROWS + 4))], axis=1)
        k = jnp.exp2(e_s[slot].reshape(256, 128))
        hi, lo = split2(k)
        acc[l] += jnp.dot(m, jnp.concatenate([hi, lo], axis=1), preferred_element_type=F32)

    half = 8
    for u in range(half):
        exponents(u, u)

    def body(i, carry):
        at = 2 * half * i
        for u in range(half):
            exponents(at + half + u, half + u)
            apply(at + u, u)
        for u in range(half):
            exponents(at + 2 * half + u, u)
            apply(at + half + u, half + u)
        return carry

    lax.fori_loop(0, plan[maps + 128 * ROUNDS_AT], body, 0)

    def finish(g, carry):
        for i in range(4):
            j = 4 * g + i
            a = acc[j]
            v = (a[:32, :128] + a[:32, 128:]) + (a[32:, :128] + a[32:, 128:])
            out[j] = jnp.where(lane < used(1, j), v, 0.0)
        return carry

    lax.fori_loop(0, leaves // 4, finish, 0)


def near_call(plan, pts, dens, surf, down, down_tail):
    leaves = dens[0].shape[0]
    units = 4 * (3 * leaves + leaves + leaves // 4) + 4
    smem = pl.BlockSpec(memory_space=pltpu.SMEM)
    vmem = pl.BlockSpec(memory_space=pltpu.VMEM)
    return pl.pallas_call(
        functools.partial(near_kernel, leaves),
        out_shape=jax.ShapeDtypeStruct(dens[0].shape, F32),
        in_specs=[smem] + [vmem] * 9,
        out_specs=vmem,
        scratch_shapes=[
            pltpu.VMEM((units, 32, 128), BF),
            pltpu.VMEM((units, 64, 128), BF),
            pltpu.VMEM((leaves, 128, 128), BF),
            pltpu.VMEM((16, 2, 128, 128), F32),
            pltpu.VMEM((leaves, 64, 256), F32),
        ],
        compiler_params=pltpu.CompilerParams(vmem_limit_bytes=60 * 1024 * 1024),
        name="near",
    )(plan, *pts, *dens, surf, down, down_tail)


def dot3(a, b):
    ah, al = split2(a)
    bh, bl = split2(b)
    left = jnp.concatenate([ah, al], axis=0)
    r = jnp.dot(left, bh, preferred_element_type=F32)
    m = a.shape[0]
    return r[:m] + (r[m:] + jnp.dot(ah, bl, preferred_element_type=F32))


def up_kernel(
    counts, pts, dens, surf, count_row, vlist, up_inv, down_inv, shift_up, shift_down, coarse, table,
    pts_lo, pts_hi, dens_lo, dens_hi, count_rows, surf_near, down, down_tail,
    check, node, nodes, near_top, far_top, held, sources, far_sum, leaf_sum, surf_pad, sel_turned, picker, send, recv, table_sem,
):
    leaves, q_width = dens.shape[0], dens.shape[1]
    width = up_inv.shape[0]
    count = lax.axis_size("oct")
    me = lax.axis_index("oct")
    right = lax.rem(me + 1, count)
    left = lax.rem(me + count - 1, count)
    child = lax.rem(me, 8)
    row = me // 8
    rows = count // 8
    mates = [me - child + lax.rem(child + k, 8) for k in range(1, 8)]
    cousins = [lax.rem(row + k, rows) * 8 + child for k in range(1, rows)]

    def fetch(b):
        part = pl.ds(pl.multiple_of(STEP * b, STEP), STEP)
        return pltpu.make_async_copy(table.at[part], held.at[part], table_sem.at[b])

    def fetch_start(b, carry):
        fetch(b).start()
        return carry

    blocks = width // STEP
    lax.fori_loop(0, blocks, fetch_start, 0)
    barrier = pltpu.get_barrier_semaphore()
    for other in [left, right] + mates + cousins:
        pl.semaphore_signal(barrier, inc=1, device_id=(other,), device_id_type=pl.DeviceIdType.MESH)
    pl.semaphore_wait(barrier, 2 + len(mates) + len(cousins))

    def push(src, dst, sem, device):
        copy = pltpu.make_async_remote_copy(
            src_ref=src, dst_ref=dst, send_sem=send.at[sem], recv_sem=recv.at[sem],
            device_id=(device,), device_id_type=pl.DeviceIdType.MESH,
        )
        copy.start()
        return copy

    count_rows[1] = jnp.zeros((8, 128), jnp.int32)
    count_rows[1, :1, :leaves] = count_row[...]
    halo = [
        push(count_rows.at[1], count_rows.at[0], 28, right),
        push(count_rows.at[1], count_rows.at[2], 29, left),
        push(pts, pts_lo, 0, right),
        push(pts, pts_hi, 1, left),
        push(dens, dens_lo, 2, right),
        push(dens, dens_hi, 3, left),
    ]

    surf_pad[...] = jnp.zeros_like(surf_pad)
    surf_pad[:, :, : width - 128] = surf[:, :, 128:]
    surf_near[:, :leaves, :] = surf[:, :, :128]
    for c in range(3):
        packed = None
        for i in range(4):
            last = surf_pad[c, pl.ds(i, leaves // 4, stride=4), :]
            last = last if i == 0 else pltpu.roll(last, 32 * i, 1)
            packed = last if packed is None else packed + last
        surf_near[c, leaves:, :] = packed
    rel = vlist[...]
    rel = jnp.where(rel >= 0, rel - (me - 1) * 8, -1)
    types = rel.shape[1]
    sel_turned[...] = jnp.zeros_like(sel_turned)
    for n in range(8):
        same = jnp.broadcast_to(rel[n : n + 1], (32, types)) == rows8((32, types))
        sel_turned[32 * n : 32 * n + 32, :types] = jnp.where(same, 1.0, 0.0)
    picker[...] = sel_turned[...].T[:types].astype(BF)
    lane = lax.broadcasted_iota(jnp.int32, (32, 128), 1)
    lane_big = lax.broadcasted_iota(jnp.int32, (128, 128), 1)

    def leaf_group(g, carry):
        at = pl.ds(pl.multiple_of(8 * g, 8), 8)
        points8 = [pts[c, at, :] for c in range(3)]
        main8 = [surf_near[c, at, :] for c in range(3)]
        tail8 = [surf_pad[c, at, :] for c in range(3)]
        for half in range(2):
            tiles = []
            for i in range(4):
                r = 4 * half + i
                tiles += source_tiles([x[r : r + 1] for x in points8])
            turned = jnp.concatenate(tiles, axis=0).astype(BF).T
            for i in range(4):
                r = 4 * half + i
                own = (lane_big >= 32 * i) & (lane_big < 32 * i + 32)
                f = jnp.where(own, turned, jnp.zeros_like(turned))
                w = jnp.concatenate(
                    [
                        jnp.concatenate(target_tiles([x[r : r + 1] for x in part]), axis=0).astype(BF)
                        for part in (main8, tail8)
                    ],
                    axis=1,
                )
                k = jnp.exp2(jnp.dot(f, jnp.concatenate([w] * 4, axis=0), preferred_element_type=F32))
                hi, lo = split2(k)
                mh, ml = split2(jnp.where(lane < counts[8 * g + r], dens[8 * g + r], 0.0))
                p = jnp.dot(
                    jnp.concatenate([mh, ml], axis=0),
                    jnp.concatenate([hi, lo], axis=1),
                    preferred_element_type=F32,
                )
                check[r, pl.ds(pl.multiple_of(32 * g, 32), 32), :] = (p[:32, :256] + p[:32, 256:]) + (
                    p[32:, :256] + p[32:, 256:]
                )
        return carry

    lax.fori_loop(0, leaves // 8, leaf_group, 0)
    node[...] = jnp.zeros_like(node)
    far_sum[...] = jnp.zeros_like(far_sum)

    def merge(half, carry):
        parts = []
        for i in range(4):
            both = dot3(up_inv[...], shift_up[4 * half + i])
            parts.append(dot3(check[4 * half + i][:, :width], both))
        node[...] += (parts[0] + parts[1]) + (parts[2] + parts[3])
        return carry

    lax.fori_loop(0, 2, merge, 0)
    nodes[1, :, :width] = node[...].astype(BF)
    halo.append(push(nodes.at[1], nodes.at[0], 4, right))
    halo.append(push(nodes.at[1], nodes.at[2], 5, left))

    def climb(c, total):
        return total + dot3(node[pl.ds(pl.multiple_of(32 * c, 32), 32), :], shift_up[c])

    top = lax.fori_loop(0, 8, climb, jnp.zeros((q_width, width), F32))
    near_top[0, :, :width] = dot3(top, shift_up[child])
    copies = [push(near_top.at[0], near_top.at[k], 5 + k, mates[k - 1]) for k in range(1, 8)]

    def turn(slab):
        x = nodes[slab].astype(F32)
        for i in range(8):
            rows32 = x[32 * i : 32 * i + 32]
            turned = jnp.concatenate([rows32] * 4, axis=0).T
            sources[slab, :, i, :] = turned[:width]

    turn(1)
    for copy in halo[6:]:
        copy.wait_recv()
    turn(0)
    turn(2)
    picks = picker[...]

    def far_block(b, carry):
        fetch(b).wait()
        far_sum[:width, :] += far_step(lambda k: held[STEP * b + k], picks, lambda k: [sources[h, STEP * b + k] for h in range(3)], width)
        return carry

    lax.fori_loop(0, blocks // 3, far_block, 0)
    for copy in copies:
        copy.wait_recv()
    top1 = near_top[0, :, :width]
    for k in range(1, 8):
        top1 = top1 + near_top[k, :, :width]
    far_top[0, :, :width] = top1
    more = [push(far_top.at[0], far_top.at[k], 12 + k, cousins[k - 1]) for k in range(1, rows)]
    total = dot3(top1, coarse[child])
    lax.fori_loop(blocks // 3, 2 * blocks // 3, far_block, 0)
    for copy in more:
        copy.wait_recv()
    half = row // 8
    own = jnp.zeros((q_width, width), F32)
    other = jnp.zeros((q_width, width), F32)
    for k in range(8):
        src = lax.rem(row + rows - k, rows)
        pair = dot3(jnp.concatenate([far_top[k, :, :width], far_top[k + 8, :, :width]], axis=0), shift_up[lax.rem(src, 8)])
        same = jnp.where(src // 8 == half, 1.0, 0.0)
        a, b = pair[:q_width], pair[q_width:]
        own = own + (same * a + (1.0 - same) * b)
        other = other + ((1.0 - same) * a + same * b)
    top3 = dot3(own, shift_up[half]) + dot3(other, shift_up[1 - half])
    total = total + dot3(own, coarse[lax.rem(row, 8)]) + dot3(top3, coarse[half])
    lax.fori_loop(2 * blocks // 3, blocks, far_block, 0)
    node[...] = far_sum[...].T[:, :width]

    for c in range(8):
        at = slice(32 * c, 32 * c + 32)
        node[at, :] = node[at, :] + dot3(total, shift_down[c])
    leaf_sum[...] = jnp.zeros_like(leaf_sum)

    def descend(half, carry):
        tail = None
        for i in range(4):
            leaf_sum[i, :, :width] = dot3(node[...], dot3(shift_down[4 * half + i], down_inv[...]))
            last = leaf_sum[i, :, 128:]
            last = last if i == 0 else pltpu.roll(last, 32 * i, 1)
            tail = last if tail is None else tail + last
        for n in range(8):
            at = slice(32 * n, 32 * n + 32)
            for i in range(4):
                down[8 * n + 4 * half + i] = leaf_sum[i, at, :128]
            down_tail[2 * n + half] = tail[at]
        return carry

    lax.fori_loop(0, 2, descend, 0)
    for copy in halo[:6]:
        copy.wait_recv()
    for copy in halo + copies + more:
        copy.wait_send()


STEP = 8


def far_step(table_at, picks, rows_at, width):
    lane = lax.broadcasted_iota(jnp.int32, (32, 128), 1)
    zero = jnp.zeros((32, 128), BF)
    total = None
    for k in range(0, STEP, 2):
        sums = []
        rows = []
        for e in (k, k + 1):
            s = jnp.dot(table_at(e), picks, preferred_element_type=F32)
            hi, lo = split2(s)
            sums.append(jnp.concatenate([hi, lo], axis=0))
            x = jnp.concatenate(rows_at(e) + [jnp.zeros((8, 128), F32)], axis=0).astype(BF)
            for n in range(8):
                own = (lane >= 32 * (n % 4)) & (lane < 32 * (n % 4) + 32)
                part = jnp.where(own, x, zero)
                rows.append(jnp.concatenate([part, zero] if n < 4 else [zero, part], axis=1))
        r = jnp.dot(
            jnp.concatenate(sums, axis=1), jnp.concatenate(rows, axis=0), preferred_element_type=F32
        )
        r = r[:width] + r[width:]
        total = r if total is None else total + r
    return total


def up_call(counts, pts, dens, surf, count_row, vlist, up_inv, down_inv, shift_up, shift_down, coarse, table):
    leaves, q_width, _ = dens.shape
    width = up_inv.shape[0]
    vmem = pl.BlockSpec(memory_space=pltpu.VMEM)
    hbm = pl.BlockSpec(memory_space=pl.ANY)
    like = jax.ShapeDtypeStruct
    rows = 8 * q_width
    return pl.pallas_call(
        up_kernel,
        out_shape=[
            like(pts.shape, F32), like(pts.shape, F32), like(dens.shape, F32), like(dens.shape, F32),
            like((3, 8, 128), jnp.int32), like((3, leaves + leaves // 4, 128), F32),
            like((leaves, q_width, 128), F32), like((leaves // 4, q_width, 128), F32),
        ],
        in_specs=[pl.BlockSpec(memory_space=pltpu.SMEM)] + [vmem] * 10 + [hbm],
        out_specs=[hbm] * 4 + [vmem] * 4,
        scratch_shapes=[
            pltpu.VMEM((8, rows, 256), F32),
            pltpu.VMEM((rows, width), F32),
            pltpu.VMEM((3, rows, 256), BF),
            pltpu.VMEM((8, q_width, 256), F32),
            pltpu.VMEM((16, q_width, 256), F32),
            pltpu.VMEM(table.shape, BF),
            pltpu.VMEM((3, width, 8, 128), F32),
            pltpu.VMEM((256, rows), F32),
            pltpu.VMEM((4, rows, 256), F32),
            pltpu.VMEM((3, leaves, 128), F32),
            pltpu.VMEM((256, 384), F32),
            pltpu.VMEM((vlist.shape[1], 256), BF),
            pltpu.SemaphoreType.DMA((30,)),
            pltpu.SemaphoreType.DMA((30,)),
            pltpu.SemaphoreType.DMA((width // STEP,)),
        ],
        compiler_params=pltpu.CompilerParams(
            vmem_limit_bytes=56 * 1024 * 1024, collective_id=0, has_side_effects=True
        ),
        name="upward",
    )(counts, pts, dens, surf, count_row, vlist, up_inv, down_inv, shift_up, shift_down, coarse, table)


def local(
    points,
    dens,
    surface,
    counts,
    ulist,
    vlist,
    up_inverse,
    down_inverse,
    shift_up,
    shift_down,
    coarse,
    translate,
):
    leaf_count = dens.shape[0]
    index = lax.axis_index("oct")
    turned_points = jnp.transpose(points, (1, 0, 2))
    points_lo, points_hi, dens_lo, dens_hi, count_rows, surf_near, leaf_down, down_tail = up_call(
        counts, turned_points, dens, jnp.transpose(surface, (1, 0, 2)), counts.reshape(1, leaf_count), vlist,
        up_inverse, down_inverse, shift_up, shift_down, coarse, jnp.transpose(translate, (1, 2, 0)),
    )
    points3 = [points_lo, turned_points, points_hi]
    first = ((index - 1) * leaf_count).astype(jnp.int32).reshape(1)
    plan = plan_call(first, jnp.transpose(ulist), count_rows)
    return near_call(plan, points3, [dens_lo, dens, dens_hi], surf_near, leaf_down, down_tail)


def solution(mesh):
    placed = (
        P("oct", None, None),
        P("oct", None, None),
        P("oct", None, None),
        P("oct"),
        P("oct", None),
        P("oct", None),
        P(),
        P(),
        P(),
        P(),
        P(),
        P(),
    )
    return jax.shard_map(
        local, mesh=mesh, in_specs=placed, out_specs=P("oct", None, None), check_vma=False
    )
```

```python
import functools

import jax
import jax.numpy as jnp
from jax import lax
from jax.experimental import pallas as pl
from jax.experimental.pallas import tpu as pltpu
from jax.sharding import PartitionSpec as P

BF = jnp.bfloat16
F32 = jnp.float32


def split2(x):
    hi = x.astype(BF)
    lo = (x - hi.astype(F32)).astype(BF)
    return hi, lo


def split3(x):
    a = x.astype(BF).astype(F32)
    r = x - a
    b = r.astype(BF).astype(F32)
    return a, b, r - b


def rows8(shape):
    return lax.broadcasted_iota(jnp.int32, shape, 0)


LOG2E = 1.4426950408889634


def source_tiles(coords):
    out = []
    norm = None
    row = rows8((8, 128))
    for c in coords:
        x = jnp.broadcast_to(c, (8, 128))
        a, b, d = split3(LOG2E * x)
        first = (row <= 1) | (row == 4)
        out.append(jnp.where(first, a, jnp.where(row <= 3, b, jnp.where(row == 5, d, 0.0))))
        norm = x * x if norm is None else norm + x * x
    a, b, d = split3((-0.5 * LOG2E) * norm)
    out.append(
        jnp.where(row == 0, a, jnp.where(row == 1, b, jnp.where(row == 2, d, jnp.where(row <= 5, 1.0, 0.0))))
    )
    return out


def target_tiles(coords):
    out = []
    norm = None
    row = rows8((8, 128))
    for c in coords:
        x = jnp.broadcast_to(c, (8, 128))
        a, b, d = split3(x)
        first = (row == 0) | (row == 2) | (row == 5)
        second = (row == 1) | (row == 3)
        out.append(jnp.where(first, a, jnp.where(second, b, jnp.where(row == 4, d, 0.0))))
        norm = x * x if norm is None else norm + x * x
    a, b, d = split3((-0.5 * LOG2E) * norm)
    out.append(
        jnp.where(row <= 2, 1.0, jnp.where(row == 3, a, jnp.where(row == 4, b, jnp.where(row == 5, d, 0.0))))
    )
    return out


LIST_ROWS = 128
TABLE_ROWS = 2 * LIST_ROWS
LEAF_AT, PTR_AT, COUNT_AT, ROUNDS_AT = 0, 12, 26, 31
GROUP = 32


def plan_kernel(leaves, first, ulist, rows, out, ids):
    slots = ulist.shape[0]
    lane = lax.broadcasted_iota(jnp.int32, (32, 128), 1)
    ids[...] = jnp.full((32, 128), -1, jnp.int32)
    ids[:slots, :leaves] = ulist[...]
    rel = ids[...]
    rel = jnp.where(rel >= 0, rel - first[0], -1)
    counts = [rows[slab, :1, :] for slab in range(3)]
    nun = [jnp.right_shift(jnp.broadcast_to(c, (32, 128)) + 31, 5) for c in counts]
    low = jnp.where(lane < leaves, nun[0], pltpu.roll(nun[1], leaves, 1))
    from_low = jnp.take_along_axis(low, jnp.clip(rel, 0, 127), axis=1, mode="promise_in_bounds")
    from_high = jnp.take_along_axis(nun[2], jnp.clip(rel - 2 * leaves, 0, 127), axis=1, mode="promise_in_bounds")
    num = jnp.where(rel < 0, 0, jnp.where(rel < 2 * leaves, from_low, from_high))
    before = lax.broadcasted_iota(jnp.int32, (32, 32), 1) < lax.broadcasted_iota(jnp.int32, (32, 32), 0)
    start = 5 + jnp.dot(
        jnp.where(before, 1.0, 0.0).astype(BF), num.astype(F32).astype(BF), preferred_element_type=F32
    ).astype(jnp.int32)
    place = lax.broadcasted_iota(jnp.int32, (LIST_ROWS, 128), 0)
    mine = lax.broadcasted_iota(jnp.int32, (LIST_ROWS, 128), 1)
    unit = jnp.where(place < 4, 12 * leaves + 4 * mine + place, jnp.where(place == 4, 16 * leaves + mine, 17 * leaves))
    for s in range(slots):
        at = place - start[s : s + 1]
        inside = (at >= 0) & (at < num[s : s + 1])
        unit = jnp.where(inside, 4 * rel[s : s + 1] + at, unit)
    out[:LIST_ROWS, :] = unit
    out[LIST_ROWS:TABLE_ROWS, :] = jnp.bitwise_and(unit, -4) + jnp.bitwise_and(place - unit, 3)
    n = jnp.right_shift(start[31:] + num[31:] + 7, 3)
    n = jnp.where(lane[:1] < leaves, n, 0)
    column = jnp.broadcast_to(n.astype(F32), (128, 128)).T
    upto = lax.broadcasted_iota(jnp.int32, (128, 128), 1) <= lax.broadcasted_iota(jnp.int32, (128, 128), 0)
    end = jnp.dot(jnp.where(upto, 1.0, 0.0).astype(BF), column.astype(BF), preferred_element_type=F32)
    begin = (end - column).astype(jnp.int32)
    end = end.astype(jnp.int32)
    total = end[127:]
    out[TABLE_ROWS:, :] = jnp.zeros((32, 128), jnp.int32)
    for r in range(9):
        chunk = 128 * r + mine
        inside = (chunk >= begin) & (chunk < end)
        leaf = jnp.sum(jnp.where(inside, place, 0), axis=0, keepdims=True)
        ptr = jnp.sum(jnp.where(inside, (chunk - begin) * 1024 + place, 0), axis=0, keepdims=True)
        ptr = jnp.where(chunk[:1] < total, ptr, 120 * 128)
        out[TABLE_ROWS + LEAF_AT + r : TABLE_ROWS + LEAF_AT + r + 1, :] = leaf
        out[TABLE_ROWS + PTR_AT + r : TABLE_ROWS + PTR_AT + r + 1, :] = ptr
    for slab in range(3):
        out[TABLE_ROWS + COUNT_AT + slab : TABLE_ROWS + COUNT_AT + slab + 1, :] = counts[slab]
    out[TABLE_ROWS + ROUNDS_AT :, :] = jnp.right_shift(total + GROUP - 1, 5)


def plan_call(first, ulist, rows):
    leaves = ulist.shape[1]
    vmem = pl.BlockSpec(memory_space=pltpu.VMEM)
    return pl.pallas_call(
        functools.partial(plan_kernel, leaves),
        out_shape=jax.ShapeDtypeStruct((TABLE_ROWS + 32, 128), jnp.int32),
        in_specs=[pl.BlockSpec(memory_space=pltpu.SMEM), vmem, vmem],
        out_specs=vmem,
        scratch_shapes=[pltpu.VMEM((32, 128), jnp.int32)],
        name="plan",
    )(first, ulist, rows).reshape(-1)


def near_kernel(leaves, plan, p0, p1, p2, d0, d1, d2, surf, down, down_tail, out, f_s, m_s, w_s, e_s, acc):
    lane = lax.broadcasted_iota(jnp.int32, (32, 128), 1)
    maps = 128 * TABLE_ROWS

    def used(slab, j):
        return plan[maps + 128 * (COUNT_AT + slab) + j]

    lane_big = lax.broadcasted_iota(jnp.int32, (128, 128), 1)
    row_big = lax.broadcasted_iota(jnp.int32, (128, 128), 0)
    zero_unit = 4 * (3 * leaves + leaves + leaves // 4)
    shifts = jnp.concatenate(
        [jnp.where(lane_big == (row_big + 32 * k) % 128, 1.0, 0.0).astype(BF) for k in range(1, 4)], axis=1
    )

    def put_features(coords4, base):
        tiles = []
        for coords in coords4:
            tiles += source_tiles(coords)
        tile = jnp.concatenate(tiles, axis=0).astype(BF)
        turned = tile.T
        for i in range(4):
            own = (lane_big >= 32 * i) & (lane_big < 32 * i + 32)
            f_s[pl.ds(base + 4 * i, 4)] = jnp.where(own, turned, jnp.zeros_like(turned)).reshape(4, 32, 128)

    def put_density(tiles, base):
        parts = []
        for i, tile in enumerate(tiles):
            hi, lo = split2(tile)
            parts.append(jnp.concatenate([hi, lo], axis=0))
            m_s[base + 4 * i] = parts[i]
        moved = jnp.dot(jnp.concatenate(parts, axis=0), shifts, preferred_element_type=F32).astype(BF)
        for i in range(4):
            for k in range(1, 4):
                m_s[base + 4 * i + k] = moved[64 * i : 64 * i + 64, 128 * (k - 1) : 128 * k]

    for slab, (p, d) in enumerate(((p0, d0), (p1, d1), (p2, d2))):

        def prep(g, carry, slab=slab, p=p, d=d):
            for half in range(4):
                first = 16 * g + 4 * half
                coords4 = [[p[c, pl.ds(first + i, 1), :] for c in range(3)] for i in range(4)]
                put_features(coords4, 4 * (slab * leaves + first))
                masked = [
                    jnp.where(lane < used(slab, first + i), d[first + i], 0.0) for i in range(4)
                ]
                put_density(masked, 4 * (slab * leaves + first))
            return carry

        lax.fori_loop(0, leaves // 16, prep, 0)

    def prep_surface(count, row0, view):
        def body(g, carry):
            for half in range(4):
                first = 16 * g + 4 * half
                coords4 = [[surf[c, pl.ds(row0 + first + i, 1), :] for c in range(3)] for i in range(4)]
                put_features(coords4, 4 * (3 * leaves + row0 + first))
                put_density([view(first + i) for i in range(4)], 4 * (3 * leaves + row0 + first))
            return carry

        lax.fori_loop(0, count // 16, body, 0)

    prep_surface(leaves, 0, lambda j: down[j])
    prep_surface(leaves // 4, leaves, lambda j: down_tail[j])
    f_s[pl.ds(zero_unit, 4)] = jnp.zeros((4, 32, 128), BF)
    m_s[pl.ds(zero_unit, 4)] = jnp.zeros((4, 64, 128), BF)

    def prep_target(g, carry):
        for i in range(4):
            j = 4 * g + i
            tile = jnp.concatenate(target_tiles([p1[c, pl.ds(j, 1), :] for c in range(3)]), axis=0).astype(BF)
            w_s[j] = jnp.concatenate([tile] * 4, axis=0)
            acc[j] = jnp.zeros((64, 256), F32)
        return carry

    lax.fori_loop(0, leaves // 4, prep_target, 0)

    lane64 = lax.broadcasted_iota(jnp.int32, (64, 128), 1)

    def exponents(i, slot):
        base, l = plan[maps + 128 * PTR_AT + i], plan[maps + 128 * LEAF_AT + i]
        left = jnp.concatenate([f_s[plan[base + 128 * v]] for v in range(4)], axis=0)
        right = jnp.concatenate([f_s[plan[base + 128 * (4 + v)]] for v in range(4)], axis=0)
        w = w_s[l]
        e_s[slot, 0] = jnp.dot(left, w, preferred_element_type=F32)
        e_s[slot, 1] = jnp.dot(right, w, preferred_element_type=F32)

    def weights(base):
        t = [m_s[plan[base + 128 * v]] for v in range(4)]
        return jnp.where(
            lane64 < 64, jnp.where(lane64 < 32, t[0], t[1]), jnp.where(lane64 < 96, t[2], t[3])
        )

    def apply(i, slot):
        base, l = plan[maps + 128 * PTR_AT + i], plan[maps + 128 * LEAF_AT + i]
        m = jnp.concatenate([weights(base + 128 * LIST_ROWS), weights(base + 128 * (LIST_ROWS + 4))], axis=1)
        k = jnp.exp2(e_s[slot].reshape(256, 128))
        hi, lo = split2(k)
        acc[l] += jnp.dot(m, jnp.concatenate([hi, lo], axis=1), preferred_element_type=F32)

    half = 16
    for u in range(half):
        exponents(u, u)

    def body(i, carry):
        at = 2 * half * i
        for u in range(half):
            exponents(at + half + u, half + u)
            apply(at + u, u)
        for u in range(half):
            exponents(at + 2 * half + u, u)
            apply(at + half + u, half + u)
        return carry

    lax.fori_loop(0, plan[maps + 128 * ROUNDS_AT], body, 0)

    def finish(g, carry):
        for i in range(4):
            j = 4 * g + i
            a = acc[j]
            v = (a[:32, :128] + a[:32, 128:]) + (a[32:, :128] + a[32:, 128:])
            out[j] = jnp.where(lane < used(1, j), v, 0.0)
        return carry

    lax.fori_loop(0, leaves // 4, finish, 0)


def near_call(plan, pts, dens, surf, down, down_tail):
    leaves = dens[0].shape[0]
    units = 4 * (3 * leaves + leaves + leaves // 4) + 4
    smem = pl.BlockSpec(memory_space=pltpu.SMEM)
    vmem = pl.BlockSpec(memory_space=pltpu.VMEM)
    return pl.pallas_call(
        functools.partial(near_kernel, leaves),
        out_shape=jax.ShapeDtypeStruct(dens[0].shape, F32),
        in_specs=[smem] + [vmem] * 9,
        out_specs=vmem,
        scratch_shapes=[
            pltpu.VMEM((units, 32, 128), BF),
            pltpu.VMEM((units, 64, 128), BF),
            pltpu.VMEM((leaves, 128, 128), BF),
            pltpu.VMEM((32, 2, 128, 128), F32),
            pltpu.VMEM((leaves, 64, 256), F32),
        ],
        compiler_params=pltpu.CompilerParams(vmem_limit_bytes=60 * 1024 * 1024),
        name="near",
    )(plan, *pts, *dens, surf, down, down_tail)


def dot3(a, b):
    ah, al = split2(a)
    bh, bl = split2(b)
    left = jnp.concatenate([ah, al], axis=0)
    r = jnp.dot(left, bh, preferred_element_type=F32)
    m = a.shape[0]
    return r[:m] + (r[m:] + jnp.dot(ah, bl, preferred_element_type=F32))


def up_kernel(
    counts, pts, dens, surf, count_row, vlist, up_inv, down_inv, shift_up, shift_down, coarse, table,
    pts_lo, pts_hi, dens_lo, dens_hi, count_rows, surf_near, down, down_tail,
    check, node, nodes, near_top, far_top, held, sources, far_sum, leaf_sum, surf_pad, sel_turned, picker, send, recv, table_sem,
):
    leaves, q_width = dens.shape[0], dens.shape[1]
    width = up_inv.shape[0]
    count = lax.axis_size("oct")
    me = lax.axis_index("oct")
    right = lax.rem(me + 1, count)
    left = lax.rem(me + count - 1, count)
    child = lax.rem(me, 8)
    row = me // 8
    rows = count // 8
    mates = [me - child + lax.rem(child + k, 8) for k in range(1, 8)]
    cousins = [lax.rem(row + k, rows) * 8 + child for k in range(1, rows)]

    def fetch(b):
        part = pl.ds(pl.multiple_of(STEP * b, STEP), STEP)
        return pltpu.make_async_copy(table.at[part], held.at[part], table_sem.at[b])

    def fetch_start(b, carry):
        fetch(b).start()
        return carry

    blocks = width // STEP
    lax.fori_loop(0, blocks, fetch_start, 0)
    barrier = pltpu.get_barrier_semaphore()
    for other in [left, right] + mates + cousins:
        pl.semaphore_signal(barrier, inc=1, device_id=(other,), device_id_type=pl.DeviceIdType.MESH)
    pl.semaphore_wait(barrier, 2 + len(mates) + len(cousins))

    def push(src, dst, sem, device):
        copy = pltpu.make_async_remote_copy(
            src_ref=src, dst_ref=dst, send_sem=send.at[sem], recv_sem=recv.at[sem],
            device_id=(device,), device_id_type=pl.DeviceIdType.MESH,
        )
        copy.start()
        return copy

    count_rows[1] = jnp.zeros((8, 128), jnp.int32)
    count_rows[1, :1, :leaves] = count_row[...]
    halo = [
        push(count_rows.at[1], count_rows.at[0], 28, right),
        push(count_rows.at[1], count_rows.at[2], 29, left),
        push(pts, pts_lo, 0, right),
        push(pts, pts_hi, 1, left),
    ]

    surf_pad[...] = jnp.zeros_like(surf_pad)
    surf_pad[:, :, : width - 128] = surf[:, :, 128:]
    surf_near[:, :leaves, :] = surf[:, :, :128]
    for c in range(3):
        packed = None
        for i in range(4):
            last = surf_pad[c, pl.ds(i, leaves // 4, stride=4), :]
            last = last if i == 0 else pltpu.roll(last, 32 * i, 1)
            packed = last if packed is None else packed + last
        surf_near[c, leaves:, :] = packed
    rel = vlist[...]
    rel = jnp.where(rel >= 0, rel - (me - 1) * 8, -1)
    types = rel.shape[1]
    sel_turned[...] = jnp.zeros_like(sel_turned)
    for n in range(8):
        same = jnp.broadcast_to(rel[n : n + 1], (32, types)) == rows8((32, types))
        sel_turned[32 * n : 32 * n + 32, :types] = jnp.where(same, 1.0, 0.0)
    picker[...] = sel_turned[...].T[:types].astype(BF)
    lane = lax.broadcasted_iota(jnp.int32, (32, 128), 1)
    lane_big = lax.broadcasted_iota(jnp.int32, (128, 128), 1)

    def leaf_group(g, carry):
        at = pl.ds(pl.multiple_of(8 * g, 8), 8)
        points8 = [pts[c, at, :] for c in range(3)]
        main8 = [surf_near[c, at, :] for c in range(3)]
        tail8 = [surf_pad[c, at, :] for c in range(3)]
        for half in range(2):
            tiles = []
            for i in range(4):
                r = 4 * half + i
                tiles += source_tiles([x[r : r + 1] for x in points8])
            turned = jnp.concatenate(tiles, axis=0).astype(BF).T
            for i in range(4):
                r = 4 * half + i
                own = (lane_big >= 32 * i) & (lane_big < 32 * i + 32)
                f = jnp.where(own, turned, jnp.zeros_like(turned))
                w = jnp.concatenate(
                    [
                        jnp.concatenate(target_tiles([x[r : r + 1] for x in part]), axis=0).astype(BF)
                        for part in (main8, tail8)
                    ],
                    axis=1,
                )
                k = jnp.exp2(jnp.dot(f, jnp.concatenate([w] * 4, axis=0), preferred_element_type=F32))
                hi, lo = split2(k)
                mh, ml = split2(jnp.where(lane < counts[8 * g + r], dens[8 * g + r], 0.0))
                p = jnp.dot(
                    jnp.concatenate([mh, ml], axis=0),
                    jnp.concatenate([hi, lo], axis=1),
                    preferred_element_type=F32,
                )
                check[r, pl.ds(pl.multiple_of(32 * g, 32), 32), :] = (p[:32, :256] + p[:32, 256:]) + (
                    p[32:, :256] + p[32:, 256:]
                )
        return carry

    lax.fori_loop(0, leaves // 8, leaf_group, 0)
    node[...] = jnp.zeros_like(node)
    far_sum[...] = jnp.zeros_like(far_sum)

    def merge(half, carry):
        parts = []
        for i in range(4):
            both = dot3(up_inv[...], shift_up[4 * half + i])
            parts.append(dot3(check[4 * half + i][:, :width], both))
        node[...] += (parts[0] + parts[1]) + (parts[2] + parts[3])
        return carry

    lax.fori_loop(0, 2, merge, 0)
    nodes[1, :, :width] = node[...].astype(BF)
    halo.append(push(nodes.at[1], nodes.at[0], 4, right))
    halo.append(push(nodes.at[1], nodes.at[2], 5, left))

    def climb(c, total):
        return total + dot3(node[pl.ds(pl.multiple_of(32 * c, 32), 32), :], shift_up[c])

    top = lax.fori_loop(0, 8, climb, jnp.zeros((q_width, width), F32))
    near_top[0, :, :width] = dot3(top, shift_up[child])
    copies = [push(near_top.at[0], near_top.at[k], 5 + k, mates[k - 1]) for k in range(1, 8)]
    late = [push(dens, dens_lo, 2, right), push(dens, dens_hi, 3, left)]

    def turn(slab):
        x = nodes[slab].astype(F32)
        for i in range(8):
            rows32 = x[32 * i : 32 * i + 32]
            turned = jnp.concatenate([rows32] * 4, axis=0).T
            sources[slab, :, i, :] = turned[:width]

    turn(1)
    for copy in halo[4:]:
        copy.wait_recv()
    turn(0)
    turn(2)
    picks = picker[...]

    def far_block(b, carry):
        fetch(b).wait()
        far_sum[:width, :] += far_step(lambda k: held[STEP * b + k], picks, lambda k: [sources[h, STEP * b + k] for h in range(3)], width)
        return carry

    lax.fori_loop(0, blocks // 3 + 1, far_block, 0)
    for copy in copies:
        copy.wait_recv()
    top1 = near_top[0, :, :width]
    for k in range(1, 8):
        top1 = top1 + near_top[k, :, :width]
    far_top[0, :, :width] = top1
    more = [push(far_top.at[0], far_top.at[k], 12 + k, cousins[k - 1]) for k in range(1, rows)]
    total = dot3(top1, coarse[child])
    lax.fori_loop(blocks // 3 + 1, blocks - 3, far_block, 0)
    for copy in more:
        copy.wait_recv()
    half = row // 8
    own = jnp.zeros((q_width, width), F32)
    other = jnp.zeros((q_width, width), F32)
    for k in range(8):
        src = lax.rem(row + rows - k, rows)
        pair = dot3(jnp.concatenate([far_top[k, :, :width], far_top[k + 8, :, :width]], axis=0), shift_up[lax.rem(src, 8)])
        same = jnp.where(src // 8 == half, 1.0, 0.0)
        a, b = pair[:q_width], pair[q_width:]
        own = own + (same * a + (1.0 - same) * b)
        other = other + ((1.0 - same) * a + same * b)
    top3 = dot3(own, shift_up[half]) + dot3(other, shift_up[1 - half])
    total = total + dot3(own, coarse[lax.rem(row, 8)]) + dot3(top3, coarse[half])
    lax.fori_loop(blocks - 3, blocks, far_block, 0)
    node[...] = far_sum[...].T[:, :width]

    for c in range(8):
        at = slice(32 * c, 32 * c + 32)
        node[at, :] = node[at, :] + dot3(total, shift_down[c])
    leaf_sum[...] = jnp.zeros_like(leaf_sum)

    def descend(half, carry):
        tail = None
        for i in range(4):
            leaf_sum[i, :, :width] = dot3(node[...], dot3(shift_down[4 * half + i], down_inv[...]))
            last = leaf_sum[i, :, 128:]
            last = last if i == 0 else pltpu.roll(last, 32 * i, 1)
            tail = last if tail is None else tail + last
        for n in range(8):
            at = slice(32 * n, 32 * n + 32)
            for i in range(4):
                down[8 * n + 4 * half + i] = leaf_sum[i, at, :128]
            down_tail[2 * n + half] = tail[at]
        return carry

    lax.fori_loop(0, 2, descend, 0)
    for copy in halo[:4] + late:
        copy.wait_recv()
    for copy in halo + late + copies + more:
        copy.wait_send()


STEP = 8


def far_step(table_at, picks, rows_at, width):
    lane = lax.broadcasted_iota(jnp.int32, (32, 128), 1)
    zero = jnp.zeros((32, 128), BF)
    total = None
    for k in range(0, STEP, 2):
        sums = []
        rows = []
        for e in (k, k + 1):
            s = jnp.dot(table_at(e), picks, preferred_element_type=F32)
            hi, lo = split2(s)
            sums.append(jnp.concatenate([hi, lo], axis=0))
            x = jnp.concatenate(rows_at(e) + [jnp.zeros((8, 128), F32)], axis=0).astype(BF)
            for n in range(8):
                own = (lane >= 32 * (n % 4)) & (lane < 32 * (n % 4) + 32)
                part = jnp.where(own, x, zero)
                rows.append(jnp.concatenate([part, zero] if n < 4 else [zero, part], axis=1))
        r = jnp.dot(
            jnp.concatenate(sums, axis=1), jnp.concatenate(rows, axis=0), preferred_element_type=F32
        )
        r = r[:width] + r[width:]
        total = r if total is None else total + r
    return total


def up_call(counts, pts, dens, surf, count_row, vlist, up_inv, down_inv, shift_up, shift_down, coarse, table):
    leaves, q_width, _ = dens.shape
    width = up_inv.shape[0]
    vmem = pl.BlockSpec(memory_space=pltpu.VMEM)
    hbm = pl.BlockSpec(memory_space=pl.ANY)
    like = jax.ShapeDtypeStruct
    rows = 8 * q_width
    return pl.pallas_call(
        up_kernel,
        out_shape=[
            like(pts.shape, F32), like(pts.shape, F32), like(dens.shape, F32), like(dens.shape, F32),
            like((3, 8, 128), jnp.int32), like((3, leaves + leaves // 4, 128), F32),
            like((leaves, q_width, 128), F32), like((leaves // 4, q_width, 128), F32),
        ],
        in_specs=[pl.BlockSpec(memory_space=pltpu.SMEM)] + [vmem] * 10 + [hbm],
        out_specs=[hbm] * 4 + [vmem] * 4,
        scratch_shapes=[
            pltpu.VMEM((8, rows, 256), F32),
            pltpu.VMEM((rows, width), F32),
            pltpu.VMEM((3, rows, 256), BF),
            pltpu.VMEM((8, q_width, 256), F32),
            pltpu.VMEM((16, q_width, 256), F32),
            pltpu.VMEM(table.shape, BF),
            pltpu.VMEM((3, width, 8, 128), F32),
            pltpu.VMEM((256, rows), F32),
            pltpu.VMEM((4, rows, 256), F32),
            pltpu.VMEM((3, leaves, 128), F32),
            pltpu.VMEM((256, 384), F32),
            pltpu.VMEM((vlist.shape[1], 256), BF),
            pltpu.SemaphoreType.DMA((30,)),
            pltpu.SemaphoreType.DMA((30,)),
            pltpu.SemaphoreType.DMA((width // STEP,)),
        ],
        compiler_params=pltpu.CompilerParams(
            vmem_limit_bytes=56 * 1024 * 1024, collective_id=0, has_side_effects=True
        ),
        name="upward",
    )(counts, pts, dens, surf, count_row, vlist, up_inv, down_inv, shift_up, shift_down, coarse, table)


def local(
    points,
    dens,
    surface,
    counts,
    ulist,
    vlist,
    up_inverse,
    down_inverse,
    shift_up,
    shift_down,
    coarse,
    translate,
):
    leaf_count = dens.shape[0]
    index = lax.axis_index("oct")
    turned_points = jnp.transpose(points, (1, 0, 2))
    points_lo, points_hi, dens_lo, dens_hi, count_rows, surf_near, leaf_down, down_tail = up_call(
        counts, turned_points, dens, jnp.transpose(surface, (1, 0, 2)), counts.reshape(1, leaf_count), vlist,
        up_inverse, down_inverse, shift_up, shift_down, coarse, jnp.transpose(translate, (1, 2, 0)),
    )
    points3 = [points_lo, turned_points, points_hi]
    first = ((index - 1) * leaf_count).astype(jnp.int32).reshape(1)
    plan = plan_call(first, jnp.transpose(ulist), count_rows)
    return near_call(plan, points3, [dens_lo, dens, dens_hi], surf_near, leaf_down, down_tail)


def solution(mesh):
    placed = (
        P("oct", None, None),
        P("oct", None, None),
        P("oct", None, None),
        P("oct"),
        P("oct", None),
        P("oct", None),
        P(),
        P(),
        P(),
        P(),
        P(),
        P(),
    )
    return jax.shard_map(
        local, mesh=mesh, in_specs=placed, out_specs=P("oct", None, None), check_vma=False
    )
```

```python
import functools

import jax
import jax.numpy as jnp
from jax import lax
from jax.experimental import pallas as pl
from jax.experimental.pallas import tpu as pltpu
from jax.sharding import PartitionSpec as P

BF = jnp.bfloat16
F32 = jnp.float32


def split2(x):
    hi = x.astype(BF)
    lo = (x - hi.astype(F32)).astype(BF)
    return hi, lo


def split3(x):
    a = x.astype(BF).astype(F32)
    r = x - a
    b = r.astype(BF).astype(F32)
    return a, b, r - b


def rows8(shape):
    return lax.broadcasted_iota(jnp.int32, shape, 0)


LOG2E = 1.4426950408889634


def source_tiles(coords):
    out = []
    norm = None
    row = rows8((8, 128))
    for c in coords:
        x = jnp.broadcast_to(c, (8, 128))
        a, b, d = split3(LOG2E * x)
        first = (row <= 1) | (row == 4)
        out.append(jnp.where(first, a, jnp.where(row <= 3, b, jnp.where(row == 5, d, 0.0))))
        norm = x * x if norm is None else norm + x * x
    a, b, d = split3((-0.5 * LOG2E) * norm)
    out.append(
        jnp.where(row == 0, a, jnp.where(row == 1, b, jnp.where(row == 2, d, jnp.where(row <= 5, 1.0, 0.0))))
    )
    return out


def target_tiles(coords):
    out = []
    norm = None
    row = rows8((8, 128))
    for c in coords:
        x = jnp.broadcast_to(c, (8, 128))
        a, b, d = split3(x)
        first = (row == 0) | (row == 2) | (row == 5)
        second = (row == 1) | (row == 3)
        out.append(jnp.where(first, a, jnp.where(second, b, jnp.where(row == 4, d, 0.0))))
        norm = x * x if norm is None else norm + x * x
    a, b, d = split3((-0.5 * LOG2E) * norm)
    out.append(
        jnp.where(row <= 2, 1.0, jnp.where(row == 3, a, jnp.where(row == 4, b, jnp.where(row == 5, d, 0.0))))
    )
    return out


LIST_ROWS = 128
TABLE_ROWS = 2 * LIST_ROWS
LEAF_AT, PTR_AT, COUNT_AT, ROUNDS_AT = 0, 12, 26, 31
GROUP = 32


def plan_kernel(leaves, first, ulist, rows, out, ids):
    slots = ulist.shape[0]
    lane = lax.broadcasted_iota(jnp.int32, (32, 128), 1)
    ids[...] = jnp.full((32, 128), -1, jnp.int32)
    ids[:slots, :leaves] = ulist[...]
    rel = ids[...]
    rel = jnp.where(rel >= 0, rel - first[0], -1)
    counts = [rows[slab, :1, :] for slab in range(3)]
    nun = [jnp.right_shift(jnp.broadcast_to(c, (32, 128)) + 31, 5) for c in counts]
    low = jnp.where(lane < leaves, nun[0], pltpu.roll(nun[1], leaves, 1))
    from_low = jnp.take_along_axis(low, jnp.clip(rel, 0, 127), axis=1, mode="promise_in_bounds")
    from_high = jnp.take_along_axis(nun[2], jnp.clip(rel - 2 * leaves, 0, 127), axis=1, mode="promise_in_bounds")
    num = jnp.where(rel < 0, 0, jnp.where(rel < 2 * leaves, from_low, from_high))
    before = lax.broadcasted_iota(jnp.int32, (32, 32), 1) < lax.broadcasted_iota(jnp.int32, (32, 32), 0)
    start = 5 + jnp.dot(
        jnp.where(before, 1.0, 0.0).astype(BF), num.astype(F32).astype(BF), preferred_element_type=F32
    ).astype(jnp.int32)
    place = lax.broadcasted_iota(jnp.int32, (LIST_ROWS, 128), 0)
    mine = lax.broadcasted_iota(jnp.int32, (LIST_ROWS, 128), 1)
    unit = jnp.where(place < 4, 12 * leaves + 4 * mine + place, jnp.where(place == 4, 16 * leaves + mine, 17 * leaves))
    for s in range(slots):
        at = place - start[s : s + 1]
        inside = (at >= 0) & (at < num[s : s + 1])
        unit = jnp.where(inside, 4 * rel[s : s + 1] + at, unit)
    out[:LIST_ROWS, :] = unit
    out[LIST_ROWS:TABLE_ROWS, :] = jnp.bitwise_and(unit, -4) + jnp.bitwise_and(place - unit, 3)
    n = jnp.right_shift(start[31:] + num[31:] + 7, 3)
    n = jnp.where(lane[:1] < leaves, n, 0)
    column = jnp.broadcast_to(n.astype(F32), (128, 128)).T
    upto = lax.broadcasted_iota(jnp.int32, (128, 128), 1) <= lax.broadcasted_iota(jnp.int32, (128, 128), 0)
    end = jnp.dot(jnp.where(upto, 1.0, 0.0).astype(BF), column.astype(BF), preferred_element_type=F32)
    begin = (end - column).astype(jnp.int32)
    end = end.astype(jnp.int32)
    total = end[127:]
    out[TABLE_ROWS:, :] = jnp.zeros((32, 128), jnp.int32)
    for r in range(9):
        chunk = 128 * r + mine
        inside = (chunk >= begin) & (chunk < end)
        leaf = jnp.sum(jnp.where(inside, place, 0), axis=0, keepdims=True)
        ptr = jnp.sum(jnp.where(inside, (chunk - begin) * 1024 + place, 0), axis=0, keepdims=True)
        ptr = jnp.where(chunk[:1] < total, ptr, 120 * 128)
        out[TABLE_ROWS + LEAF_AT + r : TABLE_ROWS + LEAF_AT + r + 1, :] = leaf
        out[TABLE_ROWS + PTR_AT + r : TABLE_ROWS + PTR_AT + r + 1, :] = ptr
    for slab in range(3):
        out[TABLE_ROWS + COUNT_AT + slab : TABLE_ROWS + COUNT_AT + slab + 1, :] = counts[slab]
    out[TABLE_ROWS + ROUNDS_AT :, :] = jnp.right_shift(total + GROUP - 1, 5)


def plan_call(first, ulist, rows):
    leaves = ulist.shape[1]
    vmem = pl.BlockSpec(memory_space=pltpu.VMEM)
    return pl.pallas_call(
        functools.partial(plan_kernel, leaves),
        out_shape=jax.ShapeDtypeStruct((TABLE_ROWS + 32, 128), jnp.int32),
        in_specs=[pl.BlockSpec(memory_space=pltpu.SMEM), vmem, vmem],
        out_specs=vmem,
        scratch_shapes=[pltpu.VMEM((32, 128), jnp.int32)],
        name="plan",
    )(first, ulist, rows).reshape(-1)


def near_kernel(leaves, plan, p0, p1, p2, d0, d1, d2, surf, down, down_tail, out, f_s, m_s, w_s, e_s, acc):
    lane = lax.broadcasted_iota(jnp.int32, (32, 128), 1)
    maps = 128 * TABLE_ROWS

    def used(slab, j):
        return plan[maps + 128 * (COUNT_AT + slab) + j]

    lane_big = lax.broadcasted_iota(jnp.int32, (128, 128), 1)
    row_big = lax.broadcasted_iota(jnp.int32, (128, 128), 0)
    zero_unit = 4 * (3 * leaves + leaves + leaves // 4)
    shifts = jnp.concatenate(
        [jnp.where(lane_big == (row_big + 32 * k) % 128, 1.0, 0.0).astype(BF) for k in range(1, 4)], axis=1
    )

    def put_features(coords4, base):
        tiles = []
        for coords in coords4:
            tiles += source_tiles(coords)
        tile = jnp.concatenate(tiles, axis=0).astype(BF)
        turned = tile.T
        for i in range(4):
            own = (lane_big >= 32 * i) & (lane_big < 32 * i + 32)
            f_s[pl.ds(base + 4 * i, 4)] = jnp.where(own, turned, jnp.zeros_like(turned)).reshape(4, 32, 128)

    def put_density(tiles, base):
        parts = []
        for i, tile in enumerate(tiles):
            hi, lo = split2(tile)
            parts.append(jnp.concatenate([hi, lo], axis=0))
            m_s[base + 4 * i] = parts[i]
        moved = jnp.dot(jnp.concatenate(parts, axis=0), shifts, preferred_element_type=F32).astype(BF)
        for i in range(4):
            for k in range(1, 4):
                m_s[base + 4 * i + k] = moved[64 * i : 64 * i + 64, 128 * (k - 1) : 128 * k]

    for slab, (p, d) in enumerate(((p0, d0), (p1, d1), (p2, d2))):

        def prep(g, carry, slab=slab, p=p, d=d):
            for half in range(4):
                first = 16 * g + 4 * half
                coords4 = [[p[c, pl.ds(first + i, 1), :] for c in range(3)] for i in range(4)]
                put_features(coords4, 4 * (slab * leaves + first))
                masked = [
                    jnp.where(lane < used(slab, first + i), d[first + i], 0.0) for i in range(4)
                ]
                put_density(masked, 4 * (slab * leaves + first))
            return carry

        lax.fori_loop(0, leaves // 16, prep, 0)

    def prep_surface(count, row0, view):
        def body(g, carry):
            for half in range(4):
                first = 16 * g + 4 * half
                coords4 = [[surf[c, pl.ds(row0 + first + i, 1), :] for c in range(3)] for i in range(4)]
                put_features(coords4, 4 * (3 * leaves + row0 + first))
                put_density([view(first + i) for i in range(4)], 4 * (3 * leaves + row0 + first))
            return carry

        lax.fori_loop(0, count // 16, body, 0)

    prep_surface(leaves, 0, lambda j: down[j])
    prep_surface(leaves // 4, leaves, lambda j: down_tail[j])
    f_s[pl.ds(zero_unit, 4)] = jnp.zeros((4, 32, 128), BF)
    m_s[pl.ds(zero_unit, 4)] = jnp.zeros((4, 64, 128), BF)

    def prep_target(g, carry):
        for i in range(4):
            j = 4 * g + i
            tile = jnp.concatenate(target_tiles([p1[c, pl.ds(j, 1), :] for c in range(3)]), axis=0).astype(BF)
            w_s[j] = jnp.concatenate([tile] * 4, axis=0)
            acc[j] = jnp.zeros((64, 256), F32)
        return carry

    lax.fori_loop(0, leaves // 4, prep_target, 0)

    lane64 = lax.broadcasted_iota(jnp.int32, (64, 128), 1)

    def exponents(i, slot):
        base, l = plan[maps + 128 * PTR_AT + i], plan[maps + 128 * LEAF_AT + i]
        left = jnp.concatenate([f_s[plan[base + 128 * v]] for v in range(4)], axis=0)
        right = jnp.concatenate([f_s[plan[base + 128 * (4 + v)]] for v in range(4)], axis=0)
        w = w_s[l]
        e_s[slot, 0] = jnp.dot(left, w, preferred_element_type=F32)
        e_s[slot, 1] = jnp.dot(right, w, preferred_element_type=F32)

    def weights(base):
        t = [m_s[plan[base + 128 * v]] for v in range(4)]
        return jnp.where(
            lane64 < 64, jnp.where(lane64 < 32, t[0], t[1]), jnp.where(lane64 < 96, t[2], t[3])
        )

    def apply(i, slot):
        base, l = plan[maps + 128 * PTR_AT + i], plan[maps + 128 * LEAF_AT + i]
        m = jnp.concatenate([weights(base + 128 * LIST_ROWS), weights(base + 128 * (LIST_ROWS + 4))], axis=1)
        k = jnp.exp2(e_s[slot].reshape(256, 128))
        hi, lo = split2(k)
        acc[l] += jnp.dot(m, jnp.concatenate([hi, lo], axis=1), preferred_element_type=F32)

    half = 16
    for u in range(half):
        exponents(u, u)

    def body(i, carry):
        at = 2 * half * i
        for u in range(half):
            exponents(at + half + u, half + u)
            apply(at + u, u)
        for u in range(half):
            exponents(at + 2 * half + u, u)
            apply(at + half + u, half + u)
        return carry

    lax.fori_loop(0, plan[maps + 128 * ROUNDS_AT], body, 0)

    def finish(g, carry):
        for i in range(4):
            j = 4 * g + i
            a = acc[j]
            v = (a[:32, :128] + a[:32, 128:]) + (a[32:, :128] + a[32:, 128:])
            out[j] = jnp.where(lane < used(1, j), v, 0.0)
        return carry

    lax.fori_loop(0, leaves // 4, finish, 0)


def near_call(plan, pts, dens, surf, down, down_tail):
    leaves = dens[0].shape[0]
    units = 4 * (3 * leaves + leaves + leaves // 4) + 4
    smem = pl.BlockSpec(memory_space=pltpu.SMEM)
    vmem = pl.BlockSpec(memory_space=pltpu.VMEM)
    return pl.pallas_call(
        functools.partial(near_kernel, leaves),
        out_shape=jax.ShapeDtypeStruct(dens[0].shape, F32),
        in_specs=[smem] + [vmem] * 9,
        out_specs=vmem,
        scratch_shapes=[
            pltpu.VMEM((units, 32, 128), BF),
            pltpu.VMEM((units, 64, 128), BF),
            pltpu.VMEM((leaves, 128, 128), BF),
            pltpu.VMEM((32, 2, 128, 128), F32),
            pltpu.VMEM((leaves, 64, 256), F32),
        ],
        compiler_params=pltpu.CompilerParams(vmem_limit_bytes=60 * 1024 * 1024),
        name="near",
    )(plan, *pts, *dens, surf, down, down_tail)


def dot3(a, b):
    ah, al = split2(a)
    bh, bl = split2(b)
    left = jnp.concatenate([ah, al], axis=0)
    r = jnp.dot(left, bh, preferred_element_type=F32)
    m = a.shape[0]
    return r[:m] + (r[m:] + jnp.dot(ah, bl, preferred_element_type=F32))


def up_kernel(
    counts, pts, dens, surf, count_row, vlist, up_inv, down_inv, shift_up, shift_down, coarse, table,
    pts_lo, pts_hi, dens_lo, dens_hi, count_rows, surf_near, down, down_tail,
    check, node, nodes, near_top, far_top, held, sources, far_sum, leaf_sum, surf_pad, sel_turned, picker, send, recv, table_sem,
):
    leaves, q_width = dens.shape[0], dens.shape[1]
    width = up_inv.shape[0]
    count = lax.axis_size("oct")
    me = lax.axis_index("oct")
    right = lax.rem(me + 1, count)
    left = lax.rem(me + count - 1, count)
    child = lax.rem(me, 8)
    row = me // 8
    rows = count // 8
    mates = [me - child + lax.rem(child + k, 8) for k in range(1, 8)]
    cousins = [lax.rem(row + k, rows) * 8 + child for k in range(1, rows)]

    def fetch(b):
        part = pl.ds(pl.multiple_of(STEP * b, STEP), STEP)
        return pltpu.make_async_copy(table.at[part], held.at[part], table_sem.at[b])

    def fetch_start(b, carry):
        fetch(b).start()
        return carry

    blocks = width // STEP
    lax.fori_loop(0, blocks, fetch_start, 0)
    barrier = pltpu.get_barrier_semaphore()
    for other in [left, right] + mates + cousins:
        pl.semaphore_signal(barrier, inc=1, device_id=(other,), device_id_type=pl.DeviceIdType.MESH)
    pl.semaphore_wait(barrier, 2 + len(mates) + len(cousins))

    def push(src, dst, sem, device):
        copy = pltpu.make_async_remote_copy(
            src_ref=src, dst_ref=dst, send_sem=send.at[sem], recv_sem=recv.at[sem],
            device_id=(device,), device_id_type=pl.DeviceIdType.MESH,
        )
        copy.start()
        return copy

    count_rows[1] = jnp.zeros((8, 128), jnp.int32)
    count_rows[1, :1, :leaves] = count_row[...]
    halo = [
        push(count_rows.at[1], count_rows.at[0], 28, right),
        push(count_rows.at[1], count_rows.at[2], 29, left),
        push(pts, pts_lo, 0, right),
        push(pts, pts_hi, 1, left),
    ]

    surf_pad[...] = jnp.zeros_like(surf_pad)
    surf_pad[:, :, : width - 128] = surf[:, :, 128:]
    surf_near[:, :leaves, :] = surf[:, :, :128]
    for c in range(3):
        packed = None
        for i in range(4):
            last = surf_pad[c, pl.ds(i, leaves // 4, stride=4), :]
            last = last if i == 0 else pltpu.roll(last, 32 * i, 1)
            packed = last if packed is None else packed + last
        surf_near[c, leaves:, :] = packed
    rel = vlist[...]
    rel = jnp.where(rel >= 0, rel - (me - 1) * 8, -1)
    types = rel.shape[1]
    sel_turned[...] = jnp.zeros_like(sel_turned)
    for n in range(8):
        same = jnp.broadcast_to(rel[n : n + 1], (32, types)) == rows8((32, types))
        sel_turned[32 * n : 32 * n + 32, :types] = jnp.where(same, 1.0, 0.0)
    picker[...] = sel_turned[...].T[:types].astype(BF)
    lane = lax.broadcasted_iota(jnp.int32, (32, 128), 1)
    lane_big = lax.broadcasted_iota(jnp.int32, (128, 128), 1)

    def leaf_node(g):
        at = pl.ds(pl.multiple_of(8 * g, 8), 8)
        points8 = [pts[c, at, :] for c in range(3)]
        main8 = [surf_near[c, at, :] for c in range(3)]
        tail8 = [surf_pad[c, at, :] for c in range(3)]
        for half in range(2):
            tiles = []
            for i in range(4):
                r = 4 * half + i
                tiles += source_tiles([x[r : r + 1] for x in points8])
            turned = jnp.concatenate(tiles, axis=0).astype(BF).T
            for i in range(4):
                r = 4 * half + i
                own = (lane_big >= 32 * i) & (lane_big < 32 * i + 32)
                f = jnp.where(own, turned, jnp.zeros_like(turned))
                w = jnp.concatenate(
                    [
                        jnp.concatenate(target_tiles([x[r : r + 1] for x in part]), axis=0).astype(BF)
                        for part in (main8, tail8)
                    ],
                    axis=1,
                )
                k = jnp.exp2(jnp.dot(f, jnp.concatenate([w] * 4, axis=0), preferred_element_type=F32))
                hi, lo = split2(k)
                mh, ml = split2(jnp.where(lane < counts[8 * g + r], dens[8 * g + r], 0.0))
                p = jnp.dot(
                    jnp.concatenate([mh, ml], axis=0),
                    jnp.concatenate([hi, lo], axis=1),
                    preferred_element_type=F32,
                )
                check[r, pl.ds(pl.multiple_of(32 * g, 32), 32), :] = (p[:32, :256] + p[:32, 256:]) + (
                    p[32:, :256] + p[32:, 256:]
                )

    def leaf_group(g, carry):
        leaf_node(2 * g)
        leaf_node(2 * g + 1)
        return carry

    lax.fori_loop(0, leaves // 16, leaf_group, 0)
    node[...] = jnp.zeros_like(node)
    far_sum[...] = jnp.zeros_like(far_sum)

    def merge(half, carry):
        parts = []
        for i in range(4):
            both = dot3(up_inv[...], shift_up[4 * half + i])
            parts.append(dot3(check[4 * half + i][:, :width], both))
        node[...] += (parts[0] + parts[1]) + (parts[2] + parts[3])
        return carry

    lax.fori_loop(0, 2, merge, 0)
    nodes[1, :, :width] = node[...].astype(BF)
    halo.append(push(nodes.at[1], nodes.at[0], 4, right))
    halo.append(push(nodes.at[1], nodes.at[2], 5, left))

    def climb(c, total):
        return total + dot3(node[pl.ds(pl.multiple_of(32 * c, 32), 32), :], shift_up[c])

    top = lax.fori_loop(0, 8, climb, jnp.zeros((q_width, width), F32))
    near_top[0, :, :width] = dot3(top, shift_up[child])
    copies = [push(near_top.at[0], near_top.at[k], 5 + k, mates[k - 1]) for k in range(1, 8)]

    def turn(slab):
        x = nodes[slab].astype(F32)
        for i in range(8):
            rows32 = x[32 * i : 32 * i + 32]
            turned = jnp.concatenate([rows32] * 4, axis=0).T
            sources[slab, :, i, :] = turned[:width]

    turn(1)
    for copy in halo[4:]:
        copy.wait_recv()
    turn(0)
    turn(2)
    picks = picker[...]

    def far_part(b):
        return far_step(lambda k: held[STEP * b + k], picks, lambda k: [sources[h, STEP * b + k] for h in range(3)], width)

    def far_pair(b, carry):
        fetch(2 * b).wait()
        fetch(2 * b + 1).wait()
        far_sum[:width, :] += far_part(2 * b) + far_part(2 * b + 1)
        return carry

    lax.fori_loop(0, 2, far_pair, 0)
    for copy in copies:
        copy.wait_recv()
    top1 = near_top[0, :, :width]
    for k in range(1, 8):
        top1 = top1 + near_top[k, :, :width]
    far_top[0, :, :width] = top1
    more = [push(far_top.at[0], far_top.at[k], 12 + k, cousins[k - 1]) for k in range(1, rows)]
    late = [push(dens, dens_lo, 2, right), push(dens, dens_hi, 3, left)]
    total = dot3(top1, coarse[child])
    lax.fori_loop(2, blocks // 2, far_pair, 0)
    for copy in more:
        copy.wait_recv()
    half = row // 8
    own = jnp.zeros((q_width, width), F32)
    other = jnp.zeros((q_width, width), F32)
    for k in range(8):
        src = lax.rem(row + rows - k, rows)
        pair = dot3(jnp.concatenate([far_top[k, :, :width], far_top[k + 8, :, :width]], axis=0), shift_up[lax.rem(src, 8)])
        same = jnp.where(src // 8 == half, 1.0, 0.0)
        a, b = pair[:q_width], pair[q_width:]
        own = own + (same * a + (1.0 - same) * b)
        other = other + ((1.0 - same) * a + same * b)
    top3 = dot3(own, shift_up[half]) + dot3(other, shift_up[1 - half])
    total = total + dot3(own, coarse[lax.rem(row, 8)]) + dot3(top3, coarse[half])
    for b in range(2 * (blocks // 2), blocks):
        fetch(b).wait()
        far_sum[:width, :] += far_part(b)
    node[...] = far_sum[...].T[:, :width]

    for c in range(8):
        at = slice(32 * c, 32 * c + 32)
        node[at, :] = node[at, :] + dot3(total, shift_down[c])
    leaf_sum[...] = jnp.zeros_like(leaf_sum)

    def descend(half, carry):
        tail = None
        for i in range(4):
            leaf_sum[i, :, :width] = dot3(node[...], dot3(shift_down[4 * half + i], down_inv[...]))
            last = leaf_sum[i, :, 128:]
            last = last if i == 0 else pltpu.roll(last, 32 * i, 1)
            tail = last if tail is None else tail + last
        for n in range(8):
            at = slice(32 * n, 32 * n + 32)
            for i in range(4):
                down[8 * n + 4 * half + i] = leaf_sum[i, at, :128]
            down_tail[2 * n + half] = tail[at]
        return carry

    lax.fori_loop(0, 2, descend, 0)
    for copy in halo[:4] + late:
        copy.wait_recv()
    for copy in halo + late + copies + more:
        copy.wait_send()


STEP = 8


def far_step(table_at, picks, rows_at, width):
    lane = lax.broadcasted_iota(jnp.int32, (32, 128), 1)
    zero = jnp.zeros((32, 128), BF)
    total = None
    for k in range(0, STEP, 2):
        sums = []
        rows = []
        for e in (k, k + 1):
            s = jnp.dot(table_at(e), picks, preferred_element_type=F32)
            hi, lo = split2(s)
            sums.append(jnp.concatenate([hi, lo], axis=0))
            x = jnp.concatenate(rows_at(e) + [jnp.zeros((8, 128), F32)], axis=0).astype(BF)
            for n in range(8):
                own = (lane >= 32 * (n % 4)) & (lane < 32 * (n % 4) + 32)
                part = jnp.where(own, x, zero)
                rows.append(jnp.concatenate([part, zero] if n < 4 else [zero, part], axis=1))
        r = jnp.dot(
            jnp.concatenate(sums, axis=1), jnp.concatenate(rows, axis=0), preferred_element_type=F32
        )
        r = r[:width] + r[width:]
        total = r if total is None else total + r
    return total


def up_call(counts, pts, dens, surf, count_row, vlist, up_inv, down_inv, shift_up, shift_down, coarse, table):
    leaves, q_width, _ = dens.shape
    width = up_inv.shape[0]
    vmem = pl.BlockSpec(memory_space=pltpu.VMEM)
    hbm = pl.BlockSpec(memory_space=pl.ANY)
    like = jax.ShapeDtypeStruct
    rows = 8 * q_width
    return pl.pallas_call(
        up_kernel,
        out_shape=[
            like(pts.shape, F32), like(pts.shape, F32), like(dens.shape, F32), like(dens.shape, F32),
            like((3, 8, 128), jnp.int32), like((3, leaves + leaves // 4, 128), F32),
            like((leaves, q_width, 128), F32), like((leaves // 4, q_width, 128), F32),
        ],
        in_specs=[pl.BlockSpec(memory_space=pltpu.SMEM)] + [vmem] * 10 + [hbm],
        out_specs=[hbm] * 4 + [vmem] * 4,
        scratch_shapes=[
            pltpu.VMEM((8, rows, 256), F32),
            pltpu.VMEM((rows, width), F32),
            pltpu.VMEM((3, rows, 256), BF),
            pltpu.VMEM((8, q_width, 256), F32),
            pltpu.VMEM((16, q_width, 256), F32),
            pltpu.VMEM(table.shape, BF),
            pltpu.VMEM((3, width, 8, 128), F32),
            pltpu.VMEM((256, rows), F32),
            pltpu.VMEM((4, rows, 256), F32),
            pltpu.VMEM((3, leaves, 128), F32),
            pltpu.VMEM((256, 384), F32),
            pltpu.VMEM((vlist.shape[1], 256), BF),
            pltpu.SemaphoreType.DMA((30,)),
            pltpu.SemaphoreType.DMA((30,)),
            pltpu.SemaphoreType.DMA((width // STEP,)),
        ],
        compiler_params=pltpu.CompilerParams(
            vmem_limit_bytes=56 * 1024 * 1024, collective_id=0, has_side_effects=True
        ),
        name="upward",
    )(counts, pts, dens, surf, count_row, vlist, up_inv, down_inv, shift_up, shift_down, coarse, table)


def local(
    points,
    dens,
    surface,
    counts,
    ulist,
    vlist,
    up_inverse,
    down_inverse,
    shift_up,
    shift_down,
    coarse,
    translate,
):
    leaf_count = dens.shape[0]
    index = lax.axis_index("oct")
    turned_points = jnp.transpose(points, (1, 0, 2))
    points_lo, points_hi, dens_lo, dens_hi, count_rows, surf_near, leaf_down, down_tail = up_call(
        counts, turned_points, dens, jnp.transpose(surface, (1, 0, 2)), counts.reshape(1, leaf_count), vlist,
        up_inverse, down_inverse, shift_up, shift_down, coarse, jnp.transpose(translate, (1, 2, 0)),
    )
    points3 = [points_lo, turned_points, points_hi]
    first = ((index - 1) * leaf_count).astype(jnp.int32).reshape(1)
    plan = plan_call(first, jnp.transpose(ulist), count_rows)
    return near_call(plan, points3, [dens_lo, dens, dens_hi], surf_near, leaf_down, down_tail)


def solution(mesh):
    placed = (
        P("oct", None, None),
        P("oct", None, None),
        P("oct", None, None),
        P("oct"),
        P("oct", None),
        P("oct", None),
        P(),
        P(),
        P(),
        P(),
        P(),
        P(),
    )
    return jax.shard_map(
        local, mesh=mesh, in_specs=placed, out_specs=P("oct", None, None), check_vma=False
    )
```

```python
import functools

import jax
import jax.numpy as jnp
from jax import lax
from jax.experimental import pallas as pl
from jax.experimental.pallas import tpu as pltpu
from jax.sharding import PartitionSpec as P

BF = jnp.bfloat16
F32 = jnp.float32


def split2(x):
    hi = x.astype(BF)
    lo = (x - hi.astype(F32)).astype(BF)
    return hi, lo


def split3(x):
    a = x.astype(BF).astype(F32)
    r = x - a
    b = r.astype(BF).astype(F32)
    return a, b, r - b


def rows8(shape):
    return lax.broadcasted_iota(jnp.int32, shape, 0)


LOG2E = 1.4426950408889634


def source_tiles(coords):
    out = []
    norm = None
    row = rows8((8, 128))
    for c in coords:
        x = jnp.broadcast_to(c, (8, 128))
        a, b, d = split3(LOG2E * x)
        first = (row <= 1) | (row == 4)
        out.append(jnp.where(first, a, jnp.where(row <= 3, b, jnp.where(row == 5, d, 0.0))))
        norm = x * x if norm is None else norm + x * x
    a, b, d = split3((-0.5 * LOG2E) * norm)
    out.append(
        jnp.where(row == 0, a, jnp.where(row == 1, b, jnp.where(row == 2, d, jnp.where(row <= 5, 1.0, 0.0))))
    )
    return out


def target_tiles(coords):
    out = []
    norm = None
    row = rows8((8, 128))
    for c in coords:
        x = jnp.broadcast_to(c, (8, 128))
        a, b, d = split3(x)
        first = (row == 0) | (row == 2) | (row == 5)
        second = (row == 1) | (row == 3)
        out.append(jnp.where(first, a, jnp.where(second, b, jnp.where(row == 4, d, 0.0))))
        norm = x * x if norm is None else norm + x * x
    a, b, d = split3((-0.5 * LOG2E) * norm)
    out.append(
        jnp.where(row <= 2, 1.0, jnp.where(row == 3, a, jnp.where(row == 4, b, jnp.where(row == 5, d, 0.0))))
    )
    return out


LIST_ROWS = 128
TABLE_ROWS = 2 * LIST_ROWS
LEAF_AT, PTR_AT, COUNT_AT, ROUNDS_AT = 0, 12, 26, 31
GROUP = 32


def plan_kernel(leaves, first, ulist, rows, out, ids):
    slots = ulist.shape[0]
    lane = lax.broadcasted_iota(jnp.int32, (32, 128), 1)
    ids[...] = jnp.full((32, 128), -1, jnp.int32)
    ids[:slots, :leaves] = ulist[...]
    rel = ids[...]
    rel = jnp.where(rel >= 0, rel - first[0], -1)
    counts = [rows[slab, :1, :] for slab in range(3)]
    nun = [jnp.right_shift(jnp.broadcast_to(c, (32, 128)) + 31, 5) for c in counts]
    low = jnp.where(lane < leaves, nun[0], pltpu.roll(nun[1], leaves, 1))
    from_low = jnp.take_along_axis(low, jnp.clip(rel, 0, 127), axis=1, mode="promise_in_bounds")
    from_high = jnp.take_along_axis(nun[2], jnp.clip(rel - 2 * leaves, 0, 127), axis=1, mode="promise_in_bounds")
    num = jnp.where(rel < 0, 0, jnp.where(rel < 2 * leaves, from_low, from_high))
    before = lax.broadcasted_iota(jnp.int32, (32, 32), 1) < lax.broadcasted_iota(jnp.int32, (32, 32), 0)
    start = 5 + jnp.dot(
        jnp.where(before, 1.0, 0.0).astype(BF), num.astype(F32).astype(BF), preferred_element_type=F32
    ).astype(jnp.int32)
    place = lax.broadcasted_iota(jnp.int32, (LIST_ROWS, 128), 0)
    mine = lax.broadcasted_iota(jnp.int32, (LIST_ROWS, 128), 1)
    unit = jnp.where(place < 4, 12 * leaves + 4 * mine + place, jnp.where(place == 4, 16 * leaves + mine, 17 * leaves))
    for s in range(slots):
        at = place - start[s : s + 1]
        inside = (at >= 0) & (at < num[s : s + 1])
        unit = jnp.where(inside, 4 * rel[s : s + 1] + at, unit)
    out[:LIST_ROWS, :] = unit
    out[LIST_ROWS:TABLE_ROWS, :] = jnp.bitwise_and(unit, -4) + jnp.bitwise_and(place - unit, 3)
    n = jnp.right_shift(start[31:] + num[31:] + 7, 3)
    n = jnp.where(lane[:1] < leaves, n, 0)
    column = jnp.broadcast_to(n.astype(F32), (128, 128)).T
    upto = lax.broadcasted_iota(jnp.int32, (128, 128), 1) <= lax.broadcasted_iota(jnp.int32, (128, 128), 0)
    end = jnp.dot(jnp.where(upto, 1.0, 0.0).astype(BF), column.astype(BF), preferred_element_type=F32)
    begin = (end - column).astype(jnp.int32)
    end = end.astype(jnp.int32)
    total = end[127:]
    out[TABLE_ROWS:, :] = jnp.zeros((32, 128), jnp.int32)
    for r in range(9):
        chunk = 128 * r + mine
        inside = (chunk >= begin) & (chunk < end)
        leaf = jnp.sum(jnp.where(inside, place, 0), axis=0, keepdims=True)
        ptr = jnp.sum(jnp.where(inside, (chunk - begin) * 1024 + place, 0), axis=0, keepdims=True)
        ptr = jnp.where(chunk[:1] < total, ptr, 120 * 128)
        out[TABLE_ROWS + LEAF_AT + r : TABLE_ROWS + LEAF_AT + r + 1, :] = leaf
        out[TABLE_ROWS + PTR_AT + r : TABLE_ROWS + PTR_AT + r + 1, :] = ptr
    for slab in range(3):
        out[TABLE_ROWS + COUNT_AT + slab : TABLE_ROWS + COUNT_AT + slab + 1, :] = counts[slab]
    out[TABLE_ROWS + ROUNDS_AT :, :] = jnp.right_shift(total + GROUP - 1, 5)


def plan_call(first, ulist, rows):
    leaves = ulist.shape[1]
    vmem = pl.BlockSpec(memory_space=pltpu.VMEM)
    return pl.pallas_call(
        functools.partial(plan_kernel, leaves),
        out_shape=jax.ShapeDtypeStruct((TABLE_ROWS + 32, 128), jnp.int32),
        in_specs=[pl.BlockSpec(memory_space=pltpu.SMEM), vmem, vmem],
        out_specs=vmem,
        scratch_shapes=[pltpu.VMEM((32, 128), jnp.int32)],
        name="plan",
    )(first, ulist, rows).reshape(-1)


def near_kernel(leaves, plan, p0, p1, p2, d0, d1, d2, surf, down, down_tail, out, f_s, m_s, w_s, e_s, acc):
    lane = lax.broadcasted_iota(jnp.int32, (32, 128), 1)
    maps = 128 * TABLE_ROWS

    def used(slab, j):
        return plan[maps + 128 * (COUNT_AT + slab) + j]

    lane_big = lax.broadcasted_iota(jnp.int32, (128, 128), 1)
    row_big = lax.broadcasted_iota(jnp.int32, (128, 128), 0)
    zero_unit = 4 * (3 * leaves + leaves + leaves // 4)
    shifts = jnp.concatenate(
        [jnp.where(lane_big == (row_big + 32 * k) % 128, 1.0, 0.0).astype(BF) for k in range(1, 4)], axis=1
    )

    def put_features(coords4, base):
        tiles = []
        for coords in coords4:
            tiles += source_tiles(coords)
        tile = jnp.concatenate(tiles, axis=0).astype(BF)
        turned = tile.T
        for i in range(4):
            own = (lane_big >= 32 * i) & (lane_big < 32 * i + 32)
            f_s[pl.ds(base + 4 * i, 4)] = jnp.where(own, turned, jnp.zeros_like(turned)).reshape(4, 32, 128)

    def put_density(tiles, base):
        parts = []
        for i, tile in enumerate(tiles):
            hi, lo = split2(tile)
            parts.append(jnp.concatenate([hi, lo], axis=0))
            m_s[base + 4 * i] = parts[i]
        moved = jnp.dot(jnp.concatenate(parts, axis=0), shifts, preferred_element_type=F32).astype(BF)
        for i in range(4):
            for k in range(1, 4):
                m_s[base + 4 * i + k] = moved[64 * i : 64 * i + 64, 128 * (k - 1) : 128 * k]

    for slab, (p, d) in enumerate(((p0, d0), (p1, d1), (p2, d2))):

        def prep(g, carry, slab=slab, p=p, d=d):
            for half in range(4):
                first = 16 * g + 4 * half
                coords4 = [[p[c, pl.ds(first + i, 1), :] for c in range(3)] for i in range(4)]
                put_features(coords4, 4 * (slab * leaves + first))
                masked = [
                    jnp.where(lane < used(slab, first + i), d[first + i], 0.0) for i in range(4)
                ]
                put_density(masked, 4 * (slab * leaves + first))
            return carry

        lax.fori_loop(0, leaves // 16, prep, 0)

    def prep_surface(count, row0, view):
        def body(g, carry):
            for half in range(4):
                first = 16 * g + 4 * half
                coords4 = [[surf[c, pl.ds(row0 + first + i, 1), :] for c in range(3)] for i in range(4)]
                put_features(coords4, 4 * (3 * leaves + row0 + first))
                put_density([view(first + i) for i in range(4)], 4 * (3 * leaves + row0 + first))
            return carry

        lax.fori_loop(0, count // 16, body, 0)

    prep_surface(leaves, 0, lambda j: down[j])
    prep_surface(leaves // 4, leaves, lambda j: down_tail[j])
    f_s[pl.ds(zero_unit, 4)] = jnp.zeros((4, 32, 128), BF)
    m_s[pl.ds(zero_unit, 4)] = jnp.zeros((4, 64, 128), BF)

    def prep_target(g, carry):
        for i in range(4):
            j = 4 * g + i
            tile = jnp.concatenate(target_tiles([p1[c, pl.ds(j, 1), :] for c in range(3)]), axis=0).astype(BF)
            w_s[j] = jnp.concatenate([tile] * 4, axis=0)
            acc[j] = jnp.zeros((64, 256), F32)
        return carry

    lax.fori_loop(0, leaves // 4, prep_target, 0)

    lane64 = lax.broadcasted_iota(jnp.int32, (64, 128), 1)

    def exponents(i, slot):
        base, l = plan[maps + 128 * PTR_AT + i], plan[maps + 128 * LEAF_AT + i]
        left = jnp.concatenate([f_s[plan[base + 128 * v]] for v in range(4)], axis=0)
        right = jnp.concatenate([f_s[plan[base + 128 * (4 + v)]] for v in range(4)], axis=0)
        w = w_s[l]
        e_s[slot, 0] = jnp.dot(left, w, preferred_element_type=F32)
        e_s[slot, 1] = jnp.dot(right, w, preferred_element_type=F32)

    def weights(base):
        t = [m_s[plan[base + 128 * v]] for v in range(4)]
        return jnp.where(
            lane64 < 64, jnp.where(lane64 < 32, t[0], t[1]), jnp.where(lane64 < 96, t[2], t[3])
        )

    def apply(i, slot):
        base, l = plan[maps + 128 * PTR_AT + i], plan[maps + 128 * LEAF_AT + i]
        m = jnp.concatenate([weights(base + 128 * LIST_ROWS), weights(base + 128 * (LIST_ROWS + 4))], axis=1)
        k = jnp.exp2(e_s[slot].reshape(256, 128))
        hi, lo = split2(k)
        acc[l] += jnp.dot(m, jnp.concatenate([hi, lo], axis=1), preferred_element_type=F32)

    half = 16
    for u in range(half):
        exponents(u, u)

    def body(i, carry):
        at = 2 * half * i
        for u in range(half):
            exponents(at + half + u, half + u)
            apply(at + u, u)
        for u in range(half):
            exponents(at + 2 * half + u, u)
            apply(at + half + u, half + u)
        return carry

    lax.fori_loop(0, plan[maps + 128 * ROUNDS_AT], body, 0)

    def finish(g, carry):
        for i in range(4):
            j = 4 * g + i
            a = acc[j]
            v = (a[:32, :128] + a[:32, 128:]) + (a[32:, :128] + a[32:, 128:])
            out[j] = jnp.where(lane < used(1, j), v, 0.0)
        return carry

    lax.fori_loop(0, leaves // 4, finish, 0)


def near_call(plan, pts, dens, surf, down, down_tail):
    leaves = dens[0].shape[0]
    units = 4 * (3 * leaves + leaves + leaves // 4) + 4
    smem = pl.BlockSpec(memory_space=pltpu.SMEM)
    vmem = pl.BlockSpec(memory_space=pltpu.VMEM)
    return pl.pallas_call(
        functools.partial(near_kernel, leaves),
        out_shape=jax.ShapeDtypeStruct(dens[0].shape, F32),
        in_specs=[smem] + [vmem] * 9,
        out_specs=vmem,
        scratch_shapes=[
            pltpu.VMEM((units, 32, 128), BF),
            pltpu.VMEM((units, 64, 128), BF),
            pltpu.VMEM((leaves, 128, 128), BF),
            pltpu.VMEM((32, 2, 128, 128), F32),
            pltpu.VMEM((leaves, 64, 256), F32),
        ],
        compiler_params=pltpu.CompilerParams(vmem_limit_bytes=60 * 1024 * 1024),
        name="near",
    )(plan, *pts, *dens, surf, down, down_tail)


def dot3(a, b):
    ah, al = split2(a)
    bh, bl = split2(b)
    left = jnp.concatenate([ah, al], axis=0)
    r = jnp.dot(left, bh, preferred_element_type=F32)
    m = a.shape[0]
    return r[:m] + (r[m:] + jnp.dot(ah, bl, preferred_element_type=F32))


def up_kernel(
    counts, pts, dens, surf, count_row, vlist, up_inv, down_inv, shift_up, shift_down, coarse, table,
    pts_lo, pts_hi, dens_lo, dens_hi, count_rows, surf_near, down, down_tail,
    check, node, nodes, near_top, far_top, held, sources, far_sum, leaf_sum, surf_pad, sel_turned, picker, send, recv, table_sem,
):
    leaves, q_width = dens.shape[0], dens.shape[1]
    width = up_inv.shape[0]
    count = lax.axis_size("oct")
    me = lax.axis_index("oct")
    right = lax.rem(me + 1, count)
    left = lax.rem(me + count - 1, count)
    child = lax.rem(me, 8)
    row = me // 8
    rows = count // 8
    mates = [me - child + lax.rem(child + k, 8) for k in range(1, 8)]
    cousins = [lax.rem(row + k, rows) * 8 + child for k in range(1, rows)]

    def fetch(b):
        part = pl.ds(pl.multiple_of(STEP * b, STEP), STEP)
        return pltpu.make_async_copy(table.at[part], held.at[part], table_sem.at[b])

    def fetch_start(b, carry):
        fetch(b).start()
        return carry

    blocks = width // STEP
    lax.fori_loop(0, blocks, fetch_start, 0)
    barrier = pltpu.get_barrier_semaphore()
    for other in [left, right] + mates + cousins:
        pl.semaphore_signal(barrier, inc=1, device_id=(other,), device_id_type=pl.DeviceIdType.MESH)
    pl.semaphore_wait(barrier, 2 + len(mates) + len(cousins))

    def push(src, dst, sem, device):
        copy = pltpu.make_async_remote_copy(
            src_ref=src, dst_ref=dst, send_sem=send.at[sem], recv_sem=recv.at[sem],
            device_id=(device,), device_id_type=pl.DeviceIdType.MESH,
        )
        copy.start()
        return copy

    early, rest = pl.ds(0, leaves // 2), pl.ds(leaves // 2, leaves // 2)
    count_rows[1] = jnp.zeros((8, 128), jnp.int32)
    count_rows[1, :1, :leaves] = count_row[...]
    halo = [
        push(count_rows.at[1], count_rows.at[0], 28, right),
        push(count_rows.at[1], count_rows.at[2], 29, left),
        push(pts, pts_lo, 0, right),
        push(pts, pts_hi, 1, left),
        push(dens.at[early], dens_lo.at[early], 2, right),
        push(dens.at[early], dens_hi.at[early], 3, left),
    ]

    surf_pad[...] = jnp.zeros_like(surf_pad)
    surf_pad[:, :, : width - 128] = surf[:, :, 128:]
    surf_near[:, :leaves, :] = surf[:, :, :128]
    for c in range(3):
        packed = None
        for i in range(4):
            last = surf_pad[c, pl.ds(i, leaves // 4, stride=4), :]
            last = last if i == 0 else pltpu.roll(last, 32 * i, 1)
            packed = last if packed is None else packed + last
        surf_near[c, leaves:, :] = packed
    rel = vlist[...]
    rel = jnp.where(rel >= 0, rel - (me - 1) * 8, -1)
    types = rel.shape[1]
    sel_turned[...] = jnp.zeros_like(sel_turned)
    for n in range(8):
        same = jnp.broadcast_to(rel[n : n + 1], (32, types)) == rows8((32, types))
        sel_turned[32 * n : 32 * n + 32, :types] = jnp.where(same, 1.0, 0.0)
    picker[...] = sel_turned[...].T[:types].astype(BF)
    lane = lax.broadcasted_iota(jnp.int32, (32, 128), 1)
    lane_big = lax.broadcasted_iota(jnp.int32, (128, 128), 1)

    def leaf_node(g):
        at = pl.ds(pl.multiple_of(8 * g, 8), 8)
        points8 = [pts[c, at, :] for c in range(3)]
        main8 = [surf_near[c, at, :] for c in range(3)]
        tail8 = [surf_pad[c, at, :] for c in range(3)]
        for half in range(2):
            tiles = []
            for i in range(4):
                r = 4 * half + i
                tiles += source_tiles([x[r : r + 1] for x in points8])
            turned = jnp.concatenate(tiles, axis=0).astype(BF).T
            for i in range(4):
                r = 4 * half + i
                own = (lane_big >= 32 * i) & (lane_big < 32 * i + 32)
                f = jnp.where(own, turned, jnp.zeros_like(turned))
                w = jnp.concatenate(
                    [
                        jnp.concatenate(target_tiles([x[r : r + 1] for x in part]), axis=0).astype(BF)
                        for part in (main8, tail8)
                    ],
                    axis=1,
                )
                k = jnp.exp2(jnp.dot(f, jnp.concatenate([w] * 4, axis=0), preferred_element_type=F32))
                hi, lo = split2(k)
                mh, ml = split2(jnp.where(lane < counts[8 * g + r], dens[8 * g + r], 0.0))
                p = jnp.dot(
                    jnp.concatenate([mh, ml], axis=0),
                    jnp.concatenate([hi, lo], axis=1),
                    preferred_element_type=F32,
                )
                check[r, pl.ds(pl.multiple_of(32 * g, 32), 32), :] = (p[:32, :256] + p[:32, 256:]) + (
                    p[32:, :256] + p[32:, 256:]
                )

    def leaf_group(g, carry):
        leaf_node(2 * g)
        leaf_node(2 * g + 1)
        return carry

    lax.fori_loop(0, leaves // 16, leaf_group, 0)
    node[...] = jnp.zeros_like(node)
    far_sum[...] = jnp.zeros_like(far_sum)

    def merge(half, carry):
        parts = []
        for i in range(4):
            both = dot3(up_inv[...], shift_up[4 * half + i])
            parts.append(dot3(check[4 * half + i][:, :width], both))
        node[...] += (parts[0] + parts[1]) + (parts[2] + parts[3])
        return carry

    lax.fori_loop(0, 2, merge, 0)
    nodes[1, :, :width] = node[...].astype(BF)
    halo.append(push(nodes.at[1], nodes.at[0], 4, right))
    halo.append(push(nodes.at[1], nodes.at[2], 5, left))

    def climb(c, total):
        return total + dot3(node[pl.ds(pl.multiple_of(32 * c, 32), 32), :], shift_up[c])

    top = lax.fori_loop(0, 8, climb, jnp.zeros((q_width, width), F32))
    near_top[0, :, :width] = dot3(top, shift_up[child])
    copies = [push(near_top.at[0], near_top.at[k], 5 + k, mates[k - 1]) for k in range(1, 8)]

    def turn(slab):
        x = nodes[slab].astype(F32)
        for i in range(8):
            rows32 = x[32 * i : 32 * i + 32]
            turned = jnp.concatenate([rows32] * 4, axis=0).T
            sources[slab, :, i, :] = turned[:width]

    turn(1)
    for copy in halo[6:]:
        copy.wait_recv()
    turn(0)
    turn(2)
    picks = picker[...]

    def far_part(b):
        return far_step(lambda k: held[STEP * b + k], picks, lambda k: [sources[h, STEP * b + k] for h in range(3)], width)

    def far_pair(b, carry):
        fetch(2 * b).wait()
        fetch(2 * b + 1).wait()
        far_sum[:width, :] += far_part(2 * b) + far_part(2 * b + 1)
        return carry

    lax.fori_loop(0, 2, far_pair, 0)
    for copy in copies:
        copy.wait_recv()
    top1 = near_top[0, :, :width]
    for k in range(1, 8):
        top1 = top1 + near_top[k, :, :width]
    far_top[0, :, :width] = top1
    more = [push(far_top.at[0], far_top.at[k], 12 + k, cousins[k - 1]) for k in range(1, rows)]
    late = [
        push(dens.at[rest], dens_lo.at[rest], 30, right),
        push(dens.at[rest], dens_hi.at[rest], 31, left),
    ]
    total = dot3(top1, coarse[child])
    lax.fori_loop(2, blocks // 2, far_pair, 0)
    for copy in more:
        copy.wait_recv()
    half = row // 8
    own = jnp.zeros((q_width, width), F32)
    other = jnp.zeros((q_width, width), F32)
    for k in range(8):
        src = lax.rem(row + rows - k, rows)
        pair = dot3(jnp.concatenate([far_top[k, :, :width], far_top[k + 8, :, :width]], axis=0), shift_up[lax.rem(src, 8)])
        same = jnp.where(src // 8 == half, 1.0, 0.0)
        a, b = pair[:q_width], pair[q_width:]
        own = own + (same * a + (1.0 - same) * b)
        other = other + ((1.0 - same) * a + same * b)
    top3 = dot3(own, shift_up[half]) + dot3(other, shift_up[1 - half])
    total = total + dot3(own, coarse[lax.rem(row, 8)]) + dot3(top3, coarse[half])
    for b in range(2 * (blocks // 2), blocks):
        fetch(b).wait()
        far_sum[:width, :] += far_part(b)
    node[...] = far_sum[...].T[:, :width]

    for c in range(8):
        at = slice(32 * c, 32 * c + 32)
        node[at, :] = node[at, :] + dot3(total, shift_down[c])
    leaf_sum[...] = jnp.zeros_like(leaf_sum)

    def descend(half, carry):
        tail = None
        for i in range(4):
            leaf_sum[i, :, :width] = dot3(node[...], dot3(shift_down[4 * half + i], down_inv[...]))
            last = leaf_sum[i, :, 128:]
            last = last if i == 0 else pltpu.roll(last, 32 * i, 1)
            tail = last if tail is None else tail + last
        for n in range(8):
            at = slice(32 * n, 32 * n + 32)
            for i in range(4):
                down[8 * n + 4 * half + i] = leaf_sum[i, at, :128]
            down_tail[2 * n + half] = tail[at]
        return carry

    lax.fori_loop(0, 2, descend, 0)
    for copy in halo[:6] + late:
        copy.wait_recv()
    for copy in halo + late + copies + more:
        copy.wait_send()


STEP = 8


def far_step(table_at, picks, rows_at, width):
    lane = lax.broadcasted_iota(jnp.int32, (32, 128), 1)
    zero = jnp.zeros((32, 128), BF)
    total = None
    for k in range(0, STEP, 2):
        sums = []
        rows = []
        for e in (k, k + 1):
            s = jnp.dot(table_at(e), picks, preferred_element_type=F32)
            hi, lo = split2(s)
            sums.append(jnp.concatenate([hi, lo], axis=0))
            x = jnp.concatenate(rows_at(e) + [jnp.zeros((8, 128), F32)], axis=0).astype(BF)
            for n in range(8):
                own = (lane >= 32 * (n % 4)) & (lane < 32 * (n % 4) + 32)
                part = jnp.where(own, x, zero)
                rows.append(jnp.concatenate([part, zero] if n < 4 else [zero, part], axis=1))
        r = jnp.dot(
            jnp.concatenate(sums, axis=1), jnp.concatenate(rows, axis=0), preferred_element_type=F32
        )
        r = r[:width] + r[width:]
        total = r if total is None else total + r
    return total


def up_call(counts, pts, dens, surf, count_row, vlist, up_inv, down_inv, shift_up, shift_down, coarse, table):
    leaves, q_width, _ = dens.shape
    width = up_inv.shape[0]
    vmem = pl.BlockSpec(memory_space=pltpu.VMEM)
    hbm = pl.BlockSpec(memory_space=pl.ANY)
    like = jax.ShapeDtypeStruct
    rows = 8 * q_width
    return pl.pallas_call(
        up_kernel,
        out_shape=[
            like(pts.shape, F32), like(pts.shape, F32), like(dens.shape, F32), like(dens.shape, F32),
            like((3, 8, 128), jnp.int32), like((3, leaves + leaves // 4, 128), F32),
            like((leaves, q_width, 128), F32), like((leaves // 4, q_width, 128), F32),
        ],
        in_specs=[pl.BlockSpec(memory_space=pltpu.SMEM)] + [vmem] * 10 + [hbm],
        out_specs=[hbm] * 4 + [vmem] * 4,
        scratch_shapes=[
            pltpu.VMEM((8, rows, 256), F32),
            pltpu.VMEM((rows, width), F32),
            pltpu.VMEM((3, rows, 256), BF),
            pltpu.VMEM((8, q_width, 256), F32),
            pltpu.VMEM((16, q_width, 256), F32),
            pltpu.VMEM(table.shape, BF),
            pltpu.VMEM((3, width, 8, 128), F32),
            pltpu.VMEM((256, rows), F32),
            pltpu.VMEM((4, rows, 256), F32),
            pltpu.VMEM((3, leaves, 128), F32),
            pltpu.VMEM((256, 384), F32),
            pltpu.VMEM((vlist.shape[1], 256), BF),
            pltpu.SemaphoreType.DMA((32,)),
            pltpu.SemaphoreType.DMA((32,)),
            pltpu.SemaphoreType.DMA((width // STEP,)),
        ],
        compiler_params=pltpu.CompilerParams(
            vmem_limit_bytes=56 * 1024 * 1024, collective_id=0, has_side_effects=True
        ),
        name="upward",
    )(counts, pts, dens, surf, count_row, vlist, up_inv, down_inv, shift_up, shift_down, coarse, table)


def local(
    points,
    dens,
    surface,
    counts,
    ulist,
    vlist,
    up_inverse,
    down_inverse,
    shift_up,
    shift_down,
    coarse,
    translate,
):
    leaf_count = dens.shape[0]
    index = lax.axis_index("oct")
    turned_points = jnp.transpose(points, (1, 0, 2))
    points_lo, points_hi, dens_lo, dens_hi, count_rows, surf_near, leaf_down, down_tail = up_call(
        counts, turned_points, dens, jnp.transpose(surface, (1, 0, 2)), counts.reshape(1, leaf_count), vlist,
        up_inverse, down_inverse, shift_up, shift_down, coarse, jnp.transpose(translate, (1, 2, 0)),
    )
    points3 = [points_lo, turned_points, points_hi]
    first = ((index - 1) * leaf_count).astype(jnp.int32).reshape(1)
    plan = plan_call(first, jnp.transpose(ulist), count_rows)
    return near_call(plan, points3, [dens_lo, dens, dens_hi], surf_near, leaf_down, down_tail)


def solution(mesh):
    placed = (
        P("oct", None, None),
        P("oct", None, None),
        P("oct", None, None),
        P("oct"),
        P("oct", None),
        P("oct", None),
        P(),
        P(),
        P(),
        P(),
        P(),
        P(),
    )
    return jax.shard_map(
        local, mesh=mesh, in_specs=placed, out_specs=P("oct", None, None), check_vma=False
    )
```
